32 devices in a mesh: dp: 8 (over z, x), fsdp: 4 (over y, core).
Axes of the slice: x: 2, y: 2, z: 4, core: 2. Of those that a mesh axis runs over, the one named last changes fastest.
Arguments:
- inputs: bfloat16 [2, 3072, 1024], P(None, ('dp', 'fsdp')), may hold values from -6 to 6
- cotangent: bfloat16 [2, 3072, 1024], P(None, ('dp', 'fsdp')), may hold values from -6 to 6
- segments: int32 [2, 3072], P(None, ('dp', 'fsdp')), may hold values from 0 to 63, never falling along the last dimension, each value on 1 to 96 neighbouring positions
- pack_length: int32 [2, 32], P(None, ('dp', 'fsdp')), may hold values from 48 to 96, as said below
- norm_gain: bfloat16 [2, 1024], P(None, ('dp', 'fsdp')), may hold values from 0.5 to 1.5
- norm_shift: bfloat16 [2, 1024], P(None, ('dp', 'fsdp')), may hold values from -4 to 4
- qkv_weight: bfloat16 [2, 1024, 3072], P(None, ('dp', 'fsdp')), may hold values from -0.1875 to 0.1875
- qv_bias: bfloat16 [2, 2048], P(None, ('dp', 'fsdp')), may hold values from -6 to 6
- proj_weight: bfloat16 [2, 1024, 1024], P(None, ('dp', 'fsdp')), may hold values from -0.75 to 0.75
- proj_bias: bfloat16 [2, 1024], P(None, ('dp', 'fsdp')), may hold values from -4 to 4
- up_weight: bfloat16 [2, 1024, 4096], P(None, ('dp', 'fsdp')), may hold values from -0.1875 to 0.1875
- up_bias: bfloat16 [2, 4096], P(None, ('dp', 'fsdp')), may hold values from -6 to 6
- down_weight: bfloat16 [2, 4096, 1024], P(None, ('dp', 'fsdp')), may hold values from -0.09375 to 0.09375
- down_bias: bfloat16 [2, 1024], P(None, ('dp', 'fsdp')), may hold values from -4 to 4
Outputs:
- outputs: bfloat16 [2, 3072, 1024], P(None, ('dp', 'fsdp'))
- input_grad: float32 [2, 3072, 1024], P(None, ('dp', 'fsdp'))
- gain_grad: float32 [2, 1024], P(None, ('dp', 'fsdp'))
- shift_grad: float32 [2, 1024], P(None, ('dp', 'fsdp'))
- qkv_grad: float32 [2, 1024, 3072], P(None, ('dp', 'fsdp'))
- qvbias_grad: float32 [2, 2048], P(None, ('dp', 'fsdp'))
- proj_grad: float32 [2, 1024, 1024], P(None, ('dp', 'fsdp'))
- projbias_grad: float32 [2, 1024], P(None, ('dp', 'fsdp'))
- up_grad: float32 [2, 1024, 4096], P(None, ('dp', 'fsdp'))
- upbias_grad: float32 [2, 4096], P(None, ('dp', 'fsdp'))
- down_grad: float32 [2, 4096, 1024], P(None, ('dp', 'fsdp'))
- downbias_grad: float32 [2, 1024], P(None, ('dp', 'fsdp'))
The draws below stay inside these ranges and needn't reach their ends.
Inputs may be any that keep to these rules, and one draw needn't show every extreme that they name: `segments`: along each micro-batch the numbers never fall; every number is used; a document spans 1 to 96 rows and one spans exactly 96. `pack_length`: some pack is full and some holds exactly 48 live rows.
All inputs are finite; a program needn't handle non-finite values.
Results may differ from the reference program's by a relative error of at most 0.013.
Values may be sent and summed in bfloat16 or wider, within the bound.
A program may use at most 320 MiB of HBM per device.

```python
import math
import jax
import jax.numpy as jnp
import numpy as np
from jax import lax

D = 1024
FF = 4096
HEAD_DIM = 64
ROT = 16
LAYERS = 2
MICRO = 2
TOK_DEV = 96
TOKENS = 3072
DEVICES = 32


def draw_pack_length(key, part):
    key = jax.random.fold_in(key, 11)
    packs = TOKENS // TOK_DEV
    counts = jax.random.randint(key, (MICRO, packs), TOK_DEV // 2, TOK_DEV + 1)
    counts = counts.at[0, 0].set(TOK_DEV)
    counts = counts.at[MICRO - 1, packs - 1].set(TOK_DEV // 2)
    return counts.astype(jnp.int32)


def with_spikes(entries, rng, source, target, parts, factor):
    owner, partner = [(jnp.arange(entries.shape[dim]) // (entries.shape[dim] // parts)).reshape([-1 if axis == dim else 1 for axis in range(entries.ndim)]) for dim in (source, target)]
    chosen = jax.random.permutation(rng, parts)[partner]
    strong = (owner == chosen) | (owner == (partner + parts // 2) % parts)
    return jnp.where(strong, factor * entries, entries)


def levels(rng, dims, shards, low, high):
    loudness, own = 1.0, jax.random.fold_in(rng, 6)
    for dim, blocks in shards:
        draws = jnp.exp(jax.random.uniform(jax.random.fold_in(own, dim), (blocks,), jnp.float32, low / len(shards), high / len(shards)))
        loudness = loudness * jnp.repeat(draws, dims[dim] // blocks).reshape([-1 if axis == dim else 1 for axis in range(len(dims))])
    return loudness


def split_up(number_of, total, limit, slope):
    loads = [(1 << 20) // math.isqrt(grade ** slope) + 1 for grade in range(2, number_of + 1)]
    surplus, given = total - limit - (number_of - 1), [1] * (number_of - 1)
    while surplus > 0:
        free = [i for i in range(number_of - 1) if given[i] < limit]
        whole, remaining = sum([loads[i] for i in free]), surplus
        for i in free:
            more = min(limit - given[i], max(1, remaining * loads[i] // whole), surplus)
            given[i] = given[i] + more
            surplus = surplus - more
    return np.array([limit] + given)


def uneven_parts(rng, amount, total, most, skew):
    if amount == 2:
        one = jax.random.randint(rng, (), max(1, total - most), min(most, total - 1) + 1)
        return jnp.stack([one, total - one])
    sizes = jnp.asarray(split_up(amount, total, most, skew), jnp.int32)
    couples = (amount - 1) // 2
    donor, taker = sizes[1:1 + 2 * couples:2], sizes[2:2 + 2 * couples:2]
    slack = jnp.minimum(donor - 1, most - taker)
    moved = jax.random.randint(jax.random.fold_in(rng, 1), (couples,), 0, 1 << 20) % (slack + 1)
    sizes = sizes.at[1:1 + 2 * couples:2].set(donor - moved).at[2:2 + 2 * couples:2].set(taker + moved)
    return sizes[jax.random.permutation(jax.random.fold_in(rng, 2), amount)]


def bell_draw(stream_key, shape, scale, bound, cuts=(), kind=jnp.bfloat16):
    entries = jax.random.normal(stream_key, shape, jnp.float32) * scale
    if len(cuts) > 0:
        entries = levels(stream_key, shape, cuts, -0.22, 0.18) * entries
    return jnp.clip(entries, min=-bound, max=bound).astype(kind)


def bell_draw_with(key, extent, spread, reach, pieces, heavy, kind=jnp.bfloat16):
    entries = spread * jax.random.normal(key, extent, jnp.float32)
    if pieces:
        entries = entries * levels(key, extent, pieces, -0.22, 0.18)
    return jnp.clip(with_spikes(entries, jax.random.fold_in(key, 3), *heavy), -reach, reach).astype(kind)


def setup_inputs(seed: int = 0) -> dict:
    keys = jax.random.split(jax.random.key(seed), 15)
    return {
        "inputs": bell_draw(keys[0], (MICRO, TOKENS, D), 1.0, 6.0, ((1, 32),)),
        "cotangent": bell_draw_with(keys[1], (MICRO, TOKENS, D), 1.0, 6.0, ((1, 32),), (1, 2, 32, 2.75)),
        "segments": jax.vmap(lambda own: jnp.searchsorted(jnp.cumsum(uneven_parts(own, 2 * DEVICES, TOKENS, TOK_DEV, 0)), jnp.arange(TOKENS), side="right"))(jax.random.split(keys[2], MICRO)).reshape((MICRO, TOKENS)).astype(jnp.int32),
        "pack_length": draw_pack_length(jax.random.fold_in(keys[14], 71), 0),
        "norm_gain": jnp.clip(1.0 + 0.1 * jax.random.normal(keys[4], (LAYERS, D), jnp.float32), 0.5, 1.5).astype(jnp.bfloat16),
        "norm_shift": bell_draw(keys[5], (LAYERS, D), 0.3, 4.0, ((1, 32),)),
        "qkv_weight": bell_draw(keys[6], (LAYERS, D, 3 * D), D ** -0.5, 0.1875, ((1, 32),)),
        "qv_bias": bell_draw(keys[7], (LAYERS, 2 * D), 0.5, 6.0, ((1, 32),)),
        "proj_weight": bell_draw(keys[8], (LAYERS, D, D), (D // 16) ** -0.5, 0.75, ((1, 32),)),
        "proj_bias": bell_draw(keys[9], (LAYERS, D), 0.3, 4.0, ((1, 32),)),
        "up_weight": bell_draw(keys[10], (LAYERS, D, FF), D ** -0.5, 0.1875, ((1, 32),)),
        "up_bias": bell_draw(keys[11], (LAYERS, FF), 0.5, 6.0, ((1, 32),)),
        "down_weight": bell_draw(keys[12], (LAYERS, FF, D), FF ** -0.5, 0.09375, ((1, 32),)),
        "down_bias": bell_draw(keys[13], (LAYERS, D), 0.3, 4.0, ((1, 32),)),
    }


HIGH = lax.Precision.HIGHEST
EPS = 1e-05

@jax.custom_vjp
def low(v):
    return lax.optimization_barrier(v.astype(jnp.bfloat16)).astype(jnp.float32)

@jax.custom_vjp
def low_back(v):
    return v

def low_keep(v):
    return (low(v), None)

def low_pass(kept, grad):
    return (grad,)

def back_keep(v):
    return (v, None)

def back_low(kept, grad):
    return (low(grad),)
low.defvjp(low_keep, low_pass)
low_back.defvjp(back_keep, back_low)

def product(left_side, right_side):
    return jnp.dot(left_side, right_side, precision=HIGH, preferred_element_type=jnp.float32)

def rotate(vectors, cosine, sine_table):
    half_dims = cosine.shape[-1]
    first_half = vectors[..., :half_dims]
    second = vectors[..., half_dims:2 * half_dims]
    remainder = vectors[..., 2 * half_dims:]
    cos_rows = cosine[:, None, :]
    sin_rows = sine_table[:, None, :]
    return jnp.concatenate([first_half * cos_rows - second * sin_rows, second * cos_rows + first_half * sin_rows, remainder], axis=-1)

def attend(block):
    queries, key_vectors, value_vectors, allowed = block
    scores = jnp.einsum('pqhd,pkhd->phqk', queries, key_vectors, precision=HIGH, preferred_element_type=jnp.float32) * (1.0 / math.sqrt(HEAD_DIM))
    scores = low_back(scores)
    scores = jnp.where(allowed[:, None], scores, -1e+30)
    soft_weights = low(jax.nn.softmax(scores, axis=-1))
    return jnp.einsum('phqk,pkhd->pqhd', soft_weights, value_vectors, precision=HIGH, preferred_element_type=jnp.float32)

def layer(params, stream, allowed, cosine, sine_table):
    norm_gain, norm_shift, qkv_weight, qv_bias, proj_weight, proj_bias, up_weight, up_bias, down_weight, down_bias = params
    packs, row_count, model_width = stream.shape
    head_count = model_width // HEAD_DIM
    average = lax.optimization_barrier(jnp.mean(stream, axis=-1, keepdims=True))
    centred = stream - average
    variance = lax.optimization_barrier(jnp.mean(centred * centred, axis=-1, keepdims=True))
    hidden = low(centred * lax.rsqrt(variance + EPS) * norm_gain + norm_shift)
    entry_bias = jnp.concatenate([qv_bias[:model_width], jnp.zeros_like(qv_bias[:model_width]), qv_bias[model_width:]])
    merged = low_back(product(hidden, qkv_weight) + entry_bias)
    head_shape = (packs, row_count, head_count, HEAD_DIM)
    queries = low(rotate(merged[..., :model_width].reshape(head_shape), cosine, sine_table))
    key_vectors = low(rotate(merged[..., model_width:2 * model_width].reshape(head_shape), cosine, sine_table))
    value_vectors = low(merged[..., 2 * model_width:].reshape(head_shape))
    per_step = math.gcd(packs, max(1, 4096 // row_count))
    step_count = packs // per_step

    def regroup(array):
        return array.reshape((step_count, per_step) + array.shape[1:])
    context = lax.map(jax.checkpoint(attend), (regroup(queries), regroup(key_vectors), regroup(value_vectors), regroup(allowed)))
    context = low(low_back(context.reshape(packs, row_count, model_width)))
    attention_out = low_back(product(context, proj_weight) + proj_bias)
    up_proj = low_back(product(hidden, up_weight) + up_bias)
    activation = low(jax.nn.gelu(up_proj, approximate=False))
    mlp_out = low_back(product(activation, down_weight) + down_bias)
    return stream + attention_out + mlp_out

def reference(inputs, cotangent, segments, pack_length, norm_gain, norm_shift, qkv_weight, qv_bias, proj_weight, proj_bias, up_weight, up_bias, down_weight, down_bias):
    packs = MICRO * (TOKENS // TOK_DEV)
    stream = inputs.astype(jnp.float32).reshape(packs, TOK_DEV, D)
    position = jnp.arange(TOK_DEV)
    live_rows = position[None, :] < pack_length.reshape(packs, 1)
    pack_segments = segments.reshape(packs, TOK_DEV)
    causal = position[:, None] >= position[None, :]
    diagonal = position[:, None] == position[None, :]
    allowed = (pack_segments[:, :, None] == pack_segments[:, None, :]) & causal[None] & (live_rows[:, None, :] | diagonal[None])
    angle = position.astype(jnp.float32)[:, None] * (10000.0 ** (-jnp.arange(0, ROT, 2, dtype=jnp.float32) / ROT))[None, :]
    cosine = jnp.cos(angle)
    sine_table = jnp.sin(angle)
    weights = tuple((weight.astype(jnp.float32) for weight in (norm_gain, norm_shift, qkv_weight, qv_bias, proj_weight, proj_bias, up_weight, up_bias, down_weight, down_bias)))

    def forward(stream_in, weights_in):
        for layer_index in range(LAYERS):
            stream_in = layer(tuple((weight[layer_index] for weight in weights_in)), stream_in, allowed, cosine, sine_table)
        return stream_in
    result, pullback = jax.vjp(forward, stream, weights)
    upstream = cotangent.astype(jnp.float32).reshape(packs, TOK_DEV, D) * live_rows[..., None].astype(jnp.float32)
    input_grad, weight_grads = pullback(upstream)
    return (result.reshape(MICRO, TOKENS, D).astype(jnp.bfloat16), input_grad.reshape(MICRO, TOKENS, D), weight_grads[0], weight_grads[1], weight_grads[2], weight_grads[3], weight_grads[4], weight_grads[5], weight_grads[6], weight_grads[7], weight_grads[8], weight_grads[9])
```

```python
import math

import jax
import jax.numpy as jnp
from jax import lax
from jax.sharding import Mesh
from jax.sharding import PartitionSpec as P

HEAD_DIM = 64
ROT = 16
EPS = 1e-05

AXES = ("e", "zh", "zl", "x", "y", "c")
HEAD_BITS = ("zh", "zl", "x", "y")
T1, T2, D1, D2 = "y", "zl", "zh", "x"
TP = (T1, T2, "c")
DP = ("e", D1, D2)

F32, BF16 = jnp.float32, jnp.bfloat16


def swap(value, *axes):
    pairs = []
    sizes = 2 ** len(axes)
    for i in range(sizes):
        pairs.append((i, sizes - 1 - i))
    return lax.ppermute(value, tuple(sorted(axes, key=AXES.index)), pairs)


def pick(value, dim, index):
    return lax.dynamic_index_in_dim(value, index, dim, keepdims=False)


def pair(value, axis):
    other = swap(value, axis)
    first = lax.axis_index(axis) == 0
    return jnp.where(first, jnp.stack([value, other]), jnp.stack([other, value]))


def gather_dp(value):
    out = pair(pair(value, D1), D2)
    out = jnp.swapaxes(out, 0, 1)
    return lax.all_gather(out, "e", axis=0)


def fold(value, dim, axis):
    index = lax.axis_index(axis)
    kept = pick(value, dim, index)
    sent = pick(value, dim, 1 - index).astype(BF16)
    return kept + swap(sent, axis).astype(F32)


def scatter_dp(value):
    if value.shape[0] > 1:
        value = lax.psum_scatter(value, "e", scatter_dimension=0, tiled=True)
    value = value[0]
    return fold(fold(value, 1, D2), 0, D1)


def trade(value, dim, axis):
    index = lax.axis_index(axis)
    kept = pick(value, dim, index)
    got = swap(pick(value, dim, 1 - index), axis)
    return jnp.where(
        index == 0, jnp.stack([kept, got], dim), jnp.stack([got, kept], dim)
    )


def trade_tp(value):
    return trade(trade(trade(value, 2, "c"), 1, T2), 0, T1)


def gather_rows(value):
    pieces = [value, swap(value, T2), swap(value, T1), swap(value, T1, T2)]
    near = jnp.stack(pieces)
    return jnp.stack([near, swap(near, "c")], 1)


def scatter_rows(value):
    near = value[:, 0] + swap(value[:, 1].astype(BF16), "c").astype(F32)
    sent = near[1:].astype(BF16)
    got = [swap(sent[0], T2), swap(sent[1], T1), swap(sent[2], T1, T2)]
    return near[0] + got[0].astype(F32) + got[1].astype(F32) + got[2].astype(F32)


def gather_small(value):
    for axis in reversed(AXES[1:]):
        value = pair(value, axis)
        value = value.reshape((-1,) + value.shape[2:]) if value.ndim > 2 else value
    return lax.all_gather(value, "e", axis=0, tiled=True)


def scatter_small(value):
    devices = value.shape[0]
    extra = devices // 32
    if extra > 1:
        value = lax.psum_scatter(value, "e", scatter_dimension=0, tiled=True)
    for axis in AXES[1:]:
        value = value.reshape((2, value.shape[0] // 2) + value.shape[1:])
        index = lax.axis_index(axis)
        value = pick(value, 0, index) + swap(pick(value, 0, 1 - index), axis)
    return value[0]


def split_heads(value, parts):
    lead = value.ndim - 1
    value = value.reshape(value.shape[:-1] + (parts, 2, 2, 2, 2, HEAD_DIM))
    place = {axis: lead + 1 + i for i, axis in enumerate(HEAD_BITS)}
    order = [place[T1], place[T2], place[D2]] + list(range(lead + 1)) + [place[D1], lead + 5]
    return value.transpose(order)


def join_heads(value):
    lead = value.ndim - 6
    names = {T1: 0, T2: 1, D2: 2, D1: lead + 4}
    order = [3 + i for i in range(lead)] + [3 + lead] + [names[a] for a in HEAD_BITS] + [lead + 5]
    value = value.transpose(order)
    return value.reshape(value.shape[:lead] + (-1,))


def split_hidden(value, extra):
    lead = value.ndim - 1
    value = value.reshape(value.shape[:-1] + (extra, 2, 2, 2, 2, 2, -1))
    place = {axis: lead + i for i, axis in enumerate(AXES)}
    order = [place[a] for a in TP] + list(range(lead)) + [place[a] for a in DP] + [lead + 6]
    return value.transpose(order)


def join_hidden(value):
    lead = value.ndim - 7
    names = {a: i for i, a in enumerate(TP)} | {a: 3 + lead + i for i, a in enumerate(DP)}
    order = [3 + i for i in range(lead)] + [names[a] for a in AXES] + [lead + 6]
    value = value.transpose(order)
    return value.reshape(value.shape[:lead] + (-1,))


def whole_rows(value):
    names = {a: i for i, a in enumerate(DP + TP)}
    order = [names[a] for a in AXES] + list(range(6, value.ndim))
    value = value.transpose(order)
    return value.reshape((-1,) + value.shape[7:])


def part_rows(value, extra):
    rows = value.shape[0]
    value = value.reshape((extra, 2, 2, 2, 2, 2, rows // (32 * extra)) + value.shape[1:])
    place = {axis: i for i, axis in enumerate(AXES)}
    return value.transpose([place[a] for a in DP + TP] + list(range(6, value.ndim)))


def own_part(value):
    for axis in TP:
        value = pick(value, 0, lax.axis_index(axis))
    return value


def gather_proj(block, extra):
    width = block.shape[1]
    if extra > 1:
        whole = lax.all_gather(block, AXES, axis=0, tiled=True)
        parted = split_heads(whole.T, 1)
        return own_part(parted).reshape(width, -1).T
    near = pair(pair(block, D1), D2)
    near = trade(near, 0, "c")
    return near.transpose(1, 0, 2, 3).reshape(-1, width)


def scatter_proj(value, extra):
    width = value.shape[1]
    if extra > 1:
        whole = jnp.zeros((2, 2, 2, 1, 2, HEAD_DIM, width), F32)
        place = [lax.axis_index(a) for a in TP] + [0, 0, 0, 0]
        whole = lax.dynamic_update_slice(whole, value.reshape(1, 1, 1, 1, 2, HEAD_DIM, width), place)
        names = {T1: 0, T2: 1, D2: 2, D1: 4}
        whole = whole.transpose([names[a] for a in HEAD_BITS] + [3, 5, 6]).reshape(-1, width)
        return lax.psum_scatter(whole, AXES, scatter_dimension=0, tiled=True)
    value = value.reshape(2, 2, HEAD_DIM // 2, width).transpose(1, 0, 2, 3)
    index = lax.axis_index("c")
    kept = pick(value, 0, index)
    got = swap(pick(value, 0, 1 - index).astype(BF16), "c").astype(F32)
    value = jnp.where(index == 0, jnp.stack([kept, got]), jnp.stack([got, kept]))
    return fold(fold(value, 0, D2), 0, D1)


def rotate(vectors, cosine, sine):
    half = cosine.shape[-1]
    a, b = vectors[..., :half], vectors[..., half : 2 * half]
    return jnp.concatenate(
        [a * cosine - b * sine, b * cosine + a * sine, vectors[..., 2 * half :]], axis=-1
    )


def normalise(stream):
    average = jnp.mean(stream, axis=-1, keepdims=True)
    centred = stream - average
    variance = jnp.mean(centred * centred, axis=-1, keepdims=True)
    inverse = lax.rsqrt(variance + EPS)
    return centred * inverse, inverse


def dot(a, b, contract):
    return lax.dot_general(a, b, (contract, ((), ())), preferred_element_type=F32)


def forward(hidden, weights, allowed, cosine, sine):
    qkv, qkv_bias, proj, up, up_bias, down = weights
    rows, packs, pack = hidden.shape[0], allowed.shape[0], allowed.shape[1]
    merged = dot(hidden, qkv, ((1,), (0,))) + qkv_bias
    merged = merged.reshape(packs, pack, 3, 2, HEAD_DIM)
    queries = rotate(merged[:, :, 0], cosine, sine).astype(BF16)
    keys = rotate(merged[:, :, 1], cosine, sine).astype(BF16)
    values = merged[:, :, 2].astype(BF16)
    scores = jnp.einsum("pqhd,pkhd->phqk", queries, keys, preferred_element_type=F32)
    scores = jnp.where(allowed[:, None], scores * (1.0 / math.sqrt(HEAD_DIM)), -1e30)
    shifted = jnp.exp(scores - jnp.max(scores, axis=-1, keepdims=True))
    soft = shifted / jnp.sum(shifted, axis=-1, keepdims=True)
    context = jnp.einsum("phqk,pkhd->pqhd", soft.astype(BF16), values, preferred_element_type=F32)
    context = context.reshape(rows, 2 * HEAD_DIM).astype(BF16)
    raised = dot(hidden, up, ((1,), (0,))) + up_bias
    cdf = 0.5 * (1.0 + lax.erf(raised * 0.7071067811865476))
    density = jnp.exp(-0.5 * raised * raised) * 0.3989422804014327
    activation = (raised * cdf).astype(BF16)
    slope = cdf + raised * density
    partial = dot(context, proj, ((1,), (0,))) + dot(activation, down, ((1,), (0,)))
    return partial, (queries, keys, values, soft, context, activation, slope)


def backward(hidden, rounded, weights, stored, cosine, sine):
    qkv, _, proj, up, _, down = weights
    queries, keys, values, soft, context, activation, slope = stored
    rows, packs, pack = hidden.shape[0], queries.shape[0], queries.shape[1]
    up_delta = (dot(rounded, down, ((1,), (1,))) * slope).astype(BF16)
    context_delta = dot(rounded, proj, ((1,), (1,))).astype(BF16)
    context_delta = context_delta.reshape(packs, pack, 2, HEAD_DIM)
    down_grad = dot(activation, rounded, ((0,), (0,)))
    proj_grad = dot(context, rounded, ((0,), (0,)))
    value_delta = jnp.einsum(
        "phqk,pqhd->pkhd", soft.astype(BF16), context_delta, preferred_element_type=F32
    )
    prob_delta = jnp.einsum("pqhd,pkhd->phqk", context_delta, values, preferred_element_type=F32)
    row_delta = jnp.sum(soft * prob_delta, axis=-1, keepdims=True)
    score_delta = (soft * (prob_delta - row_delta)).astype(BF16)
    scale = 1.0 / math.sqrt(HEAD_DIM)
    query_delta = jnp.einsum("phqk,pkhd->pqhd", score_delta, keys, preferred_element_type=F32)
    key_delta = jnp.einsum("phqk,pqhd->pkhd", score_delta, queries, preferred_element_type=F32)
    merged_delta = jnp.stack(
        [
            rotate(query_delta * scale, cosine, -sine),
            rotate(key_delta * scale, cosine, -sine),
            value_delta,
        ],
        axis=2,
    )
    merged_delta = merged_delta.astype(BF16).reshape(rows, -1)
    partial = dot(merged_delta, qkv, ((1,), (1,))) + dot(up_delta, up, ((1,), (1,)))
    up_grad = dot(hidden, up_delta, ((0,), (0,)))
    qkv_grad = dot(hidden, merged_delta, ((0,), (0,)))
    upbias_grad = jnp.sum(up_delta, axis=0, dtype=F32)
    qkvbias_grad = jnp.sum(merged_delta, axis=0, dtype=F32)
    return partial, (qkv_grad, qkvbias_grad, proj_grad, up_grad, upbias_grad, down_grad)


def shards(
    inputs,
    cotangent,
    segments,
    pack_length,
    norm_gain,
    norm_shift,
    qkv_weight,
    qv_bias,
    proj_weight,
    proj_bias,
    up_weight,
    up_bias,
    down_weight,
    down_bias,
):
    micros, pack, width = inputs.shape
    layers = qkv_weight.shape[0]
    extra = lax.axis_size("e")
    devices = 32 * extra
    position = jnp.arange(pack)
    is_live = position[None, :] < pack_length
    marks = gather_rows(jnp.concatenate([segments, pack_length], axis=1)).reshape(-1, pack + 1)
    group_segments, group_length = marks[:, :pack], marks[:, pack:]
    group_live = position[None, :] < group_length
    causal = position[:, None] >= position[None, :]
    diagonal = position[:, None] == position[None, :]
    allowed = (
        (group_segments[:, :, None] == group_segments[:, None, :])
        & causal
        & (group_live[:, None, :] | diagonal)
    )
    angle = position.astype(F32)[:, None] * (
        10000.0 ** (-jnp.arange(0, ROT, 2, dtype=F32) / ROT)
    )[None, :]
    cosine, sine = jnp.cos(angle)[:, None, :], jnp.sin(angle)[:, None, :]

    small = jnp.concatenate(
        [norm_gain, norm_shift, qv_bias, proj_bias, up_bias, down_bias], axis=1
    )
    cuts = [norm_gain.shape[1], norm_shift.shape[1], qv_bias.shape[1], proj_bias.shape[1]]
    cuts = cuts + [up_bias.shape[1], down_bias.shape[1]]
    offsets = [sum(cuts[:i]) for i in range(7)]
    small = gather_small(small.reshape(-1)).reshape(devices, layers, -1).astype(F32)
    vectors = []
    for layer in range(layers):
        vectors.append(
            [small[:, layer, offsets[i] : offsets[i + 1]].reshape(-1) for i in range(6)]
        )

    weights = []
    for layer in range(layers):
        gain, shift, qv, projb, upb, downb = vectors[layer]
        qkv_parts = split_heads(qkv_weight[layer], 3)
        qkv_parts = qkv_parts.reshape(qkv_parts.shape[:4] + (-1,))
        up_parts = split_hidden(up_weight[layer], extra)
        up_parts = up_parts.reshape(up_parts.shape[:4] + (-1,))
        qkv_block = trade_tp(qkv_parts)
        up_block = trade_tp(up_parts)
        qkv = whole_rows(gather_dp(qkv_block))
        up = whole_rows(gather_dp(up_block))
        proj = gather_proj(proj_weight[layer], extra)
        down = gather_dp(down_weight[layer]).reshape(-1, width)
        q_bias = own_part(split_heads(qv[:width], 1)).reshape(-1)
        v_bias = own_part(split_heads(qv[width:], 1)).reshape(-1)
        bias = jnp.concatenate([q_bias, jnp.zeros_like(q_bias), v_bias])
        upb = own_part(split_hidden(upb, extra)).reshape(-1)
        weights.append((qkv, bias, proj, up, upb, down))

    stream = inputs.astype(F32)
    kept = []
    for layer in range(layers):
        gain, shift, _, projb, _, downb = vectors[layer]
        normed, inverse = normalise(stream)
        hidden = (normed * gain + shift).astype(BF16)
        group_hidden = gather_rows(hidden).reshape(-1, width)
        partial, stored = forward(group_hidden, weights[layer], allowed, cosine, sine)
        kept.append((normed, inverse, group_hidden, stored))
        total = scatter_rows(partial.reshape(4, 2, micros, pack, width))
        stream = stream + total + (projb + downb)
    outputs = stream.astype(BF16)

    upstream = cotangent.astype(F32) * is_live[:, :, None].astype(F32)
    grads = [None] * layers
    for layer in reversed(range(layers)):
        gain = vectors[layer][0]
        normed, inverse, group_hidden, stored = kept[layer]
        rounded = upstream.astype(BF16)
        bias_sum = jnp.sum(rounded, axis=(0, 1), dtype=F32)
        group_rounded = gather_rows(rounded).reshape(-1, width)
        partial, slices = backward(
            group_hidden, group_rounded, weights[layer], stored, cosine, sine
        )
        qkv_grad, qkvbias_grad, proj_grad, up_grad, upbias_grad, down_grad = slices
        hidden_delta = scatter_rows(partial.reshape(4, 2, micros, pack, width))
        gain_grad = jnp.sum(hidden_delta * normed, axis=(0, 1))
        shift_grad = jnp.sum(hidden_delta, axis=(0, 1))
        scaled = hidden_delta * gain
        upstream = upstream + inverse * (
            scaled
            - jnp.mean(scaled, axis=-1, keepdims=True)
            - normed * jnp.mean(scaled * normed, axis=-1, keepdims=True)
        )
        down_own = scatter_dp(down_grad.reshape(extra, 2, 2, -1, width))
        proj_own = scatter_proj(proj_grad, extra)
        up_own = trade_tp(scatter_dp(part_rows(up_grad, extra)).astype(BF16))
        qkv_own = trade_tp(scatter_dp(part_rows(qkv_grad, extra)).astype(BF16))
        rows = up_own.shape[3]
        up_own = join_hidden(up_own.reshape(2, 2, 2, rows, extra, 2, 2, -1)).astype(F32)
        qkv_own = join_heads(qkv_own.reshape(2, 2, 2, rows, 3, 2, HEAD_DIM)).astype(F32)

        place = [lax.axis_index(a) for a in TP]
        per = qkvbias_grad.shape[0] // 3
        wide = jnp.zeros((2, 2, 2, 2, 2, HEAD_DIM), F32)
        both = jnp.stack([qkvbias_grad[:per], qkvbias_grad[2 * per :]]).reshape(1, 1, 1, 2, 2, HEAD_DIM)
        qv_full = join_heads(lax.dynamic_update_slice(wide, both, place + [0, 0, 0])[:, :, :, :, :, :])
        chunk = up_bias.shape[1]
        wide = jnp.zeros((2, 2, 2, extra, 2, 2, chunk), F32)
        upb_full = join_hidden(
            lax.dynamic_update_slice(
                wide, upbias_grad.reshape(1, 1, 1, extra, 2, 2, chunk), place + [0] * 4
            )
        )
        small_grad = jnp.concatenate(
            [
                v.reshape(devices, -1)
                for v in (gain_grad, shift_grad, qv_full, bias_sum, upb_full)
            ],
            axis=1,
        )
        grads[layer] = (small_grad, qkv_own, proj_own, up_own, down_own)
    input_grad = upstream

    small_out = scatter_small(jnp.stack([g[0] for g in grads], axis=1))
    bounds = [0]
    for size in (cuts[0], cuts[1], cuts[2], cuts[3], cuts[4]):
        bounds.append(bounds[-1] + size)
    gain_out, shift_out, qvbias_out, projbias_out, upbias_out = [
        small_out[:, bounds[i] : bounds[i + 1]] for i in range(5)
    ]
    return (
        outputs,
        input_grad,
        gain_out,
        shift_out,
        jnp.stack([g[1] for g in grads]),
        qvbias_out,
        jnp.stack([g[2] for g in grads]),
        projbias_out,
        jnp.stack([g[3] for g in grads]),
        upbias_out,
        jnp.stack([g[4] for g in grads]),
        projbias_out,
    )


def solution(mesh):
    devices = mesh.devices.size
    fine = Mesh(mesh.devices.reshape(devices // 32, 2, 2, 2, 2, 2), AXES)
    cube, flat = P(None, AXES, None), P(None, AXES)
    placed = (cube, cube, flat, flat, flat, flat, cube, flat, cube, flat, cube, flat, cube, flat)
    given = (cube, cube, flat, flat, cube, flat, cube, flat, cube, flat, cube, flat)
    return jax.shard_map(shards, mesh=fine, in_specs=placed, out_specs=given, check_vma=False)
```

```python
import math

import jax
import jax.numpy as jnp
from jax import lax
from jax.experimental import pallas as pl
from jax.experimental.pallas import tpu as pltpu
from jax.sharding import Mesh
from jax.sharding import PartitionSpec as P

HEAD_DIM = 64
ROT = 16
EPS = 1e-05

AXES = ("e", "zh", "zl", "x", "y", "c")
HEAD_BITS = ("zh", "zl", "x", "y")
T1, T2, D1, D2 = "y", "zl", "zh", "x"
TP = (T1, T2, "c")
DP = (D1, D2)

F32, BF16 = jnp.float32, jnp.bfloat16


def swap(value, *axes):
    pairs = []
    sizes = 2 ** len(axes)
    for i in range(sizes):
        pairs.append((i, sizes - 1 - i))
    return lax.ppermute(value, tuple(sorted(axes, key=AXES.index)), pairs)


def pick(value, dim, index):
    return lax.dynamic_index_in_dim(value, index, dim, keepdims=False)


def pair(value, axis):
    other = swap(value, axis)
    first = lax.axis_index(axis) == 0
    return jnp.where(first, jnp.stack([value, other]), jnp.stack([other, value]))


def fold(value, dim, axis):
    index = lax.axis_index(axis)
    kept = pick(value, dim, index)
    sent = pick(value, dim, 1 - index).astype(BF16)
    return kept + swap(sent, axis).astype(F32)


def trade(value, dim, axis):
    index = lax.axis_index(axis)
    kept = pick(value, dim, index)
    got = swap(pick(value, dim, 1 - index), axis)
    return jnp.where(
        index == 0, jnp.stack([kept, got], dim), jnp.stack([got, kept], dim)
    )


def trade_tp(value):
    return trade(trade(trade(value, 2, "c"), 1, T2), 0, T1)


def gather_rows(value):
    pieces = [value, swap(value, T2), swap(value, T1), swap(value, T1, T2)]
    near = jnp.stack(pieces)
    return jnp.stack([near, swap(near, "c")], 1)


def scatter_rows(value):
    near = value[:, 0] + swap(value[:, 1].astype(BF16), "c").astype(F32)
    sent = near[1:].astype(BF16)
    got = [swap(sent[0], T2), swap(sent[1], T1), swap(sent[2], T1, T2)]
    return near[0] + got[0].astype(F32) + got[1].astype(F32) + got[2].astype(F32)


def gather_small(value):
    for axis in reversed(AXES[1:]):
        value = pair(value, axis)
        value = value.reshape((-1,) + value.shape[2:]) if value.ndim > 2 else value
    return lax.all_gather(value, "e", axis=0, tiled=True)


def scatter_small(value):
    devices = value.shape[0]
    extra = devices // 32
    if extra > 1:
        value = lax.psum_scatter(value, "e", scatter_dimension=0, tiled=True)
    for axis in AXES[1:]:
        value = value.reshape((2, value.shape[0] // 2) + value.shape[1:])
        index = lax.axis_index(axis)
        value = pick(value, 0, index) + swap(pick(value, 0, 1 - index), axis)
    return value[0]


def split_heads(value, parts):
    lead = value.ndim - 1
    value = value.reshape(value.shape[:-1] + (parts, 2, 2, 2, 2, HEAD_DIM))
    place = {axis: lead + 1 + i for i, axis in enumerate(HEAD_BITS)}
    order = [place[T1], place[T2], place[D2]] + list(range(lead + 1)) + [place[D1], lead + 5]
    return value.transpose(order)


def join_heads(value):
    lead = value.ndim - 6
    names = {T1: 0, T2: 1, D2: 2, D1: lead + 4}
    order = [3 + i for i in range(lead)] + [3 + lead] + [names[a] for a in HEAD_BITS] + [lead + 5]
    value = value.transpose(order)
    return value.reshape(value.shape[:lead] + (-1,))


def part_rows(value):
    value = value.reshape((2, 2, 2, 2, 2, value.shape[0] // 32) + value.shape[1:])
    place = {axis: i for i, axis in enumerate(AXES[1:])}
    return value.transpose([place[a] for a in DP + TP] + list(range(5, value.ndim)))


def own_part(value):
    for axis in TP:
        value = pick(value, 0, lax.axis_index(axis))
    return value


def scatter_proj(value):
    width = value.shape[1]
    value = value.reshape(2, 2, HEAD_DIM // 2, width).transpose(1, 0, 2, 3)
    index = lax.axis_index("c")
    kept = pick(value, 0, index)
    got = swap(pick(value, 0, 1 - index).astype(BF16), "c").astype(F32)
    value = jnp.where(index == 0, jnp.stack([kept, got]), jnp.stack([got, kept]))
    return fold(fold(value, 0, D2), 0, D1)


MESH = pl.DeviceIdType.MESH
NEAR = (("c",), (T1,), (T2,), (T1, "c"), (T2, "c"), (T1, T2), (T1, T2, "c"))
FAR = ((D1,), (D2,))


class Links:
    def __init__(self, send_sem, recv_sem):
        self.place = {axis: lax.axis_index(axis) for axis in AXES}
        self.send_sem, self.recv_sem, self.used = send_sem, recv_sem, 0

    def peer(self, axes):
        return {axis: 1 - self.place[axis] for axis in axes}

    def meet(self):
        barrier = pltpu.get_barrier_semaphore()
        for axes in NEAR + FAR:
            pl.semaphore_signal(barrier, inc=1, device_id=self.peer(axes), device_id_type=MESH)
        pl.semaphore_wait(barrier, len(NEAR) + len(FAR))

    def copy(self, source, target, axes):
        i = self.used
        self.used += 1
        return pltpu.make_async_remote_copy(
            src_ref=source,
            dst_ref=target,
            send_sem=self.send_sem.at[i],
            recv_sem=self.recv_sem.at[i],
            device_id=self.peer(axes),
            device_id_type=MESH,
        )


def rank_of(place):
    return place[T1] * 4 + place[T2] * 2 + place["c"]


def block_of(place):
    index = place["zh"]
    for axis in AXES[2:]:
        index = index * 2 + place[axis]
    return index


def flipped(place, axes):
    return {a: (1 - i if a in axes else i) for a, i in place.items()}


def gather_kernel(parts, down, proj, cat_all, down_all, proj_all, send_sem, recv_sem, own_sem):
    links = Links(send_sem, recv_sem)
    me = links.place
    layers = parts.shape[0]
    own = []
    for layer in range(layers):
        own.append(
            pltpu.make_async_copy(
                parts.at[layer, rank_of(me)], cat_all.at[layer, block_of(me)], own_sem.at[layer, 0]
            )
        )
        own.append(
            pltpu.make_async_copy(
                down.at[layer], down_all.at[layer, me[D2] * 2 + me[D1]], own_sem.at[layer, 1]
            )
        )
    for copy in own:
        copy.start()
    links.meet()
    for layer in range(layers):
        trades = []
        for axes in NEAR:
            trades.append(
                links.copy(
                    parts.at[layer, rank_of(flipped(me, axes))],
                    cat_all.at[layer, block_of(me)],
                    axes,
                )
            )
        for copy in trades:
            copy.start()
        slot = me[D2] * 2 + me[D1]
        down_first = links.copy(down.at[layer], down_all.at[layer, slot], (D1,))
        down_first.start()
        half = proj_all.at[layer, me["zh"], me["c"]]
        to_core = links.copy(proj.at[layer], half, ("c",))
        stays = pltpu.make_async_copy(proj.at[layer], half, own_sem.at[layer, 2])
        mine = me["c"] == me[D2]

        @pl.when(mine)
        def _():
            stays.start()
            stays.wait()

        @pl.when(jnp.logical_not(mine))
        def _():
            to_core.start()
            to_core.wait_send()

        proj_first = links.copy(
            proj_all.at[layer, me["zh"]], proj_all.at[layer, me["zh"]], (D1,)
        )
        proj_second = links.copy(proj_all.at[layer], proj_all.at[layer], (D2,))

        @pl.when(mine)
        def _():
            to_core.wait_recv()
            proj_first.start()

        for copy in trades:
            copy.wait()
        own[2 * layer].wait()
        own[2 * layer + 1].wait()
        firsts = []
        for zl in range(2):
            rows = cat_all.at[layer, pl.ds(me["zh"] * 16 + zl * 8 + me["x"] * 4, 4)]
            firsts.append(links.copy(rows, rows, (D1,)))
        for copy in firsts:
            copy.start()
        down_first.wait()
        both = down_all.at[layer, pl.ds(me[D2] * 2, 2)]
        down_second = links.copy(both, both, (D2,))
        down_second.start()

        @pl.when(mine)
        def _():
            proj_first.wait()
            proj_second.start()
            proj_second.wait_send()

        seconds = []
        for zl in range(2):
            firsts[zl].wait()
            for zh in range(2):
                rows = cat_all.at[layer, pl.ds(zh * 16 + zl * 8 + me["x"] * 4, 4)]
                copy = links.copy(rows, rows, (D2,))
                copy.start()
                seconds.append(copy)
        for copy in seconds:
            copy.wait()
        down_second.wait()

        @pl.when(jnp.logical_not(mine))
        def _():
            proj_second.wait_recv()


def gather_weights(parts, down, proj):
    layers, _, rows, columns = parts.shape
    copies = 32 * layers
    vmem = pl.BlockSpec(memory_space=pltpu.VMEM)
    return pl.pallas_call(
        gather_kernel,
        out_shape=(
            jax.ShapeDtypeStruct((layers, 32, rows, columns), BF16),
            jax.ShapeDtypeStruct((layers, 4) + down.shape[1:], BF16),
            jax.ShapeDtypeStruct((layers, 2, 2) + proj.shape[1:], BF16),
        ),
        in_specs=[vmem] * 3,
        out_specs=(vmem, vmem, vmem),
        scratch_shapes=[
            pltpu.SemaphoreType.DMA((copies,)),
            pltpu.SemaphoreType.DMA((copies,)),
            pltpu.SemaphoreType.DMA((layers, 3)),
        ],
        compiler_params=pltpu.CompilerParams(
            collective_id=0, has_side_effects=True, vmem_limit_bytes=48 << 20
        ),
    )(parts, down, proj)


def refold(block, extra, width):
    if extra == 1:
        return block
    whole = lax.all_gather(block, AXES, axis=1, tiled=True)
    index = lax.axis_index(AXES[1:])
    rows = whole.shape[1] // 32
    return lax.dynamic_slice_in_dim(whole, index * rows, rows, 1)


def unfold(block, extra):
    if extra == 1:
        return block
    rows = block.shape[0]
    whole = jnp.zeros((32 * rows,) + block.shape[1:], F32)
    whole = lax.dynamic_update_slice_in_dim(whole, block, lax.axis_index(AXES[1:]) * rows, 0)
    return lax.psum_scatter(whole, AXES, scatter_dimension=0, tiled=True)


def join_columns(value):
    lead = value.ndim - 6
    names = {a: i for i, a in enumerate(TP)} | {D2: 3 + lead, D1: 4 + lead}
    order = [3 + i for i in range(lead)] + [names[a] for a in AXES[1:]] + [lead + 5]
    value = value.transpose(order)
    return value.reshape(value.shape[:lead] + (-1,))


def split_columns(value):
    value = value.reshape(value.shape[:2] + (2, 2, 2, 2, 2, -1))
    place = {axis: 2 + i for i, axis in enumerate(AXES[1:])}
    return value.transpose([0] + [place[a] for a in TP] + [1, place[D2], place[D1], 7])


def rotate(vectors, cosine, sine):
    half = cosine.shape[-1]
    a, b = vectors[..., :half], vectors[..., half : 2 * half]
    return jnp.concatenate(
        [a * cosine - b * sine, b * cosine + a * sine, vectors[..., 2 * half :]], axis=-1
    )


def normalise(stream):
    average = jnp.mean(stream, axis=-1, keepdims=True)
    centred = stream - average
    variance = jnp.mean(centred * centred, axis=-1, keepdims=True)
    inverse = lax.rsqrt(variance + EPS)
    return centred * inverse, inverse


def dot(a, b, contract):
    return lax.dot_general(a, b, (contract, ((), ())), preferred_element_type=F32)


def forward(hidden, weights, allowed, cosine, sine):
    qkv, qkv_bias, proj, up, up_bias, down = weights
    rows, packs, pack = hidden.shape[0], allowed.shape[0], allowed.shape[1]
    merged = dot(hidden, qkv, ((1,), (0,))) + qkv_bias
    merged = merged.reshape(packs, pack, 3, 2, HEAD_DIM)
    queries = rotate(merged[:, :, 0], cosine, sine).astype(BF16)
    keys = rotate(merged[:, :, 1], cosine, sine).astype(BF16)
    values = merged[:, :, 2].astype(BF16)
    scores = jnp.einsum("pqhd,pkhd->phqk", queries, keys, preferred_element_type=F32)
    scores = jnp.where(allowed[:, None], scores * (1.0 / math.sqrt(HEAD_DIM)), -1e30)
    shifted = jnp.exp(scores - jnp.max(scores, axis=-1, keepdims=True))
    soft = shifted / jnp.sum(shifted, axis=-1, keepdims=True)
    context = jnp.einsum("phqk,pkhd->pqhd", soft.astype(BF16), values, preferred_element_type=F32)
    context = context.reshape(rows, 2 * HEAD_DIM).astype(BF16)
    raised = dot(hidden, up, ((1,), (0,))) + up_bias
    cdf = 0.5 * (1.0 + lax.erf(raised * 0.7071067811865476))
    density = jnp.exp(-0.5 * raised * raised) * 0.3989422804014327
    activation = (raised * cdf).astype(BF16)
    slope = cdf + raised * density
    partial = dot(context, proj, ((1,), (0,))) + dot(activation, down, ((1,), (0,)))
    return partial, (queries, keys, values, soft, context, activation, slope)


def backward(hidden, rounded, weights, stored, cosine, sine):
    qkv, _, proj, up, _, down = weights
    queries, keys, values, soft, context, activation, slope = stored
    rows, packs, pack = hidden.shape[0], queries.shape[0], queries.shape[1]
    up_delta = (dot(rounded, down, ((1,), (1,))) * slope).astype(BF16)
    context_delta = dot(rounded, proj, ((1,), (1,))).astype(BF16)
    context_delta = context_delta.reshape(packs, pack, 2, HEAD_DIM)
    down_grad = dot(activation, rounded, ((0,), (0,)))
    proj_grad = dot(context, rounded, ((0,), (0,)))
    value_delta = jnp.einsum(
        "phqk,pqhd->pkhd", soft.astype(BF16), context_delta, preferred_element_type=F32
    )
    prob_delta = jnp.einsum("pqhd,pkhd->phqk", context_delta, values, preferred_element_type=F32)
    row_delta = jnp.sum(soft * prob_delta, axis=-1, keepdims=True)
    score_delta = (soft * (prob_delta - row_delta)).astype(BF16)
    scale = 1.0 / math.sqrt(HEAD_DIM)
    query_delta = jnp.einsum("phqk,pkhd->pqhd", score_delta, keys, preferred_element_type=F32)
    key_delta = jnp.einsum("phqk,pqhd->pkhd", score_delta, queries, preferred_element_type=F32)
    merged_delta = jnp.stack(
        [
            rotate(query_delta * scale, cosine, -sine),
            rotate(key_delta * scale, cosine, -sine),
            value_delta,
        ],
        axis=2,
    )
    merged_delta = merged_delta.astype(BF16).reshape(rows, -1)
    partial = dot(merged_delta, qkv, ((1,), (1,))) + dot(up_delta, up, ((1,), (1,)))
    up_grad = dot(hidden, up_delta, ((0,), (0,)))
    qkv_grad = dot(hidden, merged_delta, ((0,), (0,)))
    upbias_grad = jnp.sum(up_delta, axis=0, dtype=F32)
    qkvbias_grad = jnp.sum(merged_delta, axis=0, dtype=F32)
    return partial, (qkv_grad, qkvbias_grad, proj_grad, up_grad, upbias_grad, down_grad)


def shards(
    inputs,
    cotangent,
    segments,
    pack_length,
    norm_gain,
    norm_shift,
    qkv_weight,
    qv_bias,
    proj_weight,
    proj_bias,
    up_weight,
    up_bias,
    down_weight,
    down_bias,
):
    micros, pack, width = inputs.shape
    layers = qkv_weight.shape[0]
    extra = lax.axis_size("e")
    devices = 32 * extra
    position = jnp.arange(pack)
    is_live = position[None, :] < pack_length
    marks = gather_rows(jnp.concatenate([segments, pack_length], axis=1)).reshape(-1, pack + 1)
    group_segments, group_length = marks[:, :pack], marks[:, pack:]
    group_live = position[None, :] < group_length
    causal = position[:, None] >= position[None, :]
    diagonal = position[:, None] == position[None, :]
    allowed = (
        (group_segments[:, :, None] == group_segments[:, None, :])
        & causal
        & (group_live[:, None, :] | diagonal)
    )
    angle = position.astype(F32)[:, None] * (
        10000.0 ** (-jnp.arange(0, ROT, 2, dtype=F32) / ROT)
    )[None, :]
    cosine, sine = jnp.cos(angle)[:, None, :], jnp.sin(angle)[:, None, :]

    small = jnp.concatenate(
        [norm_gain, norm_shift, qv_bias, proj_bias, up_bias, down_bias], axis=1
    )
    cuts = [norm_gain.shape[1], norm_shift.shape[1], qv_bias.shape[1], proj_bias.shape[1]]
    cuts = cuts + [up_bias.shape[1], down_bias.shape[1]]
    offsets = [sum(cuts[:i]) for i in range(7)]
    small = gather_small(small.reshape(-1)).reshape(devices, layers, -1).astype(F32)
    vectors = []
    for layer in range(layers):
        vectors.append(
            [small[:, layer, offsets[i] : offsets[i + 1]].reshape(-1) for i in range(6)]
        )

    qkv_mine, up_mine = refold(qkv_weight, extra, width), refold(up_weight, extra, width)
    proj_mine, down_mine = refold(proj_weight, extra, width), refold(down_weight, extra, width)
    rows = qkv_mine.shape[1]
    qkv_parts = jnp.stack([split_heads(qkv_mine[l], 3) for l in range(layers)])
    parts = jnp.concatenate(
        [
            qkv_parts.reshape(layers, 8, rows, -1),
            split_columns(up_mine).reshape(layers, 8, rows, -1),
        ],
        axis=-1,
    )
    cat_all, down_all, proj_all = gather_weights(parts, down_mine, proj_mine)
    weights = []
    for layer in range(layers):
        gain, shift, qv, projb, upb, downb = vectors[layer]
        cat = cat_all[layer].reshape(width, -1)
        qkv, up = cat[:, : 6 * HEAD_DIM], cat[:, 6 * HEAD_DIM :]
        proj = proj_all[layer].reshape(-1, width)
        down = down_all[layer].reshape(-1, width)
        q_bias = own_part(split_heads(qv[:width], 1)).reshape(-1)
        v_bias = own_part(split_heads(qv[width:], 1)).reshape(-1)
        bias = jnp.concatenate([q_bias, jnp.zeros_like(q_bias), v_bias])
        upb = own_part(split_columns(upb[None, None])[0]).reshape(-1)
        weights.append((qkv, bias, proj, up, upb, down))

    stream = inputs.astype(F32)
    kept = []
    for layer in range(layers):
        gain, shift, _, projb, _, downb = vectors[layer]
        normed, inverse = normalise(stream)
        hidden = (normed * gain + shift).astype(BF16)
        group_hidden = gather_rows(hidden).reshape(-1, width)
        partial, stored = forward(group_hidden, weights[layer], allowed, cosine, sine)
        kept.append((normed, inverse, group_hidden, stored))
        total = scatter_rows(partial.reshape(4, 2, micros, pack, width))
        stream = stream + total + (projb + downb)
    outputs = stream.astype(BF16)

    upstream = cotangent.astype(F32) * is_live[:, :, None].astype(F32)
    grads = [None] * layers
    for layer in reversed(range(layers)):
        gain = vectors[layer][0]
        normed, inverse, group_hidden, stored = kept[layer]
        rounded = upstream.astype(BF16)
        bias_sum = jnp.sum(rounded, axis=(0, 1), dtype=F32)
        group_rounded = gather_rows(rounded).reshape(-1, width)
        partial, slices = backward(
            group_hidden, group_rounded, weights[layer], stored, cosine, sine
        )
        qkv_grad, qkvbias_grad, proj_grad, up_grad, upbias_grad, down_grad = slices
        hidden_delta = scatter_rows(partial.reshape(4, 2, micros, pack, width))
        gain_grad = jnp.sum(hidden_delta * normed, axis=(0, 1))
        shift_grad = jnp.sum(hidden_delta, axis=(0, 1))
        scaled = hidden_delta * gain
        upstream = upstream + inverse * (
            scaled
            - jnp.mean(scaled, axis=-1, keepdims=True)
            - normed * jnp.mean(scaled * normed, axis=-1, keepdims=True)
        )
        down_grad = down_grad.reshape(2, 2, -1, width)
        down_own = unfold(fold(fold(down_grad, 0, D2), 0, D1), extra)
        proj_own = unfold(scatter_proj(proj_grad), extra)
        cat_grad = part_rows(jnp.concatenate([qkv_grad, up_grad], axis=1))
        cat_own = trade_tp(fold(fold(cat_grad, 1, D2), 0, D1).astype(BF16))
        rows = cat_own.shape[3]
        qkv_own, up_own = cat_own[..., : 6 * HEAD_DIM], cat_own[..., 6 * HEAD_DIM :]
        up_own = unfold(join_columns(up_own.reshape(2, 2, 2, rows, 2, 2, -1)).astype(F32), extra)
        qkv_own = join_heads(qkv_own.reshape(2, 2, 2, rows, 3, 2, HEAD_DIM)).astype(F32)
        qkv_own = unfold(qkv_own, extra)

        place = [lax.axis_index(a) for a in TP]
        per = qkvbias_grad.shape[0] // 3
        wide = jnp.zeros((2, 2, 2, 2, 2, HEAD_DIM), F32)
        both = jnp.stack([qkvbias_grad[:per], qkvbias_grad[2 * per :]]).reshape(1, 1, 1, 2, 2, HEAD_DIM)
        qv_full = join_heads(lax.dynamic_update_slice(wide, both, place + [0, 0, 0]))
        wide = jnp.zeros((2, 2, 2, 2, 2, upbias_grad.shape[0] // 4), F32)
        upb_full = join_columns(
            lax.dynamic_update_slice(wide, upbias_grad.reshape(1, 1, 1, 2, 2, -1), place + [0] * 3)
        )
        small_grad = jnp.concatenate(
            [
                v.reshape(devices, -1)
                for v in (gain_grad, shift_grad, qv_full, bias_sum, upb_full)
            ],
            axis=1,
        )
        grads[layer] = (small_grad, qkv_own, proj_own, up_own, down_own)
    input_grad = upstream

    small_out = scatter_small(jnp.stack([g[0] for g in grads], axis=1))
    bounds = [0]
    for size in (cuts[0], cuts[1], cuts[2], cuts[3], cuts[4]):
        bounds.append(bounds[-1] + size)
    gain_out, shift_out, qvbias_out, projbias_out, upbias_out = [
        small_out[:, bounds[i] : bounds[i + 1]] for i in range(5)
    ]
    return (
        outputs,
        input_grad,
        gain_out,
        shift_out,
        jnp.stack([g[1] for g in grads]),
        qvbias_out,
        jnp.stack([g[2] for g in grads]),
        projbias_out,
        jnp.stack([g[3] for g in grads]),
        upbias_out,
        jnp.stack([g[4] for g in grads]),
        projbias_out,
    )


def solution(mesh):
    devices = mesh.devices.size
    fine = Mesh(mesh.devices.reshape(devices // 32, 2, 2, 2, 2, 2), AXES)
    cube, flat = P(None, AXES, None), P(None, AXES)
    placed = (cube, cube, flat, flat, flat, flat, cube, flat, cube, flat, cube, flat, cube, flat)
    given = (cube, cube, flat, flat, cube, flat, cube, flat, cube, flat, cube, flat)
    return jax.shard_map(shards, mesh=fine, in_specs=placed, out_specs=given, check_vma=False)
```

```python
import math

import jax
import jax.numpy as jnp
import numpy as np
from jax import lax
from jax.experimental import pallas as pl
from jax.experimental.pallas import tpu as pltpu
from jax.sharding import Mesh
from jax.sharding import PartitionSpec as P

HEAD_DIM = 64
ROT = 16
EPS = 1e-05
MASKED = -1e30

AXES = ("e", "zh", "zl", "x", "y", "c")
HEAD_BITS = ("zh", "zl", "x", "y")
T1, T2, D1, D2 = "y", "zl", "zh", "x"
TP = (T1, T2, "c")
RANKS = 8
NEAR = (("c",), (T1,), (T2,), (T1, "c"), (T2, "c"), (T1, T2), (T1, T2, "c"))
FAR = ((D1,), (D2,))
SMALL_AXES = ("c", T1, T2, D1, D2)

F32, BF16 = jnp.float32, jnp.bfloat16
MESH = pl.DeviceIdType.MESH

PAIR = 2 * HEAD_DIM
QKV = 3 * PAIR
SLOTS = 12


def dot(a, b, contract):
    return lax.dot_general(a, b, (contract, ((), ())), preferred_element_type=F32)


class Links:
    def __init__(self, send_sem, recv_sem):
        self.place = {axis: lax.axis_index(axis) for axis in AXES}
        self.send_sem, self.recv_sem, self.used = send_sem, recv_sem, 0

    def reserve(self, count):
        self.used += count
        return self.used - count

    def peer(self, axes):
        return {axis: 1 - self.place[axis] for axis in axes}

    def chip(self, j):
        one, two = self.place[T1], self.place[T2]
        return {T1: one + (j // 2) * (1 - 2 * one), T2: two + (j % 2) * (1 - 2 * two)}

    def meet(self):
        barrier = pltpu.get_barrier_semaphore()
        for axes in NEAR + FAR:
            pl.semaphore_signal(barrier, inc=1, device_id=self.peer(axes), device_id_type=MESH)
        pl.semaphore_wait(barrier, len(NEAR) + len(FAR))

    def copy(self, source, target, device, slot=None):
        if slot is None:
            slot = self.reserve(1)
        if not isinstance(device, dict):
            device = self.peer(device)
        return pltpu.make_async_remote_copy(
            src_ref=source,
            dst_ref=target,
            send_sem=self.send_sem.at[slot],
            recv_sem=self.recv_sem.at[slot],
            device_id=device,
            device_id_type=MESH,
        )


def rank_of(place):
    return place[T1] * 4 + place[T2] * 2 + place["c"]


def block_of(place):
    index = place["zh"]
    for axis in AXES[2:]:
        index = index * 2 + place[axis]
    return index


def flipped(place, axes):
    return {a: (1 - i if a in axes else i) for a, i in place.items()}


class Rows:
    def __init__(self, links, buffer):
        self.links, self.buffer, self.base = links, buffer, links.reserve(8)

    def core(self, j):
        return self.links.copy(
            self.buffer.at[j, 0], self.buffer.at[j, 1], ("c",), self.base + j
        )

    def chip(self, j):
        return self.links.copy(
            self.buffer.at[0, 0], self.buffer.at[j, 0], self.links.chip(j), self.base + 4 + j
        )

    def start(self):
        self.core(0).start()
        for j in (3, 2, 1):
            self.chip(j).start()

    def arrive(self, j):
        @pl.when(j > 0)
        def _():
            self.chip(j).wait_recv()
            self.core(j).start()

        self.core(j).wait_recv()

    def finish(self):
        for j in range(4):
            self.core(j).wait_send()
        for j in range(1, 4):
            self.chip(j).wait_send()


class Sums:
    def __init__(self, links, core_in, chip_in, core_out, chip_out):
        self.links, self.base = links, links.reserve(8)
        self.core_in, self.chip_in, self.core_out, self.chip_out = core_in, chip_in, core_out, chip_out

    def core(self, j):
        return self.links.copy(
            self.core_out.at[j], self.core_in.at[j], ("c",), self.base + j
        )

    def chip(self, j):
        return self.links.copy(
            self.chip_out.at[j - 1], self.chip_in.at[j - 1], self.links.chip(j), self.base + 4 + j
        )

    def run(self, term, scratch, own):
        rows = own.shape[0]

        def pass_on(j, side):
            self.core(j).wait_recv()
            total = scratch[side, :rows] + self.core_in[j].astype(F32)

            @pl.when(j > 0)
            def _():
                self.chip_out[j - 1] = total.astype(BF16)
                self.chip(j).start()

            @pl.when(j == 0)
            def _():
                own[...] = total

        def step(i, carry):
            j = 3 - i
            side = i % 2

            scratch[side] = term(j)
            self.core_out[j] = scratch[side, rows:].astype(BF16)
            self.core(j).start()

            @pl.when(i > 0)
            def _():
                pass_on(j + 1, 1 - side)

            return carry

        lax.fori_loop(0, 4, step, 0)
        pass_on(0, 1)

    def total(self, own):
        for j in (1, 2, 3):
            self.chip(j).wait_recv()
        for j in range(4):
            self.core(j).wait_send()
        for j in (1, 2, 3):
            self.chip(j).wait_send()

        def at(rows):
            value = own[rows]
            for j in (1, 2, 3):
                value = value + self.chip_in[j - 1, rows].astype(F32)
            return value

        return at


def mean_of(value):
    return jnp.sum(value, axis=-1, keepdims=True) * (1.0 / value.shape[-1])


def normalise(stream):
    centred = stream - mean_of(stream)
    inverse = lax.rsqrt(mean_of(centred * centred) + EPS)
    return centred * inverse, inverse


def layers_kernel(
    parts,
    down,
    proj,
    inputs,
    cotangent,
    mask,
    small,
    tables,
    outputs,
    input_grad,
    cat_out,
    down_out,
    proj_out,
    small_out,
    cat_all,
    dp_all,
    hid,
    rnd,
    mask_all,
    qkv_kept,
    probs,
    ca,
    slope,
    mdud,
    scratch,
    core_in,
    chip_in,
    core_out,
    chip_out,
    own,
    stream_two,
    up_one,
    small_sum,
    small_in,
    sums,
    grad_sum,
    grad_in,
    cat_own,
    cat_s1,
    cat_r1,
    cat_s2,
    cat_r2,
    cat_a,
    dp_grad,
    down_s1,
    down_r1,
    down_s2,
    down_r2,
    proj_s1,
    proj_r1,
    proj_s2,
    proj_r2,
    proj_s3,
    proj_r3,
    send_sem,
    recv_sem,
    own_sem,
    free_sem,
):
    links = Links(send_sem, recv_sem)
    me = links.place
    rank, block, slot = rank_of(me), block_of(me), me[D2] * 2 + me[D1]
    mine = me["c"] == me[D2]
    others = jnp.logical_not(mine)
    layers, wide = parts.shape[0], parts.shape[3]
    micros, pack = mask.shape[0], mask.shape[1]
    rows, width = inputs.shape
    lift = wide - QKV
    scale = 1.0 / math.sqrt(HEAD_DIM)
    lane = lax.broadcasted_iota(jnp.int32, (pack, PAIR), 1)
    first_head = lane < HEAD_DIM

    def bias_row(layer, index, columns=None):
        value = small_sum[len(SMALL_AXES), pl.ds(layer * SLOTS + index, 1), :]
        return value

    class Weights:
        def __init__(self, layer):
            self.layer = layer
            self.keep = [
                pltpu.make_async_copy(
                    parts.at[layer, rank], cat_all.at[layer, block], own_sem.at[layer, 0]
                ),
                pltpu.make_async_copy(
                    down.at[layer], self.down_rows(slot), own_sem.at[layer, 1]
                ),
            ]
            self.trades = [
                links.copy(
                    parts.at[layer, rank_of(flipped(me, axes))], cat_all.at[layer, block], axes
                )
                for axes in NEAR
            ]
            self.cat_one = []
            for zl in range(2):
                part = self.cat_rows(me["zh"], zl)
                self.cat_one.append(links.copy(part, part, (D1,)))
            self.cat_two = []
            for zl in range(2):
                for zh in range(2):
                    part = self.cat_rows(zh, zl)
                    self.cat_two.append(links.copy(part, part, (D2,)))
            self.down_one = links.copy(down.at[layer], self.down_rows(slot), (D1,))
            both = self.down_rows(me[D2] * 2, 2)
            self.down_two = links.copy(both, both, (D2,))
            count = proj.shape[1]
            half = dp_all.at[layer, pl.ds(me["zh"] * HEAD_DIM + me["c"] * count, count)]
            self.to_core = links.copy(proj.at[layer], half, ("c",))
            self.stays = pltpu.make_async_copy(proj.at[layer], half, own_sem.at[layer, 2])
            head = dp_all.at[layer, pl.ds(me["zh"] * HEAD_DIM, HEAD_DIM)]
            self.proj_one = links.copy(head, head, (D1,))
            heads = dp_all.at[layer, pl.ds(0, PAIR)]
            self.proj_two = links.copy(heads, heads, (D2,))

        def cat_rows(self, zh, zl):
            return cat_all.at[self.layer, pl.ds(zh * 16 + zl * 8 + me["x"] * 4, 4)]

        def down_rows(self, place, count=1):
            size = down.shape[1]
            return dp_all.at[self.layer, pl.ds(PAIR + place * size, count * size)]

        def start_own(self):
            for copy in self.keep:
                copy.start()

        def start_trades(self):
            for copy in self.trades:
                copy.start()

        def start_rows(self):
            self.keep[1].wait()
            self.down_one.start()

            @pl.when(mine)
            def _():
                self.stays.start()
                self.stays.wait()

            @pl.when(others)
            def _():
                self.to_core.start()
                self.to_core.wait_send()

        def cat_first(self):
            self.keep[0].wait()
            for copy in self.trades:
                copy.wait()
            for copy in self.cat_one:
                copy.start()

        def cat_second(self):
            for zl in range(2):
                self.cat_one[zl].wait()
                for zh in range(2):
                    self.cat_two[2 * zl + zh].start()

        def cat_done(self):
            for copy in self.cat_two:
                copy.wait()

        def proj_first(self):
            @pl.when(mine)
            def _():
                self.to_core.wait_recv()
                self.proj_one.start()

        def rows_second(self):
            self.down_one.wait()
            self.down_two.start()

            @pl.when(mine)
            def _():
                self.proj_one.wait()
                self.proj_two.start()

        def rows_done(self):
            self.down_two.wait()

            @pl.when(mine)
            def _():
                self.proj_two.wait_send()

            @pl.when(others)
            def _():
                self.proj_two.wait_recv()

    def turn(value, sign):
        return (
            value * tables[0]
            + pltpu.roll(value, PAIR - ROT // 2, 1) * (tables[1] * sign)
            + pltpu.roll(value, ROT // 2, 1) * (tables[2] * sign)
        )

    def by_head(value):
        zero = jnp.zeros_like(value)
        return jnp.concatenate(
            [jnp.where(first_head, value, zero), jnp.where(first_head, zero, value)], axis=0
        )

    def of_heads(value):
        return jnp.where(first_head, value[:pack], value[pack:])

    def forward(layer, j):
        hidden = hid[layer, j].reshape(2 * rows, width)
        scratch[0, :, :wide] = dot(hidden, cat_all[layer].reshape(width, wide), ((1,), (0,)))
        bias = bias_row(layer, rank)

        def each(p, carry):
            at = pl.ds(pl.multiple_of(p * pack, pack), pack)
            turned = scratch[0, at, :QKV] + bias[:, :QKV]
            queries = turn(turned[:, :PAIR], 1.0).astype(BF16)
            keys = turn(turned[:, PAIR : 2 * PAIR], 1.0).astype(BF16)
            values = turned[:, 2 * PAIR :].astype(BF16)
            qkv_kept[layer, j, at, :PAIR] = queries
            qkv_kept[layer, j, at, PAIR : 2 * PAIR] = keys
            qkv_kept[layer, j, at, 2 * PAIR :] = values
            hide = mask_all[j, p // micros, p % micros][:, :pack].astype(F32)
            scores = dot(by_head(queries), keys, ((1,), (1,))) * scale
            scores = scores + jnp.concatenate([hide, hide], axis=0)
            shifted = jnp.exp(scores - jnp.max(scores, axis=-1, keepdims=True))
            soft = shifted / jnp.sum(shifted, axis=-1, keepdims=True)
            soft = soft.astype(BF16)
            probs[layer, j, p] = soft
            ca[layer, j, at, :PAIR] = of_heads(dot(soft, values, ((1,), (0,)))).astype(BF16)
            for start in range(QKV, wide, 2 * PAIR):
                cut = slice(start, start + 2 * PAIR)
                raised = scratch[0, at, cut] + bias[:, cut]
                cdf = 0.5 * (1.0 + lax.erf(raised * 0.7071067811865476))
                density = jnp.exp(-0.5 * raised * raised) * 0.3989422804014327
                to = start - QKV
                ca[layer, j, at, PAIR + to : PAIR + to + 2 * PAIR] = (raised * cdf).astype(BF16)
                slope[layer, j, at, to : to + 2 * PAIR] = (cdf + raised * density).astype(BF16)
            return carry

        lax.fori_loop(0, 2 * micros, each, 0)

    def backward(layer, j):
        rounded = rnd[j].reshape(2 * rows, width)
        scratch[0, :, : PAIR + lift] = dot(rounded, dp_all[layer], ((1,), (1,)))

        def each(p, carry):
            at = pl.ds(pl.multiple_of(p * pack, pack), pack)
            for start in range(0, lift, 2 * PAIR):
                cut = slice(start, start + 2 * PAIR)
                grown = scratch[0, at, PAIR + start : 3 * PAIR + start]
                grown = (grown * slope[layer, j, at, cut].astype(F32)).astype(BF16)
                mdud[j, at, QKV + start : QKV + start + 2 * PAIR] = grown
                sums[:, QKV + start : QKV + start + 2 * PAIR] += jnp.sum(
                    grown.astype(F32).reshape(pack // 8, 8, 2 * PAIR), axis=0
                )
            context = by_head(scratch[0, at, :PAIR].astype(BF16))
            queries = by_head(qkv_kept[layer, j, at, :PAIR])
            keys = qkv_kept[layer, j, at, PAIR : 2 * PAIR]
            values = qkv_kept[layer, j, at, 2 * PAIR :]
            kept = probs[layer, j, p]
            soft = kept.astype(F32)
            prob_delta = dot(context, values, ((1,), (1,)))
            row_delta = jnp.sum(soft * prob_delta, axis=-1, keepdims=True)
            score_delta = (soft * (prob_delta - row_delta)).astype(BF16)
            value_delta = dot(kept, context, ((0,), (0,)))
            query_delta = of_heads(dot(score_delta, keys, ((1,), (0,)))) * scale
            key_delta = dot(score_delta, queries, ((0,), (0,))) * scale
            three = (turn(query_delta, -1.0), turn(key_delta, -1.0), value_delta)
            for i, delta in enumerate(three):
                delta = delta.astype(BF16)
                cut = slice(i * PAIR, (i + 1) * PAIR)
                mdud[j, at, cut] = delta
                sums[:, cut] += jnp.sum(delta.astype(F32).reshape(pack // 8, 8, PAIR), axis=0)
            return carry

        lax.fori_loop(0, 2 * micros, each, 0)

    def out_term(layer):
        return lambda j: dot(ca[layer, j], dp_all[layer], ((1,), (0,)))

    def hidden_term(layer):
        return lambda j: dot(mdud[j], cat_all[layer].reshape(width, wide), ((1,), (1,)))

    class Grads:
        def __init__(self, layer):
            self.layer = layer
            self.down_one = links.copy(down_s1, down_r1.at[layer], (D2,))
            self.down_two = links.copy(down_s2, down_r2.at[layer], (D1,))
            self.proj_one = links.copy(proj_s1, proj_r1.at[layer], (D2,))
            self.proj_two = links.copy(proj_s2, proj_r2.at[layer], (D1,))
            self.proj_three = links.copy(proj_s3, proj_r3.at[layer], ("c",))
            self.cat_one = [
                links.copy(cat_s1.at[i], cat_r1.at[layer, i], (D2,)) for i in range(2)
            ]
            self.cat_two = links.copy(cat_s2, cat_r2.at[layer], (D1,))
            self.trades = []
            for axes in NEAR:
                there = flipped(me, axes)
                part = cat_a.at[there["zl"], there["y"] * 2 + there["c"]]
                self.trades.append(links.copy(part, cat_out.at[layer, rank], axes))
            self.keep = pltpu.make_async_copy(
                cat_a.at[me["zl"], me["y"] * 2 + me["c"]], cat_out.at[layer, rank], own_sem.at[layer, 3]
            )

        def rows_one(self):
            layer = self.layer
            kept = ca[layer].reshape(8 * rows, PAIR + lift)
            rounded = rnd[...].reshape(8 * rows, width)
            dp_grad[pl.ds(PAIR, lift)] = dot(kept[:, PAIR:], rounded, ((0,), (0,)))
            dp_grad[pl.ds(0, PAIR)] = dot(kept[:, :PAIR], rounded, ((0,), (0,)))
            half = lift // 2
            down_s1[...] = dp_grad[pl.ds(PAIR + (1 - me[D2]) * half, half)].astype(BF16)
            self.down_one.start()

            @pl.when(others)
            def _():
                proj_s1[...] = dp_grad[pl.ds(0, PAIR)].astype(BF16)
                self.proj_one.start()

        def rows_two(self):
            layer = self.layer
            half, quarter = lift // 2, lift // 4
            base = PAIR + me[D2] * half
            self.down_one.wait()
            at = (1 - me[D1]) * quarter
            down_s2[...] = (
                dp_grad[pl.ds(base + at, quarter)]
                + down_r1[layer, pl.ds(at, quarter)].astype(F32)
            ).astype(BF16)
            self.down_two.start()

            @pl.when(others)
            def _():
                self.proj_one.wait_send()

            @pl.when(mine)
            def _():
                self.proj_one.wait_recv()
                at = (1 - me[D1]) * HEAD_DIM
                proj_s2[...] = (
                    dp_grad[pl.ds(at, HEAD_DIM)]
                    + proj_r1[layer, pl.ds(at, HEAD_DIM)].astype(F32)
                ).astype(BF16)
                self.proj_two.start()

        def rows_three(self):
            layer = self.layer
            half, quarter = lift // 2, lift // 4
            base = PAIR + me[D2] * half
            self.down_two.wait()
            at = me[D1] * quarter
            down_out[layer] = (
                dp_grad[pl.ds(base + at, quarter)]
                + down_r1[layer, pl.ds(at, quarter)].astype(F32)
                + down_r2[layer].astype(F32)
            )
            count = proj.shape[1]

            @pl.when(mine)
            def _():
                self.proj_two.wait()
                at = me[D1] * HEAD_DIM

                def half_of(which):
                    return (
                        dp_grad[pl.ds(at + which * count, count)]
                        + proj_r1[layer, pl.ds(at + which * count, count)].astype(F32)
                        + proj_r2[layer, pl.ds(which * count, count)].astype(F32)
                    )

                proj_out[layer] = half_of(me["c"])
                proj_s3[...] = half_of(1 - me["c"]).astype(BF16)
                self.proj_three.start()
                self.proj_three.wait_send()

            @pl.when(others)
            def _():
                self.proj_three.wait_recv()
                proj_out[layer] = proj_r3[layer].astype(F32)

        def cat_terms(self, i):
            layer = self.layer
            zh = me["zh"] if i else 1 - me["zh"]
            half = width // 2
            columns = pl.ds(pl.multiple_of(zh * half, half), half)
            kept = hid[layer, :, :, :, columns].reshape(8 * rows, half)
            deltas = mdud[...].reshape(8 * rows, wide)
            scratch[:, : width // 8 * 2, :wide] = dot(kept, deltas, ((0,), (0,))).reshape(
                2, width // 4, wide
            )
            size = width // 8
            for zl in range(2):
                cat_s1[i, zl] = scratch[zl, pl.ds((1 - me["x"]) * size, size), :wide].astype(BF16)
                cat_own[i, zl] = scratch[zl, pl.ds(me["x"] * size, size), :wide]
            self.cat_one[i].start()

        def cat_step_two(self):
            layer = self.layer
            self.cat_one[0].wait()
            cat_s2[...] = (cat_own[0] + cat_r1[layer, 0].astype(F32)).astype(BF16)
            self.cat_two.start()

        def cat_step_three(self):
            layer = self.layer
            self.cat_one[1].wait()
            self.cat_two.wait()
            total = cat_own[1] + cat_r1[layer, 1].astype(F32) + cat_r2[layer].astype(F32)
            cat_a[...] = total.astype(BF16).reshape(cat_a.shape)
            for copy in self.trades:
                copy.start()
            self.keep.start()

        def cat_done(self):
            for copy in self.trades:
                copy.wait()
            self.keep.wait()

    def put_sums(layer, index, value):
        grad_sum[0, pl.ds(layer * SLOTS + index, 1), : value.shape[1]] = value

    def own_rows(layer, total, stream_at, up_at, put):
        gain = bias_row(layer, RANKS)
        gain_sum = jnp.zeros((1, width), F32)
        shift_sum = jnp.zeros((1, width), F32)
        for m in range(2 * micros):
            at = pl.ds(m * (rows // (2 * micros)), rows // (2 * micros))
            delta = total(at)
            normed, inverse = normalise(stream_at(at))
            gain_sum = gain_sum + jnp.sum(delta * normed, axis=0, keepdims=True)
            shift_sum = shift_sum + jnp.sum(delta, axis=0, keepdims=True)
            scaled = delta * gain
            put(
                at,
                up_at(at) + inverse * (scaled - mean_of(scaled) - normed * mean_of(scaled * normed)),
            )
        put_sums(layer, RANKS, gain_sum)
        put_sums(layer, RANKS + 1, shift_sum)

    def bias_sums(layer):
        put_sums(layer, rank, jnp.sum(sums[...], axis=0, keepdims=True))
        rounded = jnp.zeros((8, width), F32)
        for m in range(2 * micros):
            size = rows // (2 * micros)
            part = rnd[0, 0, pl.ds(m * size, size)].astype(F32)
            rounded = rounded + jnp.sum(part.reshape(size // 8, 8, width), axis=0)
        put_sums(layer, RANKS + 2, jnp.sum(rounded, axis=0, keepdims=True))

    def give_back(turn_index):
        for axes in (("c",), (T1,), (T2,), (T1, T2)):
            pl.semaphore_signal(
                free_sem.at[turn_index], inc=1, device_id=links.peer(axes), device_id_type=MESH
            )

    def await_places(turn_index):
        pl.semaphore_wait(free_sem.at[turn_index], 4)

    taken = [Weights(layer) for layer in range(layers)]
    grads = [Grads(layer) for layer in range(layers)]
    row_gathers = [Rows(links, hid.at[1]), Rows(links, mask_all), Rows(links, rnd)]
    hidden_two, rounded_one = Rows(links, hid.at[1]), Rows(links, rnd)
    sets = (core_in, chip_in, core_out, chip_out)
    out_one, delta_two, delta_one = Sums(links, *sets), Sums(links, *sets), Sums(links, *sets)
    out_two = Sums(links, *sets)
    small_copies = [
        links.copy(small_sum.at[i], small_in.at[i], (axis,)) for i, axis in enumerate(SMALL_AXES)
    ]
    grad_copies = [
        links.copy(grad_sum.at[i], grad_in.at[i], (axis,)) for i, axis in enumerate(SMALL_AXES)
    ]

    for one in taken:
        one.start_own()
    hid[1, 0, 0] = inputs[...]
    mask_all[0, 0] = mask[...]
    rnd[0, 0] = cotangent[...]
    small_sum[0] = small[...]
    grad_sum[...] = jnp.zeros_like(grad_sum)
    links.meet()

    small_copies[0].start()
    taken[0].start_trades()
    taken[0].start_rows()
    row_gathers[1].start()
    row_gathers[0].start()
    for i in range(len(SMALL_AXES)):
        small_copies[i].wait()
        small_sum[i + 1] = small_sum[i] + small_in[i]
        if i + 1 < len(SMALL_AXES):
            small_copies[i + 1].start()
        if i == 1:
            taken[0].cat_first()
        if i == 2:
            taken[0].proj_first()
    taken[1].start_trades()
    row_gathers[2].start()

    gain, shift = bias_row(0, RANKS), bias_row(0, RANKS + 1)

    def first_norm(j, carry):
        row_gathers[0].arrive(j)
        row_gathers[1].arrive(j)

        def each(p, carry):
            size = rows // 4
            at = pl.ds(pl.multiple_of((p % 4) * size, size), size)
            normed, _ = normalise(hid[1, j, p // 4, at].astype(F32))
            hid[0, j, p // 4, at] = (normed * gain + shift).astype(BF16)
            return carry

        return lax.fori_loop(0, 8, each, carry)

    lax.fori_loop(0, 4, first_norm, 0)
    taken[0].rows_second()
    taken[0].cat_second()
    row_gathers[0].finish()
    row_gathers[1].finish()
    taken[1].cat_first()
    taken[1].start_rows()
    taken[1].proj_first()
    taken[0].cat_done()
    lax.fori_loop(0, 4, lambda j, c: (forward(0, j), c)[1], 0)
    taken[0].rows_done()
    out_one.run(out_term(0), scratch, own)
    taken[1].cat_second()

    def rest_of_rounded(j, carry):
        row_gathers[2].arrive(j)
        return carry

    lax.fori_loop(0, 4, rest_of_rounded, 0)
    row_gathers[2].finish()
    total = out_one.total(own)
    out_bias = bias_row(0, RANKS + 2)
    gain, shift = bias_row(1, RANKS), bias_row(1, RANKS + 1)
    for m in range(4):
        at = pl.ds(m * (rows // 4), rows // 4)
        stream = inputs[at].astype(F32) + total(at) + out_bias
        stream_two[at] = stream
        normed, _ = normalise(stream)
        hid[1, 0, 0, at] = (normed * gain + shift).astype(BF16)
    hidden_two.start()
    taken[1].rows_second()
    taken[1].cat_done()

    def second(j, carry):
        hidden_two.arrive(j)
        forward(1, j)
        return carry

    lax.fori_loop(0, 4, second, 0)
    hidden_two.finish()
    taken[1].rows_done()

    sums[...] = jnp.zeros_like(sums)
    lax.fori_loop(0, 4, lambda j, c: (backward(1, j), c)[1], 0)
    grads[1].rows_one()
    bias_sums(1)
    delta_two.run(hidden_term(1), scratch, own)
    grads[1].cat_terms(0)
    grads[1].cat_terms(1)
    grads[1].rows_two()
    total = delta_two.total(own)

    def put_one(at, value):
        up_one[at] = value
        rnd[0, 0, at] = value.astype(BF16)

    own_rows(1, total, lambda at: stream_two[at], lambda at: cotangent[at].astype(F32), put_one)
    rounded_one.start()
    give_back(0)
    await_places(0)
    out_two.run(out_term(1), scratch, input_grad)
    grads[1].cat_step_two()
    grads[1].rows_three()

    sums[...] = jnp.zeros_like(sums)

    def third(j, carry):
        rounded_one.arrive(j)
        backward(0, j)
        return carry

    lax.fori_loop(0, 4, third, 0)
    rounded_one.finish()
    grads[1].cat_step_three()
    total = out_two.total(input_grad)
    out_bias = bias_row(1, RANKS + 2)
    for m in range(4):
        at = pl.ds(m * (rows // 4), rows // 4)
        outputs[at] = (stream_two[at] + total(at) + out_bias).astype(BF16)
    give_back(1)
    grads[1].cat_done()
    await_places(1)
    delta_one.run(hidden_term(0), scratch, own)
    grads[0].cat_terms(0)
    grads[0].cat_terms(1)
    grads[0].rows_one()
    bias_sums(0)
    grads[0].cat_step_two()
    total = delta_one.total(own)

    def put_last(at, value):
        input_grad[at] = value

    own_rows(0, total, lambda at: inputs[at].astype(F32), lambda at: up_one[at], put_last)
    grad_copies[0].start()
    grads[0].rows_two()
    for i in range(len(SMALL_AXES)):
        grad_copies[i].wait()
        grad_sum[i + 1] = grad_sum[i] + grad_in[i]
        if i + 1 < len(SMALL_AXES):
            grad_copies[i + 1].start()
        if i == 1:
            grads[0].cat_step_three()
        if i == 3:
            grads[0].rows_three()
    small_out[...] = grad_sum[len(SMALL_AXES)]
    grads[0].cat_done()


def run_layers(parts, down, proj, inputs, cotangent, mask, small, tables):
    layers, _, count, wide = parts.shape
    rows, width = inputs.shape
    micros, pack, lanes = mask.shape
    lift = wide - QKV
    vmem = pl.BlockSpec(memory_space=pltpu.VMEM)
    anywhere = pl.BlockSpec(memory_space=pltpu.HBM)
    shape = jax.ShapeDtypeStruct
    stages = len(SMALL_AXES)
    small_rows = small.shape[0]
    copies = 256
    cat_size = width // 8
    buffers = [
        ((layers, 32, count, wide), BF16),
        ((layers, PAIR + lift, width), BF16),
        ((layers, 4, 2, rows, width), BF16),
        ((4, 2, rows, width), BF16),
        ((4, 2, micros, pack, lanes), BF16),
        ((layers, 4, 2 * rows, QKV), BF16),
        ((layers, 4, 2 * micros, 2 * pack, pack), BF16),
        ((layers, 4, 2 * rows, PAIR + lift), BF16),
        ((layers, 4, 2 * rows, lift), BF16),
        ((4, 2 * rows, wide), BF16),
        ((2, 2 * rows, width), F32),
        ((4, rows, width), BF16),
        ((3, rows, width), BF16),
        ((4, rows, width), BF16),
        ((3, rows, width), BF16),
        ((rows, width), F32),
        ((rows, width), F32),
        ((rows, width), F32),
        ((stages + 1, small_rows, width), F32),
        ((stages, small_rows, width), F32),
        ((8, wide), F32),
        ((stages + 1, small_rows, width), F32),
        ((stages, small_rows, width), F32),
        ((2, 2, cat_size, wide), F32),
        ((2, 2, cat_size, wide), BF16),
        ((layers, 2, 2, cat_size, wide), BF16),
        ((2, cat_size, wide), BF16),
        ((layers, 2, cat_size, wide), BF16),
        ((2, 4, count, wide), BF16),
        ((PAIR + lift, width), F32),
        ((lift // 2, width), BF16),
        ((layers, lift // 2, width), BF16),
        ((lift // 4, width), BF16),
        ((layers, lift // 4, width), BF16),
        ((PAIR, width), BF16),
        ((layers, PAIR, width), BF16),
        ((HEAD_DIM, width), BF16),
        ((layers, HEAD_DIM, width), BF16),
        ((HEAD_DIM // 2, width), BF16),
        ((layers, HEAD_DIM // 2, width), BF16),
    ]
    return pl.pallas_call(
        layers_kernel,
        out_shape=(
            shape((rows, width), BF16),
            shape((rows, width), F32),
            shape((layers, RANKS, count, wide), BF16),
            shape((layers,) + down.shape[1:], F32),
            shape((layers,) + proj.shape[1:], F32),
            shape(small.shape, F32),
        ),
        in_specs=[anywhere] * 3 + [vmem] * 5,
        out_specs=(vmem, vmem, anywhere, vmem, vmem, vmem),
        scratch_shapes=[pltpu.VMEM(dims, kind) for dims, kind in buffers]
        + [
            pltpu.SemaphoreType.DMA((copies,)),
            pltpu.SemaphoreType.DMA((copies,)),
            pltpu.SemaphoreType.DMA((layers, 4)),
            pltpu.SemaphoreType.REGULAR((2,)),
        ],
        compiler_params=pltpu.CompilerParams(
            collective_id=0, has_side_effects=True, vmem_limit_bytes=63 << 20
        ),
    )(parts, down, proj, inputs, cotangent, mask, small, tables)


def split_heads(value, parts):
    lead = value.ndim - 1
    value = value.reshape(value.shape[:-1] + (parts, 2, 2, 2, 2, HEAD_DIM))
    place = {axis: lead + 1 + i for i, axis in enumerate(HEAD_BITS)}
    order = [place[T1], place[T2], place[D2]] + list(range(lead + 1)) + [place[D1], lead + 5]
    return value.transpose(order)


def join_heads(value):
    lead = value.ndim - 6
    names = {T1: 0, T2: 1, D2: 2, D1: lead + 4}
    order = [3 + i for i in range(lead)] + [3 + lead] + [names[a] for a in HEAD_BITS] + [lead + 5]
    value = value.transpose(order)
    return value.reshape(value.shape[:lead] + (-1,))


def split_columns(value):
    lead = value.ndim - 1
    value = value.reshape(value.shape[:-1] + (2, 2, 2, 2, 2, -1))
    place = {axis: lead + i for i, axis in enumerate(AXES[1:])}
    order = [place[a] for a in TP] + list(range(lead)) + [place[D2], place[D1], lead + 5]
    return value.transpose(order)


def join_columns(value):
    lead = value.ndim - 6
    names = {a: i for i, a in enumerate(TP)} | {D2: 3 + lead, D1: 4 + lead}
    order = [3 + i for i in range(lead)] + [names[a] for a in AXES[1:]] + [lead + 5]
    value = value.transpose(order)
    return value.reshape(value.shape[:lead] + (-1,))


def refold(block, extra):
    if extra == 1:
        return block
    whole = lax.all_gather(block, AXES, axis=1, tiled=True)
    rows = whole.shape[1] // 32
    return lax.dynamic_slice_in_dim(whole, lax.axis_index(AXES[1:]) * rows, rows, 1)


def unfold(block, extra):
    if extra == 1:
        return block
    rows = block.shape[1]
    whole = jnp.zeros((block.shape[0], 32 * rows) + block.shape[2:], F32)
    whole = lax.dynamic_update_slice_in_dim(whole, block, lax.axis_index(AXES[1:]) * rows, 1)
    return lax.psum_scatter(whole, AXES, scatter_dimension=1, tiled=True)


def at_place(block):
    size = block.shape[1]
    whole = jnp.zeros((block.shape[0], 32 * size), F32)
    return lax.dynamic_update_slice_in_dim(
        whole, block.astype(F32), lax.axis_index(AXES[1:]) * size, 1
    )


def rope_tables(pack):
    half = ROT // 2
    angle = np.arange(pack, dtype=np.float32)[:, None] * (
        np.float32(10000.0) ** (-np.arange(0, ROT, 2, dtype=np.float32) / np.float32(ROT))
    )
    angle = angle.astype(np.float32)
    tables = np.zeros((3, pack, 2, HEAD_DIM), np.float32)
    tables[0] = 1.0
    tables[0, :, :, :half] = tables[0, :, :, half:ROT] = np.cos(angle)[:, None]
    tables[1, :, :, :half] = -np.sin(angle)[:, None]
    tables[2, :, :, half:ROT] = np.sin(angle)[:, None]
    return tables.reshape(3, pack, PAIR)


def shards(
    inputs,
    cotangent,
    segments,
    pack_length,
    norm_gain,
    norm_shift,
    qkv_weight,
    qv_bias,
    proj_weight,
    proj_bias,
    up_weight,
    up_bias,
    down_weight,
    down_bias,
):
    micros, pack, width = inputs.shape
    layers = qkv_weight.shape[0]
    extra = lax.axis_size("e")
    position = jnp.arange(pack)
    is_live = position[None, :] < pack_length
    causal = position[:, None] >= position[None, :]
    diagonal = position[:, None] == position[None, :]
    allowed = (
        (segments[:, :, None] == segments[:, None, :])
        & causal
        & (is_live[:, None, :] | diagonal)
    )
    mask = jnp.where(allowed, 0.0, MASKED).astype(BF16)
    mask = jnp.pad(mask, ((0, 0), (0, 0), (0, -pack % 128)))

    qkv_mine, up_mine = refold(qkv_weight, extra), refold(up_weight, extra)
    proj_mine, down_mine = refold(proj_weight, extra), refold(down_weight, extra)
    count = qkv_mine.shape[1]
    qkv_parts = jnp.moveaxis(split_heads(qkv_mine, 3), 3, 0).reshape(layers, RANKS, count, -1)
    up_parts = jnp.moveaxis(split_columns(up_mine), 3, 0).reshape(layers, RANKS, count, -1)
    parts = jnp.concatenate([qkv_parts, up_parts], axis=-1)

    def ranks(value):
        return jnp.moveaxis(value, 3, 0).reshape(layers, RANKS, -1)

    qv = at_place(refold(qv_bias, extra))
    upb = at_place(refold(up_bias, extra))
    q_rows, v_rows = ranks(split_heads(qv[:, :width], 1)), ranks(split_heads(qv[:, width:], 1))
    by_rank = [q_rows, jnp.zeros_like(q_rows), v_rows, ranks(split_columns(upb))]
    by_rank = jnp.concatenate(by_rank, axis=-1)
    by_rank = jnp.pad(by_rank, ((0, 0), (0, 0), (0, width - by_rank.shape[-1])))
    whole = [
        at_place(refold(norm_gain, extra)),
        at_place(refold(norm_shift, extra)),
        at_place(refold(proj_bias, extra).astype(F32) + refold(down_bias, extra).astype(F32)),
        jnp.zeros((layers, width), F32),
    ]
    small = jnp.concatenate([by_rank, jnp.stack(whole, axis=1)], axis=1)
    small = small.reshape(layers * SLOTS, width)

    live = is_live[:, :, None].astype(BF16)
    out, input_grad, cat_grad, down_grad, proj_grad, small_grad = run_layers(
        parts,
        down_mine,
        proj_mine,
        inputs.reshape(micros * pack, width),
        (cotangent * live).reshape(micros * pack, width),
        mask,
        small,
        jnp.asarray(rope_tables(pack)),
    )
    cat_grad = cat_grad.reshape(layers, 2, 2, 2, count, -1)
    qkv_grad = jnp.moveaxis(cat_grad[..., :QKV], 0, 3).reshape(
        2, 2, 2, layers, count, 3, 2, HEAD_DIM
    )
    up_grad = jnp.moveaxis(cat_grad[..., QKV:], 0, 3).reshape(2, 2, 2, layers, count, 2, 2, -1)
    small_grad = small_grad.reshape(layers, SLOTS, width)
    if extra > 1:
        small_grad = lax.psum(small_grad, "e")
    by_rank = jnp.moveaxis(small_grad[:, :RANKS].reshape(layers, 2, 2, 2, width), 0, 3)

    def heads_of(start):
        part = by_rank[..., start : start + PAIR]
        return join_heads(part.reshape(2, 2, 2, layers, 1, 2, HEAD_DIM))

    upb_grad = by_rank[..., QKV : QKV + up_parts.shape[-1]]
    upb_grad = join_columns(upb_grad.reshape(2, 2, 2, layers, 2, 2, -1))
    qvb_grad = jnp.concatenate([heads_of(0), heads_of(2 * PAIR)], axis=1)

    def own_share(value):
        size = value.shape[1] // (32 * extra)
        return lax.dynamic_slice_in_dim(value, lax.axis_index(AXES) * size, size, 1)

    bias_grad = own_share(small_grad[:, RANKS + 2])
    return (
        out.reshape(micros, pack, width),
        input_grad.reshape(micros, pack, width),
        own_share(small_grad[:, RANKS]),
        own_share(small_grad[:, RANKS + 1]),
        unfold(join_heads(qkv_grad).astype(F32), extra),
        own_share(qvb_grad),
        unfold(proj_grad, extra),
        bias_grad,
        unfold(join_columns(up_grad).astype(F32), extra),
        own_share(upb_grad),
        unfold(down_grad, extra),
        bias_grad,
    )


def solution(mesh):
    devices = mesh.devices.size
    fine = Mesh(mesh.devices.reshape(devices // 32, 2, 2, 2, 2, 2), AXES)
    cube, flat = P(None, AXES, None), P(None, AXES)
    placed = (cube, cube, flat, flat, flat, flat, cube, flat, cube, flat, cube, flat, cube, flat)
    given = (cube, cube, flat, flat, cube, flat, cube, flat, cube, flat, cube, flat)
    return jax.shard_map(shards, mesh=fine, in_specs=placed, out_specs=given, check_vma=False)
```

```python
import math

import jax
import jax.numpy as jnp
import numpy as np
from jax import lax
from jax.experimental import pallas as pl
from jax.experimental.pallas import tpu as pltpu
from jax.sharding import Mesh
from jax.sharding import PartitionSpec as P

HEAD_DIM = 64
ROT = 16
EPS = 1e-05
MASKED = -1e30

AXES = ("e", "zh", "zl", "x", "y", "c")
T1, T2, D1, D2 = "y", "zl", "zh", "x"
TP = (T1, T2, "c")
RANKS = 8
NEAR = (("c",), (T1,), (T2,), (T1, "c"), (T2, "c"), (T1, T2), (T1, T2, "c"))
FAR = ((D1,), (D2,))
SMALL_AXES = ("c", T1, T2, D1, D2)

F32, BF16 = jnp.float32, jnp.bfloat16
MESH = pl.DeviceIdType.MESH

PAIR = 2 * HEAD_DIM
QKV = 3 * PAIR


def dot(a, b, contract):
    return lax.dot_general(a, b, (contract, ((), ())), preferred_element_type=F32)


class Links:
    def __init__(self, send_sem, recv_sem):
        self.place = {axis: lax.axis_index(axis) for axis in AXES}
        self.send_sem, self.recv_sem, self.used = send_sem, recv_sem, 0

    def reserve(self, count):
        self.used += count
        return self.used - count

    def peer(self, axes):
        return {axis: 1 - self.place[axis] for axis in axes}

    def meet(self):
        barrier = pltpu.get_barrier_semaphore()
        for axes in NEAR + FAR:
            pl.semaphore_signal(barrier, inc=1, device_id=self.peer(axes), device_id_type=MESH)
        pl.semaphore_wait(barrier, len(NEAR) + len(FAR))

    def copy(self, source, target, device, slot=None):
        if slot is None:
            slot = self.reserve(1)
        if not isinstance(device, dict):
            device = self.peer(device)
        return pltpu.make_async_remote_copy(
            src_ref=source,
            dst_ref=target,
            send_sem=self.send_sem.at[slot],
            recv_sem=self.recv_sem.at[slot],
            device_id=device,
            device_id_type=MESH,
        )


def rank_of(place):
    return place[T1] * 4 + place[T2] * 2 + place["c"]


def block_of(place):
    index = place["zh"]
    for axis in AXES[2:]:
        index = index * 2 + place[axis]
    return index


def flipped(place, axes):
    return {a: (1 - i if a in axes else i) for a, i in place.items()}


class Rows:
    def __init__(self, links, buffer):
        self.links, self.buffer, self.base = links, buffer, links.reserve(8)

    def core(self, j):
        return self.links.copy(
            self.buffer.at[j, 0], self.buffer.at[j, 1], ("c",), self.base + j
        )

    def chip(self, j):
        source, axes = (0, (T1,)) if isinstance(j, jax.Array) else ((0, 0, 0, 1)[j], (T2,) if j == 1 else (T1,))
        return self.links.copy(
            self.buffer.at[source, 0], self.buffer.at[j, 0], axes, self.base + 4 + j
        )

    def start(self):
        self.core(0).start()
        self.chip(1).start()
        self.chip(2).start()

    def forward(self):
        self.chip(1).wait_recv()
        self.chip(3).start()
        self.core(1).start()

    def arrive(self, j):
        @pl.when(j > 1)
        def _():
            self.chip(j).wait_recv()
            self.core(j).start()

        self.core(j).wait_recv()

    def finish(self):
        for j in range(4):
            self.core(j).wait_send()
        for j in range(1, 4):
            self.chip(j).wait_send()


def far_first(i):
    return 3 - i


def near_first(i):
    return i + 1 - 3 * (i // 3) - (3 - i) // 3


class Sums:
    def __init__(self, links, core_in, chip_in, core_out, chip_out):
        self.links, self.base = links, links.reserve(8)
        self.core_in, self.chip_in, self.core_out, self.chip_out = core_in, chip_in, core_out, chip_out

    def core(self, j):
        return self.links.copy(
            self.core_out.at[j], self.core_in.at[j], ("c",), self.base + j
        )

    def chip(self, j):
        return self.links.copy(
            self.chip_out.at[j - 1],
            self.chip_in.at[j - 1],
            (T2,) if j == 1 else (T1,),
            self.base + 4 + j,
        )

    def run(self, before, term, scratch, own, order):
        rows = own.shape[0]

        def pass_on(j):
            self.core(j).wait_recv()
            for m in range(2):
                at = pl.ds(m * (rows // 2), rows // 2)
                total = scratch[1, at] + self.core_in[j, at].astype(F32)
                for k in (1, 2, 3):

                    @pl.when(j == k)
                    def _():
                        value = total
                        if k == 1:
                            if m == 0:
                                self.chip(3).wait_recv()
                            value = value + self.chip_in[2, at].astype(F32)
                        self.chip_out[k - 1, at] = value.astype(BF16)
                        if m == 1:
                            self.chip(k).start()

                @pl.when(j == 0)
                def _():
                    own[at] = total

        def step(i, carry):
            j = order(i)
            before(i, j)

            @pl.when(i > 0)
            def _():
                pass_on(order(i - 1))

            term(j, scratch.at[1])
            self.core_out[j] = scratch[1, rows:].astype(BF16)
            self.core(j).start()
            return carry

        lax.fori_loop(0, 4, step, 0)
        pass_on(order(3))

    def total(self, own):
        for j in (1, 2):
            self.chip(j).wait_recv()
        for j in range(4):
            self.core(j).wait_send()
        for j in (1, 2, 3):
            self.chip(j).wait_send()

        def at(rows):
            value = own[rows]
            for j in (1, 2):
                value = value + self.chip_in[j - 1, rows].astype(F32)
            return value

        return at


def mean_of(value):
    return jnp.sum(value, axis=-1, keepdims=True) * (1.0 / value.shape[-1])


def normalise(stream):
    centred = stream - mean_of(stream)
    inverse = lax.rsqrt(mean_of(centred * centred) + EPS)
    return centred * inverse, inverse


def layers_kernel(
    qkv,
    up,
    down,
    proj,
    inputs,
    cotangent,
    marks,
    small,
    tables,
    outputs,
    input_grad,
    gain_out,
    shift_out,
    qkv_out,
    qvb_out,
    proj_out,
    bias_out,
    up_out,
    upb_out,
    down_out,
    parts,
    cat_all,
    dp_all,
    hid,
    rnd,
    mask_all,
    qkv_kept,
    probs,
    ca,
    slope,
    mdud,
    scratch,
    core_in,
    chip_in,
    core_out,
    chip_out,
    own,
    stream_two,
    up_one,
    small_sum,
    small_in,
    sums,
    grad_sum,
    cat_own,
    cat_s1,
    cat_r1,
    cat_s2,
    cat_r2,
    cat_a,
    dp_grad,
    down_s1,
    down_r1,
    down_s2,
    down_r2,
    proj_s1,
    proj_r1,
    proj_s2,
    proj_r2,
    proj_s3,
    proj_r3,
    send_sem,
    recv_sem,
    own_sem,
    free_sem,
    fetch_sem,
):
    links = Links(send_sem, recv_sem)
    me = links.place
    rank, block, slot = rank_of(me), block_of(me), me[D2] * 2 + me[D1]
    mine = me["c"] == me[D2]
    others = jnp.logical_not(mine)
    layers, wide = parts.shape[0], parts.shape[3]
    micros, lanes = marks.shape
    rows, width = inputs.shape
    pack = rows // micros
    count = qkv.shape[1]
    lift = wide - QKV
    scale = 1.0 / math.sqrt(HEAD_DIM)
    lane = lax.broadcasted_iota(jnp.int32, (pack, PAIR), 1)
    first_head = lane < HEAD_DIM

    def ranks_row(layer):
        return layer * RANKS + rank

    def named_row(layer, index):
        return layers * RANKS + 3 * layer + index

    def bias_row(index):
        return small_sum[len(SMALL_AXES), pl.ds(index, 1), :]

    pieces = 3 + up.shape[2] // width
    raw = [core_out.at[i // 6, pl.ds(i % 6 * count, count)] for i in range(layers * pieces)]
    final = [scratch.at[i // 8, pl.ds(i % 8 * count, count)] for i in range(layers * pieces)]

    def fetch_columns():
        copies = []
        for i in range(layers * pieces):
            layer, k = i // pieces, i % pieces
            source = qkv.at[layer, :, pl.ds(k * width, width)] if k < 3 else up.at[
                layer, :, pl.ds((k - 3) * width, width)
            ]
            copies.append(pltpu.make_async_copy(source, raw[i], fetch_sem.at[i]))
        return copies

    def return_columns(layer):
        copies = []
        for k in range(pieces):
            i = layer * pieces + k
            target = qkv_out.at[layer, :, pl.ds(k * width, width)] if k < 3 else up_out.at[
                layer, :, pl.ds((k - 3) * width, width)
            ]
            copies.append(pltpu.make_async_copy(final[i], target, fetch_sem.at[i]))
        return copies

    lane_row = lax.broadcasted_iota(jnp.int32, (count, PAIR), 1) < HEAD_DIM

    def shared(one, other):
        one, other = one.astype(F32), other.astype(F32)
        return (
            jnp.where(lane_row, one, pltpu.roll(other, HEAD_DIM, 1)),
            jnp.where(lane_row, pltpu.roll(one, HEAD_DIM, 1), other),
        )

    def columns_by_rank(layer):
        base = layer * pieces
        for p in range(3):
            for zl in range(2):
                for x in range(2):
                    tiles = [
                        raw[base + p][:, (zh * 4 + zl * 2 + x) * PAIR : (zh * 4 + zl * 2 + x + 1) * PAIR]
                        for zh in range(2)
                    ]
                    for y, tile in enumerate(shared(*tiles)):
                        parts[layer, y * 4 + zl * 2 + x, :, p * PAIR : (p + 1) * PAIR] = tile.astype(BF16)
        size = up.shape[2] // 32
        for b in range(32):
            zh, zl, x, y, c = b // 16, b // 8 % 2, b // 4 % 2, b // 2 % 2, b % 2
            k, at = b * size // width, b * size % width
            to = QKV + (x * 2 + zh) * size
            parts[layer, y * 4 + zl * 2 + c, :, to : to + size] = raw[base + 3 + k][:, at : at + size]

    def columns_by_name(layer):
        base = layer * pieces
        for p in range(3):
            for zl in range(2):
                for x in range(2):
                    tiles = [
                        parts[layer, y * 4 + zl * 2 + x, :, p * PAIR : (p + 1) * PAIR] for y in range(2)
                    ]
                    for zh, tile in enumerate(shared(*tiles)):
                        at = (zh * 4 + zl * 2 + x) * PAIR
                        final[base + p][:, at : at + PAIR] = tile
        size = up.shape[2] // 32
        for b in range(32):
            zh, zl, x, y, c = b // 16, b // 8 % 2, b // 4 % 2, b // 2 % 2, b % 2
            k, at = b * size // width, b * size % width
            to = QKV + (x * 2 + zh) * size
            tile = parts[layer, y * 4 + zl * 2 + c, :, to : to + size]
            final[base + 3 + k][:, at : at + size] = tile.astype(F32)

    head_rank = me["c"] * 4 + me["x"] * 2 + me["y"]
    head_cut = pl.ds(pl.multiple_of(me["zh"] * 2 * PAIR, PAIR), PAIR)
    up_size = up.shape[2] // 32
    up_cut = pl.ds(pl.multiple_of(QKV + slot * up_size, PAIR), up_size)

    ranked = layers * RANKS
    named = small_sum.shape[1] - ranked
    rank_row = lax.broadcasted_iota(jnp.int32, (RANKS, PAIR), 0)

    def spread_small():
        small_sum[0, :ranked] = jnp.zeros((ranked, width), F32)
        small_sum[0, ranked:] = pltpu.roll(small[:named], block * (width // 32), 1)
        for layer in range(layers):
            at = slice(layer * RANKS, (layer + 1) * RANKS)
            pair = jnp.broadcast_to(small[named + layer : named + layer + 1, :PAIR], (RANKS, PAIR))
            pair = pltpu.roll(pair, me["zl"] * HEAD_DIM, 1)
            small_sum[0, at, head_cut] = jnp.where(rank_row == head_rank, pair, 0.0)
            more = named + layers + layer
            more = jnp.broadcast_to(small[more : more + 1, :up_size], (RANKS, up_size))
            small_sum[0, at, up_cut] = jnp.where(rank_row == rank, more, 0.0)

    def own_small(total):
        share = width // 32
        moved = pltpu.roll(total[ranked:], (32 - block) % 32 * share, 1)
        for layer in range(layers):
            start = layer * 3
            gain_out[layer : layer + 1] = moved[start : start + 1, :share]
            shift_out[layer : layer + 1] = moved[start + 1 : start + 2, :share]
            bias_out[layer : layer + 1] = moved[start + 2 : start + 3, :share]
            at = slice(layer * RANKS, (layer + 1) * RANKS)
            pair = pltpu.roll(total[at, head_cut], me["zl"] * HEAD_DIM, 1)
            pair = jnp.where(rank_row == head_rank, pair, 0.0)
            qvb_out[layer : layer + 1] = jnp.sum(pair, axis=0, keepdims=True)[:, :HEAD_DIM]
            more = jnp.where(rank_row == rank, total[at, up_cut], 0.0)
            upb_out[layer : layer + 1] = jnp.sum(more, axis=0, keepdims=True)

    def build_mask(m):
        row = lax.broadcasted_iota(jnp.int32, (lanes, lanes), 0)
        column = lax.broadcasted_iota(jnp.int32, (lanes, lanes), 1)
        across = jnp.broadcast_to(marks[pl.ds(m, 1), :], (lanes, lanes))
        length = marks[pl.ds(m, 1), pack : pack + 1]
        live = column.astype(F32) < length
        allowed = (across.T == across) & (column <= row) & (live | (column == row))
        hidden = jnp.where(allowed, 0.0, MASKED).astype(BF16)
        mask_all[0, 0, m] = hidden[:pack]
        live = lax.broadcasted_iota(jnp.int32, (pack, 1), 0).astype(F32) < length
        at = pl.ds(m * pack, pack)
        rnd[0, 0, at] = jnp.where(live, cotangent[at].astype(F32), 0.0).astype(BF16)

    class Piece:
        def __init__(self, own, at):
            here, there = at(me["zh"]), at(1 - me["zh"])
            self.one = links.copy(here if own is None else own, here, (D1,))
            self.near = links.copy(here if own is None else own, here, (D2,))
            self.far = links.copy(there, there, (D2,))

        def start(self):
            self.one.start()

        def start_near(self):
            self.near.start()

        def step(self):
            self.one.wait()

        def start_far(self):
            self.far.start()

        def done(self):
            self.near.wait()
            self.far.wait()

    class Heads:
        def __init__(self, layer):
            self.layer = layer
            count = proj.shape[1]
            half = dp_all.at[layer, pl.ds(me["zh"] * HEAD_DIM + me["c"] * count, count)]
            self.to_core = links.copy(proj.at[layer], half, ("c",))
            self.stays = pltpu.make_async_copy(proj.at[layer], half, own_sem.at[layer, 2])
            head = dp_all.at[layer, pl.ds(me["zh"] * HEAD_DIM, HEAD_DIM)]
            self.one = links.copy(head, head, (D1,))
            heads = dp_all.at[layer, pl.ds(0, PAIR)]
            self.two = links.copy(heads, heads, (D2,))

        def prepare(self):
            @pl.when(mine)
            def _():
                self.stays.start()
                self.stays.wait()

            @pl.when(others)
            def _():
                self.to_core.start()
                self.to_core.wait_send()

        def start(self):
            @pl.when(mine)
            def _():
                self.to_core.wait_recv()
                self.one.start()

        def step(self):
            @pl.when(mine)
            def _():
                self.one.wait()

        def start_far(self):
            @pl.when(mine)
            def _():
                self.two.start()

        def done(self):
            @pl.when(mine)
            def _():
                self.two.wait_send()

            @pl.when(others)
            def _():
                self.two.wait_recv()

    class Weights:
        def __init__(self, layer):
            self.layer = layer
            size = down.shape[1]
            self.keep = [
                pltpu.make_async_copy(
                    parts.at[layer, rank], cat_all.at[layer, block], own_sem.at[layer, 0]
                ),
                pltpu.make_async_copy(
                    down.at[layer], self.down_rows(me["zh"], 0, size), own_sem.at[layer, 1]
                ),
            ]
            self.trades = [
                links.copy(
                    parts.at[layer, rank_of(flipped(me, axes))], cat_all.at[layer, block], axes
                )
                for axes in NEAR
            ]
            self.cat = [
                Piece(None, lambda zh, zl=zl, h=h: self.cat_rows(zh, zl, h))
                for zl in range(2)
                for h in range(2)
            ]
            half = size // 2
            self.down = [
                Piece(
                    down.at[layer, pl.ds(h * half, half)],
                    lambda zh, h=h: self.down_rows(zh, h * half, half),
                )
                for h in range(2)
            ]
            self.heads = Heads(layer)

        def cat_rows(self, zh, zl, h):
            return cat_all.at[self.layer, pl.ds(zh * 16 + zl * 8 + me["x"] * 4 + 2 * h, 2)]

        def down_rows(self, zh, start, count):
            size = down.shape[1]
            return dp_all.at[
                self.layer, pl.ds(PAIR + (me[D2] * 2 + zh) * size + start, count)
            ]

        def start_trades(self):
            self.keep[0].start()
            for copy in self.trades:
                copy.start()

        def traded(self):
            self.keep[0].wait()
            for copy in self.trades:
                copy.wait()

        def cat_done(self):
            for piece in self.cat:
                piece.done()

        def rows_done(self):
            self.keep[1].wait()
            for piece in self.down:
                piece.done()
            self.heads.done()

    def turn(value, sign):
        return (
            value * tables[0]
            + pltpu.roll(value, PAIR - ROT // 2, 1) * (tables[1] * sign)
            + pltpu.roll(value, ROT // 2, 1) * (tables[2] * sign)
        )

    def by_head(value):
        zero = jnp.zeros_like(value)
        return jnp.concatenate(
            [jnp.where(first_head, value, zero), jnp.where(first_head, zero, value)], axis=0
        )

    def of_heads(value):
        return jnp.where(first_head, value[:pack], value[pack:])

    def forward(layer, j):
        hidden = hid[layer, j].reshape(2 * rows, width)
        for cut in (slice(0, QKV), slice(QKV, wide)):
            columns = cat_all[layer, :, :, cut].reshape(width, -1)
            scratch[0, :, cut] = dot(hidden, columns, ((1,), (0,)))
        bias = bias_row(ranks_row(layer))

        def each(p, carry):
            at = pl.ds(pl.multiple_of(p * pack, pack), pack)
            turned = scratch[0, at, :QKV] + bias[:, :QKV]
            queries = turn(turned[:, :PAIR], 1.0).astype(BF16)
            keys = turn(turned[:, PAIR : 2 * PAIR], 1.0).astype(BF16)
            values = turned[:, 2 * PAIR :].astype(BF16)
            qkv_kept[layer, j, at, :PAIR] = queries
            qkv_kept[layer, j, at, PAIR : 2 * PAIR] = keys
            qkv_kept[layer, j, at, 2 * PAIR :] = values
            hide = mask_all[j, p // micros, p % micros][:, :pack].astype(F32)
            scores = dot(by_head(queries), keys, ((1,), (1,))) * scale
            scores = scores + jnp.concatenate([hide, hide], axis=0)
            shifted = jnp.exp(scores - jnp.max(scores, axis=-1, keepdims=True))
            soft = shifted / jnp.sum(shifted, axis=-1, keepdims=True)
            soft = soft.astype(BF16)
            probs[layer, j, p] = soft
            ca[layer, j, at, :PAIR] = of_heads(dot(soft, values, ((1,), (0,)))).astype(BF16)
            for start in range(QKV, wide, 2 * PAIR):
                cut = slice(start, start + 2 * PAIR)
                raised = scratch[0, at, cut] + bias[:, cut]
                cdf = 0.5 * (1.0 + lax.erf(raised * 0.7071067811865476))
                density = jnp.exp(-0.5 * raised * raised) * 0.3989422804014327
                to = start - QKV
                ca[layer, j, at, PAIR + to : PAIR + to + 2 * PAIR] = (raised * cdf).astype(BF16)
                slope[layer, j, at, to : to + 2 * PAIR] = (cdf + raised * density).astype(BF16)
            return carry

        lax.fori_loop(0, 2 * micros, each, 0)

    def backward(layer, j):
        rounded = rnd[j].reshape(2 * rows, width)
        for cut in (slice(0, PAIR), slice(PAIR, PAIR + lift)):
            scratch[0, :, cut] = dot(rounded, dp_all[layer, cut], ((1,), (1,)))

        def each(p, carry):
            at = pl.ds(pl.multiple_of(p * pack, pack), pack)
            for start in range(0, lift, 2 * PAIR):
                cut = slice(start, start + 2 * PAIR)
                grown = scratch[0, at, PAIR + start : 3 * PAIR + start]
                grown = (grown * slope[layer, j, at, cut].astype(F32)).astype(BF16)
                mdud[j, at, QKV + start : QKV + start + 2 * PAIR] = grown
                sums[:, QKV + start : QKV + start + 2 * PAIR] += jnp.sum(
                    grown.astype(F32).reshape(pack // 8, 8, 2 * PAIR), axis=0
                )
            context = by_head(scratch[0, at, :PAIR].astype(BF16))
            queries = by_head(qkv_kept[layer, j, at, :PAIR])
            keys = qkv_kept[layer, j, at, PAIR : 2 * PAIR]
            values = qkv_kept[layer, j, at, 2 * PAIR :]
            kept = probs[layer, j, p]
            soft = kept.astype(F32)
            prob_delta = dot(context, values, ((1,), (1,)))
            row_delta = jnp.sum(soft * prob_delta, axis=-1, keepdims=True)
            score_delta = (soft * (prob_delta - row_delta)).astype(BF16)
            value_delta = dot(kept, context, ((0,), (0,)))
            query_delta = of_heads(dot(score_delta, keys, ((1,), (0,)))) * scale
            key_delta = dot(score_delta, queries, ((0,), (0,))) * scale
            three = (turn(query_delta, -1.0), turn(key_delta, -1.0), value_delta)
            for i, delta in enumerate(three):
                delta = delta.astype(BF16)
                cut = slice(i * PAIR, (i + 1) * PAIR)
                mdud[j, at, cut] = delta
                sums[:, cut] += jnp.sum(delta.astype(F32).reshape(pack // 8, 8, PAIR), axis=0)
            return carry

        lax.fori_loop(0, 2 * micros, each, 0)

    halves = (slice(0, width // 2), slice(width // 2, width))

    def out_term(layer):
        def put(j, target):
            for cut in halves:
                target[:, cut] = dot(ca[layer, j], dp_all[layer, :, cut], ((1,), (0,)))

        return put

    def hidden_term(layer):
        def put(j, target):
            for half, cut in enumerate(halves):
                columns = cat_all[layer, pl.ds(16 * half, 16)].reshape(width // 2, wide)
                target[:, cut] = dot(mdud[j], columns, ((1,), (1,)))

        return put

    class Grads:
        def __init__(self, layer):
            self.layer = layer
            self.down_one = links.copy(down_s1, down_r1.at[layer], (D2,))
            self.down_two = links.copy(down_s2, down_r2.at[layer], (D1,))
            self.proj_one = links.copy(proj_s1, proj_r1.at[layer], (D2,))
            self.proj_two = links.copy(proj_s2, proj_r2.at[layer], (D1,))
            self.proj_three = links.copy(proj_s3, proj_r3.at[layer], ("c",))
            self.cat_one = [
                [links.copy(cat_s1.at[i, zl], cat_r1.at[layer, i, zl], (D2,)) for zl in range(2)]
                for i in range(2)
            ]
            self.cat_two = [
                links.copy(cat_s2.at[zl], cat_r2.at[layer, zl], (D1,)) for zl in range(2)
            ]
            self.trades = []
            for axes in NEAR:
                there = flipped(me, axes)
                part = cat_a.at[there["zl"], there["y"] * 2 + there["c"]]
                self.trades.append(links.copy(part, parts.at[layer, rank], axes))
            self.keep = pltpu.make_async_copy(
                cat_a.at[me["zl"], me["y"] * 2 + me["c"]], parts.at[layer, rank], own_sem.at[layer, 3]
            )

        def rows_terms(self, start, stop):
            layer = self.layer
            size = (stop - start) * 2 * rows
            kept = ca[layer, start:stop].reshape(size, PAIR + lift)
            for cut in halves:
                rounded = rnd[start:stop, :, :, cut].reshape(size, width // 2)
                for part in (pl.ds(PAIR, lift), pl.ds(0, PAIR)):
                    side = kept[:, PAIR:] if part.start else kept[:, :PAIR]
                    value = dot(side, rounded, ((0,), (0,)))
                    if start:
                        value = value + dp_grad[part, cut]
                    dp_grad[part, cut] = value

        def rows_one(self):
            half = lift // 2
            down_s1[...] = dp_grad[pl.ds(PAIR + (1 - me[D2]) * half, half)].astype(BF16)
            self.down_one.start()

            @pl.when(others)
            def _():
                proj_s1[...] = dp_grad[pl.ds(0, PAIR)].astype(BF16)
                self.proj_one.start()

        def rows_two(self):
            layer = self.layer
            half, quarter = lift // 2, lift // 4
            base = PAIR + me[D2] * half
            self.down_one.wait()
            at = (1 - me[D1]) * quarter
            down_s2[...] = (
                dp_grad[pl.ds(base + at, quarter)]
                + down_r1[layer, pl.ds(at, quarter)].astype(F32)
            ).astype(BF16)
            self.down_two.start()

            @pl.when(others)
            def _():
                self.proj_one.wait_send()

            @pl.when(mine)
            def _():
                self.proj_one.wait_recv()
                at = (1 - me[D1]) * HEAD_DIM
                proj_s2[...] = (
                    dp_grad[pl.ds(at, HEAD_DIM)]
                    + proj_r1[layer, pl.ds(at, HEAD_DIM)].astype(F32)
                ).astype(BF16)
                self.proj_two.start()

        def rows_three(self):
            layer = self.layer
            half, quarter = lift // 2, lift // 4
            base = PAIR + me[D2] * half
            self.down_two.wait()
            at = me[D1] * quarter
            down_out[layer] = (
                dp_grad[pl.ds(base + at, quarter)]
                + down_r1[layer, pl.ds(at, quarter)].astype(F32)
                + down_r2[layer].astype(F32)
            )
            count = proj.shape[1]

            @pl.when(mine)
            def _():
                self.proj_two.wait()
                at = me[D1] * HEAD_DIM

                def half_of(which):
                    return (
                        dp_grad[pl.ds(at + which * count, count)]
                        + proj_r1[layer, pl.ds(at + which * count, count)].astype(F32)
                        + proj_r2[layer, pl.ds(which * count, count)].astype(F32)
                    )

                proj_out[layer] = half_of(me["c"])
                proj_s3[...] = half_of(1 - me["c"]).astype(BF16)
                self.proj_three.start()
                self.proj_three.wait_send()

            @pl.when(others)
            def _():
                self.proj_three.wait_recv()
                proj_out[layer] = proj_r3[layer].astype(F32)

        def cat_terms(self, i):
            layer = self.layer
            zh = me["zh"] if i else 1 - me["zh"]
            deltas = mdud[...].reshape(8 * rows, wide)
            for zl in range(2):
                start = pl.multiple_of((zh * 2 + zl) * (width // 4), width // 4)
                kept = hid[layer, :, :, :, pl.ds(start, width // 4)].reshape(8 * rows, width // 4)
                scratch[zl, : width // 4, :wide] = dot(kept, deltas, ((0,), (0,)))
            size = width // 8
            for zl in range(2):
                cat_s1[i, zl] = scratch[zl, pl.ds((1 - me["x"]) * size, size), :wide].astype(BF16)
                self.cat_one[i][zl].start()
                cat_own[i, zl] = scratch[zl, pl.ds(me["x"] * size, size), :wide]

        def cat_step_two(self, zl):
            layer = self.layer
            self.cat_one[0][zl].wait()
            cat_s2[zl] = (cat_own[0, zl] + cat_r1[layer, 0, zl].astype(F32)).astype(BF16)
            self.cat_two[zl].start()

        def cat_step_three(self, zl):
            layer = self.layer
            self.cat_one[1][zl].wait()
            self.cat_two[zl].wait()
            total = (
                cat_own[1, zl]
                + cat_r1[layer, 1, zl].astype(F32)
                + cat_r2[layer, zl].astype(F32)
            )
            cat_a[zl] = total.astype(BF16).reshape(cat_a.shape[1:])

        def cat_trade(self):
            for copy in self.trades:
                copy.start()
            self.keep.start()

        def cat_done(self):
            for copy in self.trades:
                copy.wait()
            self.keep.wait()

    def put_sums(index, value):
        grad_sum[pl.ds(index, 1), : value.shape[1]] = value

    def own_rows(layer, total, stream_at, up_at, put):
        gain = bias_row(named_row(layer, 0))
        gain_sum = jnp.zeros((1, width), F32)
        shift_sum = jnp.zeros((1, width), F32)
        for m in range(2 * micros):
            at = pl.ds(m * (rows // (2 * micros)), rows // (2 * micros))
            delta = total(at)
            normed, inverse = normalise(stream_at(at))
            gain_sum = gain_sum + jnp.sum(delta * normed, axis=0, keepdims=True)
            shift_sum = shift_sum + jnp.sum(delta, axis=0, keepdims=True)
            scaled = delta * gain
            put(
                at,
                up_at(at) + inverse * (scaled - mean_of(scaled) - normed * mean_of(scaled * normed)),
            )
        put_sums(named_row(layer, 0), gain_sum)
        put_sums(named_row(layer, 1), shift_sum)

    def bias_sums(layer):
        put_sums(ranks_row(layer), jnp.sum(sums[...], axis=0, keepdims=True))
        rounded = jnp.zeros((8, width), F32)
        for m in range(2 * micros):
            size = rows // (2 * micros)
            part = rnd[0, 0, pl.ds(m * size, size)].astype(F32)
            rounded = rounded + jnp.sum(part.reshape(size // 8, 8, width), axis=0)
        put_sums(named_row(layer, 2), jnp.sum(rounded, axis=0, keepdims=True))

    def give_back(turn_index):
        for axes in (("c",), (T1,), (T2,)):
            pl.semaphore_signal(
                free_sem.at[turn_index], inc=1, device_id=links.peer(axes), device_id_type=MESH
            )

    def await_places(turn_index):
        pl.semaphore_wait(free_sem.at[turn_index], 3)

    taken = [Weights(layer) for layer in range(layers)]
    grads = [Grads(layer) for layer in range(layers)]
    row_gathers = [Rows(links, hid.at[1]), Rows(links, mask_all), Rows(links, rnd)]
    hidden_two, rounded_one = Rows(links, hid.at[1]), Rows(links, rnd)
    sets = (core_in, chip_in, core_out, chip_out)
    out_one, delta_two, delta_one = Sums(links, *sets), Sums(links, *sets), Sums(links, *sets)
    out_two = Sums(links, *sets)

    def grad_stage(i):
        return grad_sum if i == 0 else small_sum.at[i - 1]

    small_copies = [
        links.copy(small_sum.at[i], small_in.at[i], (axis,)) for i, axis in enumerate(SMALL_AXES)
    ]
    grad_copies = [
        links.copy(grad_stage(i), small_in.at[i], (axis,)) for i, axis in enumerate(SMALL_AXES)
    ]

    chain = [taken[0].down[0]] + taken[0].cat + [taken[0].down[1], taken[0].heads]
    chain = chain + taken[1].cat + taken[1].down + [taken[1].heads]

    def pump(k):
        chain[k].step()
        if k + 2 < len(chain):
            chain[k + 2].start()
        chain[k].start_far()

    def small_step(i):
        small_copies[i].wait()
        small_sum[i + 1] = small_sum[i] + small_in[i]
        if i + 1 < len(SMALL_AXES):
            small_copies[i + 1].start()

    fetched = fetch_columns()
    for copy in fetched:
        copy.start()
    for one in taken:
        one.keep[1].start()
    spread_small()
    hid[1, 0, 0] = inputs[...]
    for copy in fetched[:pieces]:
        copy.wait()
    columns_by_rank(0)
    links.meet()
    taken[0].start_trades()
    small_copies[0].start()
    chain[0].start()
    for piece in taken[0].down:
        piece.start_near()
    for m in range(micros):
        build_mask(m)
    taken[0].heads.prepare()
    taken[1].heads.prepare()
    grad_sum[...] = jnp.zeros_like(grad_sum)
    small_step(0)
    taken[0].traded()
    chain[1].start()
    row_gathers[1].start()
    row_gathers[0].start()
    for piece in taken[0].cat:
        piece.start_near()
    small_step(1)
    pump(0)
    small_step(2)
    row_gathers[1].forward()
    for copy in fetched[pieces:]:
        copy.wait()
    columns_by_rank(1)
    small_step(3)
    pump(1)
    small_step(4)
    row_gathers[0].forward()
    taken[1].start_trades()

    gain, shift = bias_row(named_row(0, 0)), bias_row(named_row(0, 1))

    def first_norm(j, carry):
        row_gathers[0].arrive(j)
        row_gathers[1].arrive(j)

        def each(p, carry):
            size = rows // 4
            at = pl.ds(pl.multiple_of((p % 4) * size, size), size)
            normed, _ = normalise(hid[1, j, p // 4, at].astype(F32))
            hid[0, j, p // 4, at] = (normed * gain + shift).astype(BF16)
            return carry

        lax.fori_loop(0, 8, each, 0)
        for k in range(3):

            @pl.when(j == k)
            def _():
                pump(2 + k)

        return carry

    lax.fori_loop(0, 4, first_norm, 0)
    row_gathers[0].finish()
    row_gathers[1].finish()
    row_gathers[2].start()
    taken[1].traded()
    pump(5)
    for piece in taken[1].cat + taken[1].down:
        piece.start_near()
    taken[0].cat_done()

    def first(i, j):
        forward(0, j)

        @pl.when(i == 0)
        def _():
            pump(6)
            taken[0].rows_done()
            row_gathers[2].forward()

        for k in range(1, 4):

            @pl.when(i == k)
            def _():
                pump(6 + k)

    out_one.run(first, out_term(0), scratch, own, far_first)
    pump(10)

    def rest_of_rounded(j, carry):
        row_gathers[2].arrive(j)
        return carry

    lax.fori_loop(0, 4, rest_of_rounded, 0)
    row_gathers[2].finish()
    total = out_one.total(own)
    out_bias = bias_row(named_row(0, 2))
    gain, shift = bias_row(named_row(1, 0)), bias_row(named_row(1, 1))
    for m in range(4):
        at = pl.ds(m * (rows // 4), rows // 4)
        stream = inputs[at].astype(F32) + total(at) + out_bias
        stream_two[at] = stream
        normed, _ = normalise(stream)
        hid[1, 0, 0, at] = (normed * gain + shift).astype(BF16)
    hidden_two.start()
    pump(11)
    taken[1].cat_done()

    def second(j, carry):
        hidden_two.arrive(j)
        forward(1, j)

        @pl.when(j == 0)
        def _():
            hidden_two.forward()
            pump(12)
            pump(13)

        @pl.when(j == 2)
        def _():
            taken[1].rows_done()
            grads[1].rows_terms(0, 3)

        return carry

    lax.fori_loop(0, 4, second, 0)
    hidden_two.finish()
    grads[1].rows_terms(3, 4)
    grads[1].rows_one()

    sums[...] = jnp.zeros_like(sums)

    def fourth(i, j):
        backward(1, j)

        @pl.when(i == 2)
        def _():
            grads[1].rows_two()

    delta_two.run(fourth, hidden_term(1), scratch, own, far_first)
    bias_sums(1)
    give_back(2)
    grads[1].cat_terms(0)
    grads[1].cat_terms(1)
    total = delta_two.total(own)
    await_places(2)

    def put_one(at, value):
        up_one[at] = value
        rnd[0, 0, at] = value.astype(BF16)

    own_rows(1, total, lambda at: stream_two[at], lambda at: rnd[0, 0, at].astype(F32), put_one)
    rounded_one.start()
    give_back(0)
    sums[...] = jnp.zeros_like(sums)
    for zl in range(2):
        grads[1].cat_step_two(zl)
    grads[1].rows_three()
    await_places(0)
    rounded_one.forward()

    def third(i, j):
        @pl.when(i == 2)
        def _():
            for zl in range(2):
                grads[1].cat_step_three(zl)
            grads[1].cat_trade()
            rounded_one.arrive(1)

        @pl.when(i < 3)
        def _():
            rounded_one.arrive(j)

        @pl.when(i == 2)
        def _():
            rounded_one.finish()
            grads[0].rows_terms(0, 4)
            grads[0].rows_one()

        backward(0, j)

    delta_one.run(third, hidden_term(0), scratch, own, near_first)
    grads[0].cat_terms(0)
    grads[0].cat_terms(1)
    bias_sums(0)
    grads[0].rows_two()
    for zl in range(2):
        grads[0].cat_step_two(zl)
    total = delta_one.total(own)

    def put_last(at, value):
        input_grad[at] = value

    own_rows(0, total, lambda at: inputs[at].astype(F32), lambda at: up_one[at], put_last)
    grad_copies[0].start()
    give_back(1)
    grads[1].cat_done()
    await_places(1)
    out_two.run(lambda i, j: None, out_term(1), scratch, own, far_first)
    for i in range(len(SMALL_AXES)):
        grad_copies[i].wait()
        grad_stage(i + 1)[...] = grad_stage(i)[...] + small_in[i]
        if i + 1 < len(SMALL_AXES):
            grad_copies[i + 1].start()
        if i == 2:
            for zl in range(2):
                grads[0].cat_step_three(zl)
            grads[0].cat_trade()
        if i == 3:
            grads[0].rows_three()
    own_small(grad_stage(len(SMALL_AXES)))
    total = out_two.total(own)
    out_bias = bias_row(named_row(1, 2))
    for m in range(4):
        at = pl.ds(m * (rows // 4), rows // 4)
        outputs[at] = (stream_two[at] + total(at) + out_bias).astype(BF16)
    returned = return_columns(1) + return_columns(0)
    columns_by_name(1)
    for copy in returned[:pieces]:
        copy.start()
    grads[0].cat_done()
    columns_by_name(0)
    for copy in returned[pieces:]:
        copy.start()
    for copy in returned:
        copy.wait()


def named_rows(layers):
    return -(-3 * layers // 8) * 8


def run_layers(qkv, up, down, proj, inputs, cotangent, marks, small, tables):
    layers, count = qkv.shape[:2]
    rows, width = inputs.shape
    micros, lanes = marks.shape
    pack = rows // micros
    lift = up.shape[2] // RANKS
    wide = QKV + lift
    vmem = pl.BlockSpec(memory_space=pltpu.VMEM)
    anywhere = pl.BlockSpec(memory_space=pltpu.HBM)
    shape = jax.ShapeDtypeStruct
    stages = len(SMALL_AXES)
    small_rows = layers * RANKS + named_rows(layers)
    copies = 256
    cat_size = width // 8
    buffers = [
        ((layers, RANKS, count, wide), BF16),
        ((layers, 32, count, wide), BF16),
        ((layers, PAIR + lift, width), BF16),
        ((layers, 4, 2, rows, width), BF16),
        ((4, 2, rows, width), BF16),
        ((4, 2, micros, pack, lanes), BF16),
        ((layers, 4, 2 * rows, QKV), BF16),
        ((layers, 4, 2 * micros, 2 * pack, pack), BF16),
        ((layers, 4, 2 * rows, PAIR + lift), BF16),
        ((layers, 4, 2 * rows, lift), BF16),
        ((4, 2 * rows, wide), BF16),
        ((2, 2 * rows, width), F32),
        ((4, rows, width), BF16),
        ((3, rows, width), BF16),
        ((4, rows, width), BF16),
        ((3, rows, width), BF16),
        ((rows, width), F32),
        ((rows, width), F32),
        ((rows, width), F32),
        ((stages + 1, small_rows, width), F32),
        ((stages, small_rows, width), F32),
        ((8, wide), F32),
        ((small_rows, width), F32),
        ((2, 2, cat_size, wide), F32),
        ((2, 2, cat_size, wide), BF16),
        ((layers, 2, 2, cat_size, wide), BF16),
        ((2, cat_size, wide), BF16),
        ((layers, 2, cat_size, wide), BF16),
        ((2, 4, count, wide), BF16),
        ((PAIR + lift, width), F32),
        ((lift // 2, width), BF16),
        ((layers, lift // 2, width), BF16),
        ((lift // 4, width), BF16),
        ((layers, lift // 4, width), BF16),
        ((PAIR, width), BF16),
        ((layers, PAIR, width), BF16),
        ((HEAD_DIM, width), BF16),
        ((layers, HEAD_DIM, width), BF16),
        ((HEAD_DIM // 2, width), BF16),
        ((layers, HEAD_DIM // 2, width), BF16),
    ]
    return pl.pallas_call(
        layers_kernel,
        out_shape=(
            shape((rows, width), BF16),
            shape((rows, width), F32),
            shape((layers, width // 32), F32),
            shape((layers, width // 32), F32),
            shape(qkv.shape, F32),
            shape((layers, 2 * width // 32), F32),
            shape(proj.shape, F32),
            shape((layers, width // 32), F32),
            shape(up.shape, F32),
            shape((layers, up.shape[2] // 32), F32),
            shape(down.shape, F32),
        ),
        in_specs=[anywhere] * 4 + [vmem] * 5,
        out_specs=(vmem,) * 4 + (anywhere,) + (vmem,) * 3 + (anywhere,) + (vmem,) * 2,
        scratch_shapes=[pltpu.VMEM(dims, kind) for dims, kind in buffers]
        + [
            pltpu.SemaphoreType.DMA((copies,)),
            pltpu.SemaphoreType.DMA((copies,)),
            pltpu.SemaphoreType.DMA((layers, 4)),
            pltpu.SemaphoreType.REGULAR((3,)),
            pltpu.SemaphoreType.DMA((layers * 7,)),
        ],
        compiler_params=pltpu.CompilerParams(
            collective_id=0, has_side_effects=True, vmem_limit_bytes=63 << 20
        ),
    )(qkv, up, down, proj, inputs, cotangent, marks, small, tables)


def refold(block, extra):
    if extra == 1:
        return block
    whole = lax.all_gather(block, AXES, axis=1, tiled=True)
    rows = whole.shape[1] // 32
    return lax.dynamic_slice_in_dim(whole, lax.axis_index(AXES[1:]) * rows, rows, 1)


def unfold(block, extra):
    if extra == 1:
        return block
    rows = block.shape[1]
    whole = jnp.zeros((block.shape[0], 32 * rows) + block.shape[2:], F32)
    whole = lax.dynamic_update_slice_in_dim(whole, block, lax.axis_index(AXES[1:]) * rows, 1)
    return lax.psum_scatter(whole, AXES, scatter_dimension=1, tiled=True)


def rope_tables(pack):
    half = ROT // 2
    angle = np.arange(pack, dtype=np.float32)[:, None] * (
        np.float32(10000.0) ** (-np.arange(0, ROT, 2, dtype=np.float32) / np.float32(ROT))
    )
    angle = angle.astype(np.float32)
    tables = np.zeros((3, pack, 2, HEAD_DIM), np.float32)
    tables[0] = 1.0
    tables[0, :, :, :half] = tables[0, :, :, half:ROT] = np.cos(angle)[:, None]
    tables[1, :, :, :half] = -np.sin(angle)[:, None]
    tables[2, :, :, half:ROT] = np.sin(angle)[:, None]
    return tables.reshape(3, pack, PAIR)


def shards(
    inputs,
    cotangent,
    segments,
    pack_length,
    norm_gain,
    norm_shift,
    qkv_weight,
    qv_bias,
    proj_weight,
    proj_bias,
    up_weight,
    up_bias,
    down_weight,
    down_bias,
):
    micros, pack, width = inputs.shape
    layers = qkv_weight.shape[0]
    extra = lax.axis_size("e")
    marks = jnp.concatenate([segments, pack_length], axis=1).astype(F32)
    marks = jnp.pad(marks, ((0, 0), (0, -(pack + 1) % 128)))

    def row(value):
        return jnp.pad(value.astype(F32), ((0, 0), (0, width - value.shape[1])))

    biases = refold(proj_bias, extra).astype(F32) + refold(down_bias, extra).astype(F32)
    vectors = [row(refold(norm_gain, extra)), row(refold(norm_shift, extra)), row(biases)]
    vectors = jnp.stack(vectors, axis=1).reshape(3 * layers, width)
    named = named_rows(layers)
    small = jnp.concatenate(
        [
            jnp.pad(vectors, ((0, named - 3 * layers), (0, 0))),
            row(refold(qv_bias, extra)),
            row(refold(up_bias, extra)),
            jnp.zeros((-2 * layers % 8, width), F32),
        ]
    )
    given = run_layers(
        refold(qkv_weight, extra),
        refold(up_weight, extra),
        refold(down_weight, extra),
        refold(proj_weight, extra),
        inputs.reshape(micros * pack, width),
        cotangent.reshape(micros * pack, width),
        marks,
        small,
        jnp.asarray(rope_tables(pack)),
    )
    out, input_grad = given[:2]
    gain, shift, qkv, qvb, proj, bias, up, upb, down = [unfold(g, extra) for g in given[2:]]
    return (
        out.reshape(micros, pack, width),
        input_grad.reshape(micros, pack, width),
        gain,
        shift,
        qkv,
        qvb,
        proj,
        bias,
        up,
        upb,
        down,
        bias,
    )


def solution(mesh):
    devices = mesh.devices.size
    fine = Mesh(mesh.devices.reshape(devices // 32, 2, 2, 2, 2, 2), AXES)
    cube, flat = P(None, AXES, None), P(None, AXES)
    placed = (cube, cube, flat, flat, flat, flat, cube, flat, cube, flat, cube, flat, cube, flat)
    given = (cube, cube, flat, flat, cube, flat, cube, flat, cube, flat, cube, flat)
    return jax.shard_map(shards, mesh=fine, in_specs=placed, out_specs=given, check_vma=False)
```

```python
import math

import jax
import jax.numpy as jnp
import numpy as np
from jax import lax
from jax.experimental import pallas as pl
from jax.experimental.pallas import tpu as pltpu
from jax.sharding import Mesh
from jax.sharding import PartitionSpec as P

HEAD_DIM = 64
ROT = 16
EPS = 1e-05
MASKED = -1e30

AXES = ("e", "zh", "zl", "x", "y", "c")
T1, T2, D1, D2 = "y", "zl", "zh", "x"
TP = (T1, T2, "c")
RANKS = 8
NEAR = (("c",), (T1,), (T2,), (T1, "c"), (T2, "c"), (T1, T2), (T1, T2, "c"))
FAR = ((D1,), (D2,))
SMALL_AXES = ("zh", "x", "zl", "y", "c")
GRAD_AXES = ("c", T1, T2, D1, D2)

F32, BF16 = jnp.float32, jnp.bfloat16
MESH = pl.DeviceIdType.MESH

PAIR = 2 * HEAD_DIM
QKV = 3 * PAIR


def dot(a, b, contract):
    return lax.dot_general(a, b, (contract, ((), ())), preferred_element_type=F32)


class Links:
    def __init__(self, send_sem, recv_sem):
        self.place = {axis: lax.axis_index(axis) for axis in AXES}
        self.send_sem, self.recv_sem, self.used = send_sem, recv_sem, 0

    def reserve(self, count):
        self.used += count
        return self.used - count

    def peer(self, axes):
        return {axis: 1 - self.place[axis] for axis in axes}

    def meet(self):
        barrier = pltpu.get_barrier_semaphore()
        for axes in NEAR + FAR:
            pl.semaphore_signal(barrier, inc=1, device_id=self.peer(axes), device_id_type=MESH)
        pl.semaphore_wait(barrier, len(NEAR) + len(FAR))

    def copy(self, source, target, device, slot=None):
        if slot is None:
            slot = self.reserve(1)
        if not isinstance(device, dict):
            device = self.peer(device)
        return pltpu.make_async_remote_copy(
            src_ref=source,
            dst_ref=target,
            send_sem=self.send_sem.at[slot],
            recv_sem=self.recv_sem.at[slot],
            device_id=device,
            device_id_type=MESH,
        )


def rank_of(place):
    return place[T1] * 4 + place[T2] * 2 + place["c"]


def block_of(place):
    index = place["zh"]
    for axis in AXES[2:]:
        index = index * 2 + place[axis]
    return index


def flipped(place, axes):
    return {a: (1 - i if a in axes else i) for a, i in place.items()}


class Rows:
    def __init__(self, links, buffer):
        self.links, self.buffer, self.base = links, buffer, links.reserve(9)
        self.near = [
            None,
            links.copy(buffer.at[0, 0], buffer.at[1, 0], (T2,), self.base + 5),
            links.copy(buffer.at[0, 0], buffer.at[2, 0], (T1,), self.base + 6),
        ]
        self.far = [
            links.copy(buffer.at[1, 0], buffer.at[3, 0], (T1,), self.base + 7),
        ]

    def core(self, j):
        return self.links.copy(
            self.buffer.at[j, 0], self.buffer.at[j, 1], ("c",), self.base + j
        )

    def start(self):
        self.core(0).start()
        self.near[1].start()
        self.near[2].start()

    def forward(self):
        self.near[1].wait_recv()
        self.far[0].start()
        self.core(1).start()
        self.near[2].wait_recv()
        self.core(2).start()

    def arrive(self, j):
        @pl.when(j == 3)
        def _():
            self.far[0].wait_recv()
            self.core(3).start()

        self.core(j).wait_recv()

    def finish(self):
        for j in range(4):
            self.core(j).wait_send()
        for copy in self.near[1:] + self.far:
            copy.wait_send()


def far_first(i):
    return 3 - i


def near_first(i):
    return i + 1 - 3 * (i // 3) - (3 - i) // 3


class Sums:
    def __init__(self, links, core_in, chip_in, core_out, chip_out, turned=False):
        self.links, self.base = links, links.reserve(8)
        self.relayed, self.far_axis = (2, T2) if turned else (1, T1)
        self.core_in, self.chip_in, self.core_out, self.chip_out = core_in, chip_in, core_out, chip_out

    def core(self, j):
        return self.links.copy(
            self.core_out.at[j], self.core_in.at[j], ("c",), self.base + j
        )

    def chip(self, j):
        return self.links.copy(
            self.chip_out.at[j - 1],
            self.chip_in.at[j - 1],
            ((T2,), (T1,), (self.far_axis,))[j - 1],
            self.base + 4 + j,
        )

    def run(self, before, term, scratch, own, order, hold=False):
        rows = own.shape[0]

        def pass_on(j):
            self.core(j).wait_recv()
            for m in range(2):
                at = pl.ds(m * (rows // 2), rows // 2)
                total = scratch[1, at] + self.core_in[j, at].astype(F32)
                for k in (1, 2, 3):

                    @pl.when(j == k)
                    def _():
                        value = total
                        if k == self.relayed and not hold:
                            if m == 0:
                                self.chip(3).wait_recv()
                            value = value + self.chip_in[2, at].astype(F32)
                        self.chip_out[k - 1, at] = value.astype(BF16)
                        if m == 1 and not hold:
                            self.chip(k).start()

                @pl.when(j == 0)
                def _():
                    own[at] = total

        def step(i, carry):
            j = order(i)
            before(i, j)

            @pl.when(i > 0)
            def _():
                pass_on(order(i - 1))

            term(j, scratch.at[1])
            self.core_out[j] = scratch[1, rows:].astype(BF16)
            self.core(j).start()
            return carry

        lax.fori_loop(0, 4, step, 0)
        return lambda: pass_on(order(3))

    def release(self):
        self.chip(3).start()
        self.chip(3 - self.relayed).start()

    def relay(self):
        self.chip(3).wait_recv()
        rows, place = self.chip_out.shape[1], self.relayed - 1
        for m in range(4):
            at = pl.ds(m * (rows // 4), rows // 4)
            value = self.chip_out[place, at].astype(F32) + self.chip_in[2, at].astype(F32)
            self.chip_out[place, at] = value.astype(BF16)
        self.chip(self.relayed).start()

    def total(self, own, held=False):
        for j in (1, 2):
            self.chip(j).wait_recv()
        if not held:
            for j in range(4):
                self.core(j).wait_send()
        for j in (1, 2, 3):
            self.chip(j).wait_send()

        def at(rows):
            value = own[rows]
            for j in (1, 2):
                value = value + self.chip_in[j - 1, rows].astype(F32)
            return value

        return at


def mean_of(value):
    return jnp.sum(value, axis=-1, keepdims=True) * (1.0 / value.shape[-1])


def normalise(stream):
    centred = stream - mean_of(stream)
    inverse = lax.rsqrt(mean_of(centred * centred) + EPS)
    return centred * inverse, inverse


def layers_kernel(
    qkv,
    up,
    down,
    proj,
    inputs,
    cotangent,
    marks,
    small,
    tables,
    outputs,
    input_grad,
    gain_out,
    shift_out,
    qkv_out,
    qvb_out,
    proj_out,
    bias_out,
    up_out,
    upb_out,
    down_out,
    parts,
    cat_all,
    dp_all,
    hid,
    rnd,
    mask_all,
    qkv_kept,
    probs,
    ca,
    slope,
    mdud,
    scratch,
    core_in,
    chip_in,
    core_out,
    chip_out,
    own,
    stream_two,
    up_one,
    small_all,
    named,
    rank_bias,
    sums,
    grad_sum,
    grad_in,
    cat_own,
    cat_s1,
    cat_r1,
    cat_s2,
    cat_r2,
    cat_a,
    dp_grad,
    down_s1,
    down_r1,
    down_s2,
    down_r2,
    proj_s1,
    proj_r1,
    proj_s2,
    proj_r2,
    proj_s3,
    proj_r3,
    send_sem,
    recv_sem,
    own_sem,
    free_sem,
    fetch_sem,
):
    links = Links(send_sem, recv_sem)
    me = links.place
    rank, block, slot = rank_of(me), block_of(me), me[D2] * 2 + me[D1]
    mine = me["c"] == me[D2]
    others = jnp.logical_not(mine)
    layers, wide = parts.shape[0], parts.shape[3]
    micros, lanes = marks.shape
    rows, width = inputs.shape
    pack = rows // micros
    count = qkv.shape[1]
    lift = wide - QKV
    scale = 1.0 / math.sqrt(HEAD_DIM)
    lane = lax.broadcasted_iota(jnp.int32, (pack, PAIR), 1)
    first_head = lane < HEAD_DIM

    def bias_row(layer, kind):
        return named[kind, layer : layer + 1, :]

    pieces = 3 + up.shape[2] // width
    raw = [core_out.at[i // 6, pl.ds(i % 6 * count, count)] for i in range(layers * pieces)]
    final = [scratch.at[i // 8, pl.ds(i % 8 * count, count)] for i in range(layers * pieces)]

    def fetch_columns():
        copies = []
        for i in range(layers * pieces):
            layer, k = i // pieces, i % pieces
            source = qkv.at[layer, :, pl.ds(k * width, width)] if k < 3 else up.at[
                layer, :, pl.ds((k - 3) * width, width)
            ]
            copies.append(pltpu.make_async_copy(source, raw[i], fetch_sem.at[i]))
        return copies

    def return_columns(layer):
        copies = []
        for k in range(pieces):
            i = layer * pieces + k
            target = qkv_out.at[layer, :, pl.ds(k * width, width)] if k < 3 else up_out.at[
                layer, :, pl.ds((k - 3) * width, width)
            ]
            copies.append(pltpu.make_async_copy(final[i], target, fetch_sem.at[i]))
        return copies

    lane_row = lax.broadcasted_iota(jnp.int32, (count, PAIR), 1) < HEAD_DIM

    def shared(one, other):
        one, other = one.astype(F32), other.astype(F32)
        return (
            jnp.where(lane_row, one, pltpu.roll(other, HEAD_DIM, 1)),
            jnp.where(lane_row, pltpu.roll(one, HEAD_DIM, 1), other),
        )

    def columns_by_rank(layer):
        base = layer * pieces
        for p in range(3):
            for zl in range(2):
                for x in range(2):
                    tiles = [
                        raw[base + p][:, (zh * 4 + zl * 2 + x) * PAIR : (zh * 4 + zl * 2 + x + 1) * PAIR]
                        for zh in range(2)
                    ]
                    for y, tile in enumerate(shared(*tiles)):
                        parts[layer, y * 4 + zl * 2 + x, :, p * PAIR : (p + 1) * PAIR] = tile.astype(BF16)
        size = up.shape[2] // 32
        for b in range(32):
            zh, zl, x, y, c = b // 16, b // 8 % 2, b // 4 % 2, b // 2 % 2, b % 2
            k, at = b * size // width, b * size % width
            to = QKV + (x * 2 + zh) * size
            parts[layer, y * 4 + zl * 2 + c, :, to : to + size] = raw[base + 3 + k][:, at : at + size]

    def columns_by_name(layer):
        base = layer * pieces
        for p in range(3):
            for zl in range(2):
                for x in range(2):
                    tiles = [
                        parts[layer, y * 4 + zl * 2 + x, :, p * PAIR : (p + 1) * PAIR] for y in range(2)
                    ]
                    for zh, tile in enumerate(shared(*tiles)):
                        at = (zh * 4 + zl * 2 + x) * PAIR
                        final[base + p][:, at : at + PAIR] = tile
        size = up.shape[2] // 32
        for b in range(32):
            zh, zl, x, y, c = b // 16, b // 8 % 2, b // 4 % 2, b // 2 % 2, b % 2
            k, at = b * size // width, b * size % width
            to = QKV + (x * 2 + zh) * size
            tile = parts[layer, y * 4 + zl * 2 + c, :, to : to + size]
            final[base + 3 + k][:, at : at + size] = tile.astype(F32)

    head_rank = me["c"] * 4 + me["x"] * 2 + me["y"]
    head_cut = pl.ds(pl.multiple_of(me["zh"] * 2 * PAIR, PAIR), PAIR)
    up_size = up.shape[2] // 32
    up_cut = pl.ds(pl.multiple_of(QKV + slot * up_size, PAIR), up_size)

    rank_row = lax.broadcasted_iota(jnp.int32, (RANKS, PAIR), 0)
    own_tile = me["c"] * 16 + me["y"] * 8 + me["zl"] * 4 + me["x"] * 2 + me["zh"]

    def expand_small():
        share = width // 32
        lanes_of = lax.broadcasted_iota(jnp.int32, (8, PAIR), 1) // share
        for group in range(8):
            zh, zl, x = group // 4, group // 2 % 2, group % 2
            tiles = [small_all[c * 16 + y * 8 + zl * 4 + x * 2 + zh] for y in range(2) for c in range(2)]
            for kind in range(3):
                value = jnp.zeros((8, PAIR), F32)
                for r, tile in enumerate(tiles):
                    moved = (r - kind) % 4 * share
                    tile = pltpu.roll(tile, moved, 1) if moved else tile
                    value = jnp.where(lanes_of == r, tile, value)
                named[kind, :, group * PAIR : (group + 1) * PAIR] = value
        rank_bias[...] = jnp.zeros_like(rank_bias)
        here = lax.broadcasted_iota(jnp.int32, (8, PAIR), 1) < HEAD_DIM
        for layer in range(layers):
            at = slice(layer, layer + 1)
            for part in range(2):
                heads = []
                for zh in range(2):
                    tile = small_all[
                        me["y"] * 16 + me["c"] * 8 + zh * 4 + me["zl"] * 2 + part, layers : layers + 1, :
                    ]
                    tile = jnp.broadcast_to(tile, (8, PAIR))
                    heads.append(tile if zh == layer else pltpu.roll(tile, HEAD_DIM, 1))
                cut = slice(2 * part * PAIR, (2 * part + 1) * PAIR)
                rank_bias[at, cut] = jnp.where(here, heads[0], heads[1])[:1]
            for x in range(2):
                for zh in range(2):
                    tile = me["c"] * 16 + me["y"] * 8 + me["zl"] * 4 + x * 2 + zh
                    to = QKV + (x * 2 + zh) * up_size
                    line = layers + 1 + layer
                    rank_bias[at, to : to + up_size] = small_all[tile, line : line + 1, :]

    def own_small(layer):
        share = width // 32
        total = grad_sum.at[layer, len(SMALL_AXES)]
        moved = pltpu.roll(total[RANKS:], (32 - block) % 32 * share, 1)
        at = slice(layer, layer + 1)
        gain_out[at] = moved[0:1, :share]
        shift_out[at] = moved[1:2, :share]
        bias_out[at] = moved[2:3, :share]
        pair = pltpu.roll(total[:RANKS, head_cut], me["zl"] * HEAD_DIM, 1)
        pair = jnp.where(rank_row == head_rank, pair, 0.0)
        qvb_out[at] = jnp.sum(pair, axis=0, keepdims=True)[:, :HEAD_DIM]
        more = jnp.where(rank_row == rank, total[:RANKS, up_cut], 0.0)
        upb_out[at] = jnp.sum(more, axis=0, keepdims=True)

    def build_mask(m):
        row = lax.broadcasted_iota(jnp.int32, (lanes, lanes), 0)
        column = lax.broadcasted_iota(jnp.int32, (lanes, lanes), 1)
        across = jnp.broadcast_to(marks[pl.ds(m, 1), :], (lanes, lanes))
        length = marks[pl.ds(m, 1), pack : pack + 1]
        live = column.astype(F32) < length
        allowed = (across.T == across) & (column <= row) & (live | (column == row))
        hidden = jnp.where(allowed, 0.0, MASKED).astype(BF16)
        mask_all[0, 0, m] = hidden[:pack]
        live = lax.broadcasted_iota(jnp.int32, (pack, 1), 0).astype(F32) < length
        at = pl.ds(m * pack, pack)
        rnd[0, 0, at] = jnp.where(live, cotangent[at].astype(F32), 0.0).astype(BF16)

    class Piece:
        def __init__(self, own, at):
            here, there = at(me["zh"]), at(1 - me["zh"])
            self.one = links.copy(here if own is None else own, here, (D1,))
            self.near = links.copy(here if own is None else own, here, (D2,))
            self.far = links.copy(there, there, (D2,))

        def start(self):
            self.one.start()

        def start_near(self):
            self.near.start()

        def step(self):
            self.one.wait()

        def start_far(self):
            self.far.start()

        def done(self):
            self.near.wait()
            self.far.wait()

    class Heads:
        def __init__(self, layer):
            self.layer = layer
            count = proj.shape[1]
            half = dp_all.at[layer, pl.ds(me["zh"] * HEAD_DIM + me["c"] * count, count)]
            self.to_core = links.copy(proj.at[layer], half, ("c",))
            self.stays = pltpu.make_async_copy(proj.at[layer], half, own_sem.at[layer, 2])
            head = dp_all.at[layer, pl.ds(me["zh"] * HEAD_DIM, HEAD_DIM)]
            self.one = links.copy(head, head, (D1,))
            heads = dp_all.at[layer, pl.ds(0, PAIR)]
            self.two = links.copy(heads, heads, (D2,))

        def prepare(self):
            @pl.when(mine)
            def _():
                self.stays.start()
                self.stays.wait()

            @pl.when(others)
            def _():
                self.to_core.start()
                self.to_core.wait_send()

        def start(self):
            @pl.when(mine)
            def _():
                self.to_core.wait_recv()
                self.one.start()

        def step(self):
            @pl.when(mine)
            def _():
                self.one.wait()

        def start_far(self):
            @pl.when(mine)
            def _():
                self.two.start()

        def done(self):
            @pl.when(mine)
            def _():
                self.two.wait_send()

            @pl.when(others)
            def _():
                self.two.wait_recv()

    class Weights:
        def __init__(self, layer):
            self.layer = layer
            size = down.shape[1]
            self.keep = [
                pltpu.make_async_copy(
                    parts.at[layer, rank], cat_all.at[layer, block], own_sem.at[layer, 0]
                ),
                pltpu.make_async_copy(
                    down.at[layer], self.down_rows(me["zh"], 0, size), own_sem.at[layer, 1]
                ),
            ]
            self.trades = [
                links.copy(
                    parts.at[layer, rank_of(flipped(me, axes))], cat_all.at[layer, block], axes
                )
                for axes in NEAR
            ]
            self.cat = [
                Piece(None, lambda zh, zl=zl, h=h: self.cat_rows(zh, zl, h))
                for zl in range(2)
                for h in range(2)
            ]
            half = size // 2
            self.down = [
                Piece(
                    down.at[layer, pl.ds(h * half, half)],
                    lambda zh, h=h: self.down_rows(zh, h * half, half),
                )
                for h in range(2)
            ]
            self.heads = Heads(layer)

        def cat_rows(self, zh, zl, h):
            return cat_all.at[self.layer, pl.ds(zh * 16 + zl * 8 + me["x"] * 4 + 2 * h, 2)]

        def down_rows(self, zh, start, count):
            size = down.shape[1]
            return dp_all.at[
                self.layer, pl.ds(PAIR + (me[D2] * 2 + zh) * size + start, count)
            ]

        def start_trades(self):
            self.keep[0].start()
            for copy in self.trades:
                copy.start()

        def traded(self):
            self.keep[0].wait()
            for copy in self.trades:
                copy.wait()

        def cat_done(self):
            for piece in self.cat:
                piece.done()

        def rows_done(self):
            self.keep[1].wait()
            for piece in self.down:
                piece.done()
            self.heads.done()

    def turn(value, sign):
        return (
            value * tables[0]
            + pltpu.roll(value, PAIR - ROT // 2, 1) * (tables[1] * sign)
            + pltpu.roll(value, ROT // 2, 1) * (tables[2] * sign)
        )

    def by_head(value):
        zero = jnp.zeros_like(value)
        return jnp.concatenate(
            [jnp.where(first_head, value, zero), jnp.where(first_head, zero, value)], axis=0
        )

    def of_heads(value):
        return jnp.where(first_head, value[:pack], value[pack:])

    def forward(layer, j):
        hidden = hid[layer, j].reshape(2 * rows, width)
        for cut in (slice(0, QKV), slice(QKV, wide)):
            columns = cat_all[layer, :, :, cut].reshape(width, -1)
            scratch[0, :, cut] = dot(hidden, columns, ((1,), (0,)))
        bias = rank_bias[layer : layer + 1, :]

        def each(p, carry):
            at = pl.ds(pl.multiple_of(p * pack, pack), pack)
            turned = scratch[0, at, :QKV] + bias[:, :QKV]
            queries = turn(turned[:, :PAIR], 1.0).astype(BF16)
            keys = turn(turned[:, PAIR : 2 * PAIR], 1.0).astype(BF16)
            values = turned[:, 2 * PAIR :].astype(BF16)
            qkv_kept[layer, j, at, :PAIR] = queries
            qkv_kept[layer, j, at, PAIR : 2 * PAIR] = keys
            qkv_kept[layer, j, at, 2 * PAIR :] = values
            hide = mask_all[j, p // micros, p % micros][:, :pack].astype(F32)
            scores = dot(by_head(queries), keys, ((1,), (1,))) * scale
            scores = scores + jnp.concatenate([hide, hide], axis=0)
            shifted = jnp.exp(scores - jnp.max(scores, axis=-1, keepdims=True))
            soft = shifted / jnp.sum(shifted, axis=-1, keepdims=True)
            soft = soft.astype(BF16)
            probs[layer, j, p] = soft
            ca[layer, j, at, :PAIR] = of_heads(dot(soft, values, ((1,), (0,)))).astype(BF16)
            for start in range(QKV, wide, 2 * PAIR):
                cut = slice(start, start + 2 * PAIR)
                raised = scratch[0, at, cut] + bias[:, cut]
                cdf = 0.5 * (1.0 + lax.erf(raised * 0.7071067811865476))
                density = jnp.exp(-0.5 * raised * raised) * 0.3989422804014327
                to = start - QKV
                ca[layer, j, at, PAIR + to : PAIR + to + 2 * PAIR] = (raised * cdf).astype(BF16)
                slope[layer, j, at, to : to + 2 * PAIR] = (cdf + raised * density).astype(BF16)
            return carry

        lax.fori_loop(0, 2 * micros, each, 0)

    def backward(layer, j):
        rounded = rnd[j].reshape(2 * rows, width)
        for cut in (slice(0, PAIR), slice(PAIR, PAIR + lift)):
            scratch[0, :, cut] = dot(rounded, dp_all[layer, cut], ((1,), (1,)))

        def each(p, carry):
            at = pl.ds(pl.multiple_of(p * pack, pack), pack)
            for start in range(0, lift, 2 * PAIR):
                cut = slice(start, start + 2 * PAIR)
                grown = scratch[0, at, PAIR + start : 3 * PAIR + start]
                grown = (grown * slope[layer, j, at, cut].astype(F32)).astype(BF16)
                mdud[j, at, QKV + start : QKV + start + 2 * PAIR] = grown
                sums[:, QKV + start : QKV + start + 2 * PAIR] += jnp.sum(
                    grown.astype(F32).reshape(pack // 8, 8, 2 * PAIR), axis=0
                )
            context = by_head(scratch[0, at, :PAIR].astype(BF16))
            queries = by_head(qkv_kept[layer, j, at, :PAIR])
            keys = qkv_kept[layer, j, at, PAIR : 2 * PAIR]
            values = qkv_kept[layer, j, at, 2 * PAIR :]
            kept = probs[layer, j, p]
            soft = kept.astype(F32)
            prob_delta = dot(context, values, ((1,), (1,)))
            row_delta = jnp.sum(soft * prob_delta, axis=-1, keepdims=True)
            score_delta = (soft * (prob_delta - row_delta)).astype(BF16)
            value_delta = dot(kept, context, ((0,), (0,)))
            query_delta = of_heads(dot(score_delta, keys, ((1,), (0,)))) * scale
            key_delta = dot(score_delta, queries, ((0,), (0,))) * scale
            three = (turn(query_delta, -1.0), turn(key_delta, -1.0), value_delta)
            for i, delta in enumerate(three):
                delta = delta.astype(BF16)
                cut = slice(i * PAIR, (i + 1) * PAIR)
                mdud[j, at, cut] = delta
                sums[:, cut] += jnp.sum(delta.astype(F32).reshape(pack // 8, 8, PAIR), axis=0)
            return carry

        lax.fori_loop(0, 2 * micros, each, 0)

    halves = (slice(0, width // 2), slice(width // 2, width))

    def out_term(layer):
        def put(j, target):
            for cut in halves:
                target[:, cut] = dot(ca[layer, j], dp_all[layer, :, cut], ((1,), (0,)))

        return put

    def hidden_term(layer):
        def put(j, target):
            for half, cut in enumerate(halves):
                columns = cat_all[layer, pl.ds(16 * half, 16)].reshape(width // 2, wide)
                target[:, cut] = dot(mdud[j], columns, ((1,), (1,)))

        return put

    class Grads:
        def __init__(self, layer):
            self.layer = layer
            self.down_one = links.copy(down_s1, down_r1.at[layer], (D2,))
            self.down_two = links.copy(down_s2, down_r2.at[layer], (D1,))
            self.proj_one = links.copy(proj_s1, proj_r1.at[layer], (D2,))
            self.proj_two = links.copy(proj_s2, proj_r2.at[layer], (D1,))
            self.proj_three = links.copy(proj_s3, proj_r3.at[layer], ("c",))
            self.cat_one = [
                [links.copy(cat_s1.at[i, zl], cat_r1.at[layer, i, zl], (D2,)) for zl in range(2)]
                for i in range(2)
            ]
            self.cat_two = [
                links.copy(cat_s2.at[zl], cat_r2.at[layer, zl], (D1,)) for zl in range(2)
            ]
            self.trades = []
            for axes in NEAR:
                there = flipped(me, axes)
                part = cat_a.at[there["zl"], there["y"] * 2 + there["c"]]
                self.trades.append(links.copy(part, parts.at[layer, rank], axes))
            self.keep = pltpu.make_async_copy(
                cat_a.at[me["zl"], me["y"] * 2 + me["c"]], parts.at[layer, rank], own_sem.at[layer, 3]
            )

        def rows_terms(self, start, stop):
            layer = self.layer
            size = (stop - start) * 2 * rows
            kept = ca[layer, start:stop].reshape(size, PAIR + lift)
            for cut in halves:
                rounded = rnd[start:stop, :, :, cut].reshape(size, width // 2)
                for part in (pl.ds(PAIR, lift), pl.ds(0, PAIR)):
                    side = kept[:, PAIR:] if part.start else kept[:, :PAIR]
                    value = dot(side, rounded, ((0,), (0,)))
                    if start:
                        value = value + dp_grad[part, cut]
                    dp_grad[part, cut] = value

        def rows_one(self):
            half = lift // 2
            down_s1[...] = dp_grad[pl.ds(PAIR + (1 - me[D2]) * half, half)].astype(BF16)
            self.down_one.start()

            @pl.when(others)
            def _():
                proj_s1[...] = dp_grad[pl.ds(0, PAIR)].astype(BF16)
                self.proj_one.start()

        def rows_two(self):
            layer = self.layer
            half, quarter = lift // 2, lift // 4
            base = PAIR + me[D2] * half
            self.down_one.wait()
            at = (1 - me[D1]) * quarter
            down_s2[...] = (
                dp_grad[pl.ds(base + at, quarter)]
                + down_r1[layer, pl.ds(at, quarter)].astype(F32)
            ).astype(BF16)
            self.down_two.start()

            @pl.when(others)
            def _():
                self.proj_one.wait_send()

            @pl.when(mine)
            def _():
                self.proj_one.wait_recv()
                at = (1 - me[D1]) * HEAD_DIM
                proj_s2[...] = (
                    dp_grad[pl.ds(at, HEAD_DIM)]
                    + proj_r1[layer, pl.ds(at, HEAD_DIM)].astype(F32)
                ).astype(BF16)
                self.proj_two.start()

        def rows_three(self):
            layer = self.layer
            half, quarter = lift // 2, lift // 4
            base = PAIR + me[D2] * half
            self.down_two.wait()
            at = me[D1] * quarter
            down_out[layer] = (
                dp_grad[pl.ds(base + at, quarter)]
                + down_r1[layer, pl.ds(at, quarter)].astype(F32)
                + down_r2[layer].astype(F32)
            )
            count = proj.shape[1]

            @pl.when(mine)
            def _():
                self.proj_two.wait()
                at = me[D1] * HEAD_DIM

                def half_of(which):
                    return (
                        dp_grad[pl.ds(at + which * count, count)]
                        + proj_r1[layer, pl.ds(at + which * count, count)].astype(F32)
                        + proj_r2[layer, pl.ds(which * count, count)].astype(F32)
                    )

                proj_out[layer] = half_of(me["c"])
                proj_s3[...] = half_of(1 - me["c"]).astype(BF16)
                self.proj_three.start()
                self.proj_three.wait_send()

            @pl.when(others)
            def _():
                self.proj_three.wait_recv()
                proj_out[layer] = proj_r3[layer].astype(F32)

        def cat_terms(self, i):
            layer = self.layer
            zh = me["zh"] if i else 1 - me["zh"]
            deltas = mdud[...].reshape(8 * rows, wide)
            for zl in range(2):
                start = pl.multiple_of((zh * 2 + zl) * (width // 4), width // 4)
                kept = hid[layer, :, :, :, pl.ds(start, width // 4)].reshape(8 * rows, width // 4)
                scratch[0, : width // 4, :wide] = dot(kept, deltas, ((0,), (0,)))
                size = width // 8
                cat_s1[i, zl] = scratch[0, pl.ds((1 - me["x"]) * size, size), :wide].astype(BF16)
                self.cat_one[i][zl].start()
                cat_own[i, zl] = scratch[0, pl.ds(me["x"] * size, size), :wide]

        def cat_step_two(self, zl):
            layer = self.layer
            self.cat_one[0][zl].wait()
            cat_s2[zl] = (cat_own[0, zl] + cat_r1[layer, 0, zl].astype(F32)).astype(BF16)
            self.cat_two[zl].start()

        def cat_step_three(self, zl):
            layer = self.layer
            self.cat_one[1][zl].wait()
            self.cat_two[zl].wait()
            total = (
                cat_own[1, zl]
                + cat_r1[layer, 1, zl].astype(F32)
                + cat_r2[layer, zl].astype(F32)
            )
            cat_a[zl] = total.astype(BF16).reshape(cat_a.shape[1:])

        def cat_trade(self):
            for copy in self.trades:
                copy.start()
            self.keep.start()

        def cat_done(self):
            for copy in self.trades:
                copy.wait()
            self.keep.wait()

    def put_sums(layer, index, value):
        grad_sum[layer, 0, pl.ds(index, 1), : value.shape[1]] = value

    def own_rows(layer, total, stream_at, up_at, put):
        gain = bias_row(layer, 0)
        gain_sum = jnp.zeros((1, width), F32)
        shift_sum = jnp.zeros((1, width), F32)
        for m in range(2 * micros):
            at = pl.ds(m * (rows // (2 * micros)), rows // (2 * micros))
            delta = total(at)
            normed, inverse = normalise(stream_at(at))
            gain_sum = gain_sum + jnp.sum(delta * normed, axis=0, keepdims=True)
            shift_sum = shift_sum + jnp.sum(delta, axis=0, keepdims=True)
            scaled = delta * gain
            put(
                at,
                up_at(at) + inverse * (scaled - mean_of(scaled) - normed * mean_of(scaled * normed)),
            )
        put_sums(layer, RANKS + 0, gain_sum)
        put_sums(layer, RANKS + 1, shift_sum)

    def bias_sums(layer):
        put_sums(layer, rank, jnp.sum(sums[...], axis=0, keepdims=True))
        rounded = jnp.zeros((8, width), F32)
        for m in range(2 * micros):
            size = rows // (2 * micros)
            part = rnd[0, 0, pl.ds(m * size, size)].astype(F32)
            rounded = rounded + jnp.sum(part.reshape(size // 8, 8, width), axis=0)
        put_sums(layer, RANKS + 2, jnp.sum(rounded, axis=0, keepdims=True))

    def give_back(turn_index):
        for axes in (("c",), (T1,), (T2,)):
            pl.semaphore_signal(
                free_sem.at[turn_index], inc=1, device_id=links.peer(axes), device_id_type=MESH
            )

    def await_places(turn_index):
        pl.semaphore_wait(free_sem.at[turn_index], 3)

    taken = [Weights(layer) for layer in range(layers)]
    grads = [Grads(layer) for layer in range(layers)]
    row_gathers = [Rows(links, hid.at[1]), Rows(links, mask_all), Rows(links, rnd)]
    hidden_two, rounded_one = Rows(links, hid.at[1]), Rows(links, rnd)
    sets = (core_in, chip_in, core_out, chip_out)
    out_one, delta_two, delta_one = Sums(links, *sets), Sums(links, *sets), Sums(links, *sets)
    spare = hid.at[1]
    out_two = Sums(links, core_in, spare.at[0:3, 0], core_out, spare.at[0:3, 1], True)
    small_copies = []
    for i, axis in enumerate(SMALL_AXES):
        tiles = small_all.at[pl.ds(own_tile // 2**i * 2**i, 2**i)]
        small_copies.append(links.copy(tiles, tiles, (axis,)))
    grad_copies = [
        [
            links.copy(grad_sum.at[layer, i], grad_in.at[layer, i], (axis,))
            for i, axis in enumerate(GRAD_AXES)
        ]
        for layer in range(layers)
    ]

    def grad_step(layer, i):
        grad_copies[layer][i].wait()
        grad_sum[layer, i + 1] = grad_sum[layer, i] + grad_in[layer, i]
        if i + 1 < len(SMALL_AXES):
            grad_copies[layer][i + 1].start()
        else:
            own_small(layer)

    chain = [taken[0].down[0]] + taken[0].cat + [taken[0].down[1], taken[0].heads]
    chain = chain + taken[1].cat + taken[1].down + [taken[1].heads]

    def pump(k):
        chain[k].step()
        for piece in chain[max(ahead(k - 1), 2) : ahead(k)]:
            piece.start()
        chain[k].start_far()

    def ahead(k):
        return min(k + 3 if k < 5 else k + 5, len(chain))

    def small_step(i):
        small_copies[i].wait()
        if i + 1 < len(SMALL_AXES):
            small_copies[i + 1].start()
        else:
            expand_small()

    fetched = fetch_columns()
    for copy in fetched:
        copy.start()
    for one in taken:
        one.keep[1].start()
    small_all[own_tile] = small[...]
    links.meet()
    small_copies[0].start()
    chain[0].start()
    for copy in fetched[:pieces]:
        copy.wait()
    columns_by_rank(0)
    taken[0].start_trades()
    for piece in taken[0].down:
        piece.start_near()
    hid[1, 0, 0] = inputs[...]
    for m in range(micros):
        build_mask(m)
    taken[0].heads.prepare()
    taken[1].heads.prepare()
    for layer in range(layers):
        grad_sum[layer, 0] = jnp.zeros_like(grad_sum[layer, 0])
    small_step(0)
    taken[0].traded()
    chain[1].start()
    row_gathers[1].start()
    row_gathers[0].start()
    for piece in taken[0].cat:
        piece.start_near()
    small_step(1)
    pump(0)
    small_step(2)
    row_gathers[1].forward()
    for copy in fetched[pieces:]:
        copy.wait()
    columns_by_rank(1)
    small_step(3)
    pump(1)
    small_step(4)
    row_gathers[0].forward()
    taken[1].start_trades()

    gain, shift = bias_row(0, 0), bias_row(0, 1)

    def first_norm(j, carry):
        row_gathers[0].arrive(j)
        row_gathers[1].arrive(j)

        def each(p, carry):
            size = rows // 4
            at = pl.ds(pl.multiple_of((p % 4) * size, size), size)
            normed, _ = normalise(hid[1, j, p // 4, at].astype(F32))
            hid[0, j, p // 4, at] = (normed * gain + shift).astype(BF16)
            return carry

        lax.fori_loop(0, 8, each, 0)
        for k in range(3):

            @pl.when(j == k)
            def _():
                pump(2 + k)

        return carry

    lax.fori_loop(0, 4, first_norm, 0)
    row_gathers[0].finish()
    row_gathers[1].finish()
    row_gathers[2].start()
    taken[1].traded()
    pump(5)
    for piece in taken[1].cat + taken[1].down:
        piece.start_near()
    taken[0].cat_done()

    def first(i, j):
        forward(0, j)

        @pl.when(i == 0)
        def _():
            pump(6)
            taken[0].rows_done()
            row_gathers[2].forward()

        for k in range(1, 4):

            @pl.when(i == k)
            def _():
                pump(6 + k)

    out_one.run(first, out_term(0), scratch, own, far_first)()
    pump(10)

    def rest_of_rounded(j, carry):
        row_gathers[2].arrive(j)
        return carry

    lax.fori_loop(0, 4, rest_of_rounded, 0)
    row_gathers[2].finish()
    total = out_one.total(own)
    out_bias = bias_row(0, 2)
    gain, shift = bias_row(1, 0), bias_row(1, 1)
    for m in range(4):
        at = pl.ds(m * (rows // 4), rows // 4)
        stream = inputs[at].astype(F32) + total(at) + out_bias
        stream_two[at] = stream
        normed, _ = normalise(stream)
        hid[1, 0, 0, at] = (normed * gain + shift).astype(BF16)
    hidden_two.start()
    pump(11)
    taken[1].cat_done()

    def second(j, carry):
        hidden_two.arrive(j)
        forward(1, j)

        @pl.when(j == 0)
        def _():
            hidden_two.forward()
            pump(12)
            pump(13)

        return carry

    lax.fori_loop(0, 4, second, 0)
    hidden_two.finish()
    taken[1].rows_done()

    sums[...] = jnp.zeros_like(sums)

    delta_two.run(lambda i, j: backward(1, j), hidden_term(1), scratch, own, far_first)()
    grads[1].cat_terms(0)
    grads[1].cat_terms(1)
    grads[1].rows_terms(0, 4)
    bias_sums(1)
    give_back(2)
    grads[1].rows_one()
    total = delta_two.total(own)
    await_places(2)

    def put_one(at, value):
        up_one[at] = value
        rnd[0, 0, at] = value.astype(BF16)

    own_rows(1, total, lambda at: stream_two[at], lambda at: rnd[0, 0, at].astype(F32), put_one)
    rounded_one.start()
    grad_copies[1][0].start()
    sums[...] = jnp.zeros_like(sums)
    out_two.run(lambda i, j: None, out_term(1), scratch, own, far_first, True)()
    for m in range(4):
        at = pl.ds(m * (rows // 4), rows // 4)
        stream_two[at] = stream_two[at] + own[at] + bias_row(1, 2)
    give_back(0)
    rounded_one.forward()
    out_two.release()
    for j in range(4):
        out_two.core(j).wait_send()
    await_places(0)

    def third(i, j):
        for k in range(4):

            @pl.when(i == k)
            def _():
                grad_step(1, k)

        @pl.when(i == 1)
        def _():
            for zl in range(2):
                grads[1].cat_step_two(zl)

        @pl.when(i == 2)
        def _():
            rounded_one.arrive(1)

        @pl.when(i < 3)
        def _():
            rounded_one.arrive(j)

        @pl.when(i == 2)
        def _():
            rounded_one.finish()

        @pl.when(i == 3)
        def _():
            grads[1].rows_two()

        backward(0, j)

    last = delta_one.run(third, hidden_term(0), scratch, own, near_first)
    for zl in range(2):
        grads[1].cat_step_three(zl)
    grads[0].cat_terms(0)
    grads[1].cat_trade()
    grads[0].cat_terms(1)
    grads[1].rows_three()
    grads[0].rows_terms(0, 4)
    grads[0].rows_one()
    out_two.relay()
    bias_sums(0)
    grad_step(1, 4)
    last()
    for zl in range(2):
        grads[0].cat_step_two(zl)
    grads[1].cat_done()
    returned = return_columns(1) + return_columns(0)
    columns_by_name(1)
    for copy in returned[:pieces]:
        copy.start()
    total = delta_one.total(own)

    def put_last(at, value):
        input_grad[at] = value

    own_rows(0, total, lambda at: inputs[at].astype(F32), lambda at: up_one[at], put_last)
    grad_copies[0][0].start()
    total = out_two.total(stream_two, True)
    for m in range(4):
        at = pl.ds(m * (rows // 4), rows // 4)
        outputs[at] = total(at).astype(BF16)
    grad_step(0, 0)
    for zl in range(2):
        grads[0].cat_step_three(zl)
    grads[0].cat_trade()
    grad_step(0, 1)
    grad_step(0, 2)
    grads[0].rows_two()
    grad_step(0, 3)
    grads[0].cat_done()
    columns_by_name(0)
    for copy in returned[pieces:]:
        copy.start()
    grad_step(0, 4)
    grads[0].rows_three()
    for copy in returned:
        copy.wait()


def run_layers(qkv, up, down, proj, inputs, cotangent, marks, small, tables):
    layers, count = qkv.shape[:2]
    rows, width = inputs.shape
    micros, lanes = marks.shape
    pack = rows // micros
    lift = up.shape[2] // RANKS
    wide = QKV + lift
    vmem = pl.BlockSpec(memory_space=pltpu.VMEM)
    anywhere = pl.BlockSpec(memory_space=pltpu.HBM)
    shape = jax.ShapeDtypeStruct
    stages = len(SMALL_AXES)
    copies = 256
    cat_size = width // 8
    buffers = [
        ((layers, RANKS, count, wide), BF16),
        ((layers, 32, count, wide), BF16),
        ((layers, PAIR + lift, width), BF16),
        ((layers, 4, 2, rows, width), BF16),
        ((4, 2, rows, width), BF16),
        ((4, 2, micros, pack, lanes), BF16),
        ((layers, 4, 2 * rows, QKV), BF16),
        ((layers, 4, 2 * micros, 2 * pack, pack), BF16),
        ((layers, 4, 2 * rows, PAIR + lift), BF16),
        ((layers, 4, 2 * rows, lift), BF16),
        ((4, 2 * rows, wide), BF16),
        ((2, 2 * rows, width), F32),
        ((4, rows, width), BF16),
        ((3, rows, width), BF16),
        ((4, rows, width), BF16),
        ((3, rows, width), BF16),
        ((rows, width), F32),
        ((rows, width), F32),
        ((rows, width), F32),
        ((32,) + small.shape, F32),
        ((3, 8, width), F32),
        ((8, wide), F32),
        ((8, wide), F32),
        ((layers, stages + 1, 2 * RANKS, width), F32),
        ((layers, stages, 2 * RANKS, width), F32),
        ((2, 2, cat_size, wide), F32),
        ((2, 2, cat_size, wide), BF16),
        ((layers, 2, 2, cat_size, wide), BF16),
        ((2, cat_size, wide), BF16),
        ((layers, 2, cat_size, wide), BF16),
        ((2, 4, count, wide), BF16),
        ((PAIR + lift, width), F32),
        ((lift // 2, width), BF16),
        ((layers, lift // 2, width), BF16),
        ((lift // 4, width), BF16),
        ((layers, lift // 4, width), BF16),
        ((PAIR, width), BF16),
        ((layers, PAIR, width), BF16),
        ((HEAD_DIM, width), BF16),
        ((layers, HEAD_DIM, width), BF16),
        ((HEAD_DIM // 2, width), BF16),
        ((layers, HEAD_DIM // 2, width), BF16),
    ]
    return pl.pallas_call(
        layers_kernel,
        out_shape=(
            shape((rows, width), BF16),
            shape((rows, width), F32),
            shape((layers, width // 32), F32),
            shape((layers, width // 32), F32),
            shape(qkv.shape, F32),
            shape((layers, 2 * width // 32), F32),
            shape(proj.shape, F32),
            shape((layers, width // 32), F32),
            shape(up.shape, F32),
            shape((layers, up.shape[2] // 32), F32),
            shape(down.shape, F32),
        ),
        in_specs=[anywhere] * 4 + [vmem] * 5,
        out_specs=(vmem,) * 4 + (anywhere,) + (vmem,) * 3 + (anywhere,) + (vmem,) * 2,
        scratch_shapes=[pltpu.VMEM(dims, kind) for dims, kind in buffers]
        + [
            pltpu.SemaphoreType.DMA((copies,)),
            pltpu.SemaphoreType.DMA((copies,)),
            pltpu.SemaphoreType.DMA((layers, 4)),
            pltpu.SemaphoreType.REGULAR((3,)),
            pltpu.SemaphoreType.DMA((layers * 7,)),
        ],
        compiler_params=pltpu.CompilerParams(
            collective_id=0, has_side_effects=True, vmem_limit_bytes=63 << 20
        ),
    )(qkv, up, down, proj, inputs, cotangent, marks, small, tables)


def refold(block, extra):
    if extra == 1:
        return block
    whole = lax.all_gather(block, AXES, axis=1, tiled=True)
    rows = whole.shape[1] // 32
    return lax.dynamic_slice_in_dim(whole, lax.axis_index(AXES[1:]) * rows, rows, 1)


def unfold(block, extra):
    if extra == 1:
        return block
    rows = block.shape[1]
    whole = jnp.zeros((block.shape[0], 32 * rows) + block.shape[2:], F32)
    whole = lax.dynamic_update_slice_in_dim(whole, block, lax.axis_index(AXES[1:]) * rows, 1)
    return lax.psum_scatter(whole, AXES, scatter_dimension=1, tiled=True)


def rope_tables(pack):
    half = ROT // 2
    angle = np.arange(pack, dtype=np.float32)[:, None] * (
        np.float32(10000.0) ** (-np.arange(0, ROT, 2, dtype=np.float32) / np.float32(ROT))
    )
    angle = angle.astype(np.float32)
    tables = np.zeros((3, pack, 2, HEAD_DIM), np.float32)
    tables[0] = 1.0
    tables[0, :, :, :half] = tables[0, :, :, half:ROT] = np.cos(angle)[:, None]
    tables[1, :, :, :half] = -np.sin(angle)[:, None]
    tables[2, :, :, half:ROT] = np.sin(angle)[:, None]
    return tables.reshape(3, pack, PAIR)


def shards(
    inputs,
    cotangent,
    segments,
    pack_length,
    norm_gain,
    norm_shift,
    qkv_weight,
    qv_bias,
    proj_weight,
    proj_bias,
    up_weight,
    up_bias,
    down_weight,
    down_bias,
):
    micros, pack, width = inputs.shape
    layers = qkv_weight.shape[0]
    extra = lax.axis_size("e")
    marks = jnp.concatenate([segments, pack_length], axis=1).astype(F32)
    marks = jnp.pad(marks, ((0, 0), (0, -(pack + 1) % 128)))

    def wide(value):
        return jnp.pad(value.astype(F32), ((0, 0), (0, PAIR - value.shape[1])))

    biases = refold(proj_bias, extra).astype(F32) + refold(down_bias, extra).astype(F32)
    three = [refold(norm_gain, extra).astype(F32), refold(norm_shift, extra).astype(F32), biases]
    small = [
        wide(jnp.concatenate(three, axis=1)),
        wide(refold(qv_bias, extra).reshape(1, -1)),
        wide(refold(up_bias, extra)),
    ]
    small = jnp.concatenate(small)
    small = jnp.pad(small, ((0, -small.shape[0] % 8), (0, 0)))
    given = run_layers(
        refold(qkv_weight, extra),
        refold(up_weight, extra),
        refold(down_weight, extra),
        refold(proj_weight, extra),
        inputs.reshape(micros * pack, width),
        cotangent.reshape(micros * pack, width),
        marks,
        small,
        jnp.asarray(rope_tables(pack)),
    )
    out, input_grad = given[:2]
    gain, shift, qkv, qvb, proj, bias, up, upb, down = [unfold(g, extra) for g in given[2:]]
    return (
        out.reshape(micros, pack, width),
        input_grad.reshape(micros, pack, width),
        gain,
        shift,
        qkv,
        qvb,
        proj,
        bias,
        up,
        upb,
        down,
        bias,
    )


def solution(mesh):
    devices = mesh.devices.size
    fine = Mesh(mesh.devices.reshape(devices // 32, 2, 2, 2, 2, 2), AXES)
    cube, flat = P(None, AXES, None), P(None, AXES)
    placed = (cube, cube, flat, flat, flat, flat, cube, flat, cube, flat, cube, flat, cube, flat)
    given = (cube, cube, flat, flat, cube, flat, cube, flat, cube, flat, cube, flat)
    return jax.shard_map(shards, mesh=fine, in_specs=placed, out_specs=given, check_vma=False)
```

```python
import math

import jax
import jax.numpy as jnp
import numpy as np
from jax import lax
from jax.experimental import pallas as pl
from jax.experimental.pallas import tpu as pltpu
from jax.sharding import Mesh
from jax.sharding import PartitionSpec as P

HEAD_DIM = 64
ROT = 16
EPS = 1e-05
MASKED = -1e30

AXES = ("e", "zh", "zl", "x", "y", "c")
T1, T2, D1, D2 = "y", "zl", "zh", "x"
TP = (T1, T2, "c")
RANKS = 8
NEAR = (("c",), (T1,), (T2,), (T1, "c"), (T2, "c"), (T1, T2), (T1, T2, "c"))
FAR = ((D1,), (D2,))
SMALL_AXES = ("zh", "x", "zl", "y", "c")
GRAD_AXES = ("c", T1, T2, D1, D2)

F32, BF16 = jnp.float32, jnp.bfloat16
MESH = pl.DeviceIdType.MESH

PAIR = 2 * HEAD_DIM
QKV = 3 * PAIR


def dot(a, b, contract):
    return lax.dot_general(a, b, (contract, ((), ())), preferred_element_type=F32)


class Links:
    def __init__(self, send_sem, recv_sem):
        self.place = {axis: lax.axis_index(axis) for axis in AXES}
        self.send_sem, self.recv_sem, self.used = send_sem, recv_sem, 0

    def reserve(self, count):
        self.used += count
        return self.used - count

    def peer(self, axes):
        return {axis: 1 - self.place[axis] for axis in axes}

    def meet(self):
        barrier = pltpu.get_barrier_semaphore()
        for axes in NEAR + FAR:
            pl.semaphore_signal(barrier, inc=1, device_id=self.peer(axes), device_id_type=MESH)
        pl.semaphore_wait(barrier, len(NEAR) + len(FAR))

    def copy(self, source, target, device, slot=None):
        if slot is None:
            slot = self.reserve(1)
        if not isinstance(device, dict):
            device = self.peer(device)
        return pltpu.make_async_remote_copy(
            src_ref=source,
            dst_ref=target,
            send_sem=self.send_sem.at[slot],
            recv_sem=self.recv_sem.at[slot],
            device_id=device,
            device_id_type=MESH,
        )


def rank_of(place):
    return place[T1] * 4 + place[T2] * 2 + place["c"]


def block_of(place):
    index = place["zh"]
    for axis in AXES[2:]:
        index = index * 2 + place[axis]
    return index


def flipped(place, axes):
    return {a: (1 - i if a in axes else i) for a, i in place.items()}


class Rows:
    def __init__(self, links, buffer):
        self.links, self.buffer, self.base = links, buffer, links.reserve(9)
        self.near = [
            None,
            links.copy(buffer.at[0, 0], buffer.at[1, 0], (T2,), self.base + 5),
            links.copy(buffer.at[0, 0], buffer.at[2, 0], (T1,), self.base + 6),
        ]
        self.far = [
            links.copy(buffer.at[1, 0], buffer.at[3, 0], (T1,), self.base + 7),
        ]

    def core(self, j):
        return self.links.copy(
            self.buffer.at[j, 0], self.buffer.at[j, 1], ("c",), self.base + j
        )

    def start(self):
        self.core(0).start()
        self.near[1].start()
        self.near[2].start()

    def forward(self):
        self.near[1].wait_recv()
        self.far[0].start()
        self.core(1).start()
        self.near[2].wait_recv()
        self.core(2).start()

    def arrive(self, j):
        @pl.when(j == 3)
        def _():
            self.far[0].wait_recv()
            self.core(3).start()

        self.core(j).wait_recv()

    def finish(self):
        for j in range(4):
            self.core(j).wait_send()
        for copy in self.near[1:] + self.far:
            copy.wait_send()


def far_first(i):
    return 3 - i


def near_first(i):
    return i + 1 - 3 * (i // 3) - (3 - i) // 3


class Sums:
    def __init__(self, links, core_in, chip_in, core_out, chip_out, turned=False):
        self.links, self.base = links, links.reserve(8)
        self.relayed, self.far_axis = (2, T2) if turned else (1, T1)
        self.core_in, self.chip_in, self.core_out, self.chip_out = core_in, chip_in, core_out, chip_out

    def core(self, j):
        return self.links.copy(
            self.core_out.at[j], self.core_in.at[j], ("c",), self.base + j
        )

    def chip(self, j):
        return self.links.copy(
            self.chip_out.at[j - 1],
            self.chip_in.at[j - 1],
            ((T2,), (T1,), (self.far_axis,))[j - 1],
            self.base + 4 + j,
        )

    def run(self, before, term, scratch, own, order, hold=False):
        rows = own.shape[0]

        def pass_on(j):
            self.core(j).wait_recv()
            for m in range(2):
                at = pl.ds(m * (rows // 2), rows // 2)
                total = scratch[1, at] + self.core_in[j, at].astype(F32)
                for k in (1, 2, 3):

                    @pl.when(j == k)
                    def _():
                        value = total
                        if k == self.relayed and not hold:
                            if m == 0:
                                self.chip(3).wait_recv()
                            value = value + self.chip_in[2, at].astype(F32)
                        self.chip_out[k - 1, at] = value.astype(BF16)
                        if m == 1 and not hold:
                            self.chip(k).start()

                @pl.when(j == 0)
                def _():
                    own[at] = total

        def step(i, carry):
            j = order(i)
            before(i, j)

            @pl.when(i > 0)
            def _():
                pass_on(order(i - 1))

            term(j, scratch.at[1])
            self.core_out[j] = scratch[1, rows:].astype(BF16)
            self.core(j).start()
            return carry

        lax.fori_loop(0, 4, step, 0)
        return lambda: pass_on(order(3))

    def release(self):
        self.chip(3).start()
        self.chip(3 - self.relayed).start()

    def relay(self):
        self.chip(3).wait_recv()
        rows, place = self.chip_out.shape[1], self.relayed - 1
        for m in range(4):
            at = pl.ds(m * (rows // 4), rows // 4)
            value = self.chip_out[place, at].astype(F32) + self.chip_in[2, at].astype(F32)
            self.chip_out[place, at] = value.astype(BF16)
        self.chip(self.relayed).start()

    def total(self, own, held=False):
        for j in (1, 2):
            self.chip(j).wait_recv()
        if not held:
            for j in range(4):
                self.core(j).wait_send()
        for j in (1, 2, 3):
            self.chip(j).wait_send()

        def at(rows):
            value = own[rows]
            for j in (1, 2):
                value = value + self.chip_in[j - 1, rows].astype(F32)
            return value

        return at


def mean_of(value):
    return jnp.sum(value, axis=-1, keepdims=True) * (1.0 / value.shape[-1])


def normalise(stream):
    centred = stream - mean_of(stream)
    inverse = lax.rsqrt(mean_of(centred * centred) + EPS)
    return centred * inverse, inverse


def layers_kernel(
    qkv,
    up,
    down,
    proj,
    inputs,
    cotangent,
    marks,
    small,
    tables,
    outputs,
    input_grad,
    gain_out,
    shift_out,
    qkv_out,
    qvb_out,
    proj_out,
    bias_out,
    up_out,
    upb_out,
    down_out,
    parts,
    cat_all,
    dp_all,
    hid,
    rnd,
    mask_all,
    qkv_kept,
    probs,
    ca,
    slope,
    mdud,
    scratch,
    core_in,
    chip_in,
    core_out,
    chip_out,
    own,
    stream_two,
    up_one,
    small_all,
    named,
    rank_bias,
    sums,
    grad_sum,
    grad_in,
    cat_own,
    cat_s1,
    cat_r1,
    cat_s2,
    cat_r2,
    cat_a,
    dp_grad,
    down_s1,
    down_r1,
    down_s2,
    down_r2,
    proj_s1,
    proj_r1,
    proj_s2,
    proj_r2,
    proj_s3,
    proj_r3,
    send_sem,
    recv_sem,
    own_sem,
    free_sem,
    fetch_sem,
):
    links = Links(send_sem, recv_sem)
    me = links.place
    rank, block, slot = rank_of(me), block_of(me), me[D2] * 2 + me[D1]
    mine = me["c"] == me[D2]
    others = jnp.logical_not(mine)
    layers, wide = parts.shape[0], parts.shape[3]
    micros, lanes = marks.shape
    rows, width = inputs.shape
    pack = rows // micros
    count = qkv.shape[1]
    lift = wide - QKV
    scale = 1.0 / math.sqrt(HEAD_DIM)
    lane = lax.broadcasted_iota(jnp.int32, (pack, PAIR), 1)
    first_head = lane < HEAD_DIM

    def bias_row(layer, kind):
        return named[kind, layer : layer + 1, :]

    pieces = 3 + up.shape[2] // width
    raw = [core_out.at[i // 6, pl.ds(i % 6 * count, count)] for i in range(layers * pieces)]
    final = [scratch.at[i // 8, pl.ds(i % 8 * count, count)] for i in range(layers * pieces)]

    def fetch_columns():
        copies = []
        for i in range(layers * pieces):
            layer, k = i // pieces, i % pieces
            source = qkv.at[layer, :, pl.ds(k * width, width)] if k < 3 else up.at[
                layer, :, pl.ds((k - 3) * width, width)
            ]
            copies.append(pltpu.make_async_copy(source, raw[i], fetch_sem.at[i]))
        return copies

    def return_columns(layer):
        copies = []
        for k in range(pieces):
            i = layer * pieces + k
            target = qkv_out.at[layer, :, pl.ds(k * width, width)] if k < 3 else up_out.at[
                layer, :, pl.ds((k - 3) * width, width)
            ]
            copies.append(pltpu.make_async_copy(final[i], target, fetch_sem.at[i]))
        return copies

    lane_row = lax.broadcasted_iota(jnp.int32, (count, PAIR), 1) < HEAD_DIM

    def shared(one, other):
        one, other = one.astype(F32), other.astype(F32)
        return (
            jnp.where(lane_row, one, pltpu.roll(other, HEAD_DIM, 1)),
            jnp.where(lane_row, pltpu.roll(one, HEAD_DIM, 1), other),
        )

    def columns_by_rank(layer):
        base = layer * pieces
        for p in range(3):
            for zl in range(2):
                for x in range(2):
                    tiles = [
                        raw[base + p][:, (zh * 4 + zl * 2 + x) * PAIR : (zh * 4 + zl * 2 + x + 1) * PAIR]
                        for zh in range(2)
                    ]
                    for y, tile in enumerate(shared(*tiles)):
                        parts[layer, y * 4 + zl * 2 + x, :, p * PAIR : (p + 1) * PAIR] = tile.astype(BF16)
        size = up.shape[2] // 32
        for b in range(32):
            zh, zl, x, y, c = b // 16, b // 8 % 2, b // 4 % 2, b // 2 % 2, b % 2
            k, at = b * size // width, b * size % width
            to = QKV + (x * 2 + zh) * size
            parts[layer, y * 4 + zl * 2 + c, :, to : to + size] = raw[base + 3 + k][:, at : at + size]

    def columns_by_name(layer):
        base = layer * pieces
        for p in range(3):
            for zl in range(2):
                for x in range(2):
                    tiles = [
                        parts[layer, y * 4 + zl * 2 + x, :, p * PAIR : (p + 1) * PAIR] for y in range(2)
                    ]
                    for zh, tile in enumerate(shared(*tiles)):
                        at = (zh * 4 + zl * 2 + x) * PAIR
                        final[base + p][:, at : at + PAIR] = tile
        size = up.shape[2] // 32
        for b in range(32):
            zh, zl, x, y, c = b // 16, b // 8 % 2, b // 4 % 2, b // 2 % 2, b % 2
            k, at = b * size // width, b * size % width
            to = QKV + (x * 2 + zh) * size
            tile = parts[layer, y * 4 + zl * 2 + c, :, to : to + size]
            final[base + 3 + k][:, at : at + size] = tile.astype(F32)

    head_rank = me["c"] * 4 + me["x"] * 2 + me["y"]
    head_cut = pl.ds(pl.multiple_of(me["zh"] * 2 * PAIR, PAIR), PAIR)
    up_size = up.shape[2] // 32
    up_cut = pl.ds(pl.multiple_of(QKV + slot * up_size, PAIR), up_size)

    rank_row = lax.broadcasted_iota(jnp.int32, (RANKS, PAIR), 0)
    own_tile = me["c"] * 16 + me["y"] * 8 + me["zl"] * 4 + me["x"] * 2 + me["zh"]

    def expand_small():
        share = width // 32
        lanes_of = lax.broadcasted_iota(jnp.int32, (8, PAIR), 1) // share
        for group in range(8):
            zh, zl, x = group // 4, group // 2 % 2, group % 2
            tiles = [small_all[c * 16 + y * 8 + zl * 4 + x * 2 + zh] for y in range(2) for c in range(2)]
            for kind in range(3):
                value = jnp.zeros((8, PAIR), F32)
                for r, tile in enumerate(tiles):
                    moved = (r - kind) % 4 * share
                    tile = pltpu.roll(tile, moved, 1) if moved else tile
                    value = jnp.where(lanes_of == r, tile, value)
                named[kind, :, group * PAIR : (group + 1) * PAIR] = value
        rank_bias[...] = jnp.zeros_like(rank_bias)
        here = lax.broadcasted_iota(jnp.int32, (8, PAIR), 1) < HEAD_DIM
        for layer in range(layers):
            at = slice(layer, layer + 1)
            for part in range(2):
                heads = []
                for zh in range(2):
                    tile = small_all[
                        me["y"] * 16 + me["c"] * 8 + zh * 4 + me["zl"] * 2 + part, layers : layers + 1, :
                    ]
                    tile = jnp.broadcast_to(tile, (8, PAIR))
                    heads.append(tile if zh == layer else pltpu.roll(tile, HEAD_DIM, 1))
                cut = slice(2 * part * PAIR, (2 * part + 1) * PAIR)
                rank_bias[at, cut] = jnp.where(here, heads[0], heads[1])[:1]
            for x in range(2):
                for zh in range(2):
                    tile = me["c"] * 16 + me["y"] * 8 + me["zl"] * 4 + x * 2 + zh
                    to = QKV + (x * 2 + zh) * up_size
                    line = layers + 1 + layer
                    rank_bias[at, to : to + up_size] = small_all[tile, line : line + 1, :]

    def own_small(layer):
        share = width // 32
        total = grad_sum.at[layer, len(SMALL_AXES)]
        moved = pltpu.roll(total[RANKS:], (32 - block) % 32 * share, 1)
        at = slice(layer, layer + 1)
        gain_out[at] = moved[0:1, :share]
        shift_out[at] = moved[1:2, :share]
        bias_out[at] = moved[2:3, :share]
        pair = pltpu.roll(total[:RANKS, head_cut], me["zl"] * HEAD_DIM, 1)
        pair = jnp.where(rank_row == head_rank, pair, 0.0)
        qvb_out[at] = jnp.sum(pair, axis=0, keepdims=True)[:, :HEAD_DIM]
        more = jnp.where(rank_row == rank, total[:RANKS, up_cut], 0.0)
        upb_out[at] = jnp.sum(more, axis=0, keepdims=True)

    def build_mask(m):
        row = lax.broadcasted_iota(jnp.int32, (lanes, lanes), 0)
        column = lax.broadcasted_iota(jnp.int32, (lanes, lanes), 1)
        across = jnp.broadcast_to(marks[pl.ds(m, 1), :], (lanes, lanes))
        length = marks[pl.ds(m, 1), pack : pack + 1]
        live = column.astype(F32) < length
        allowed = (across.T == across) & (column <= row) & (live | (column == row))
        hidden = jnp.where(allowed, 0.0, MASKED).astype(BF16)
        mask_all[0, 0, m] = hidden[:pack]
        live = lax.broadcasted_iota(jnp.int32, (pack, 1), 0).astype(F32) < length
        at = pl.ds(m * pack, pack)
        rnd[0, 0, at] = jnp.where(live, cotangent[at].astype(F32), 0.0).astype(BF16)

    class Piece:
        def __init__(self, own, at):
            here, there = at(me["zh"]), at(1 - me["zh"])
            self.one = links.copy(here if own is None else own, here, (D1,))
            self.near = links.copy(here if own is None else own, here, (D2,))
            self.far = links.copy(there, there, (D2,))

        def start(self):
            self.one.start()

        def start_near(self):
            self.near.start()

        def step(self):
            self.one.wait()

        def start_far(self):
            self.far.start()

        def done(self):
            self.near.wait()
            self.far.wait()

    class Heads:
        def __init__(self, layer):
            self.layer = layer
            count = proj.shape[1]
            half = dp_all.at[layer, pl.ds(me["zh"] * HEAD_DIM + me["c"] * count, count)]
            self.to_core = links.copy(proj.at[layer], half, ("c",))
            self.stays = pltpu.make_async_copy(proj.at[layer], half, own_sem.at[layer, 2])
            head = dp_all.at[layer, pl.ds(me["zh"] * HEAD_DIM, HEAD_DIM)]
            self.one = links.copy(head, head, (D1,))
            heads = dp_all.at[layer, pl.ds(0, PAIR)]
            self.two = links.copy(heads, heads, (D2,))

        def prepare(self):
            @pl.when(mine)
            def _():
                self.stays.start()
                self.stays.wait()

            @pl.when(others)
            def _():
                self.to_core.start()
                self.to_core.wait_send()

        def start(self):
            @pl.when(mine)
            def _():
                self.to_core.wait_recv()
                self.one.start()

        def step(self):
            @pl.when(mine)
            def _():
                self.one.wait()

        def start_far(self):
            @pl.when(mine)
            def _():
                self.two.start()

        def done(self):
            @pl.when(mine)
            def _():
                self.two.wait_send()

            @pl.when(others)
            def _():
                self.two.wait_recv()

    class Weights:
        def __init__(self, layer):
            self.layer = layer
            size = down.shape[1]
            self.keep = [
                pltpu.make_async_copy(
                    parts.at[layer, rank], cat_all.at[layer, block], own_sem.at[layer, 0]
                ),
                pltpu.make_async_copy(
                    down.at[layer], self.down_rows(me["zh"], 0, size), own_sem.at[layer, 1]
                ),
            ]
            self.trades = [
                links.copy(
                    parts.at[layer, rank_of(flipped(me, axes))], cat_all.at[layer, block], axes
                )
                for axes in NEAR
            ]
            self.cat = [
                Piece(None, lambda zh, zl=zl, h=h: self.cat_rows(zh, zl, h))
                for zl in range(2)
                for h in range(2)
            ]
            half = size // 2
            self.down = [
                Piece(
                    down.at[layer, pl.ds(h * half, half)],
                    lambda zh, h=h: self.down_rows(zh, h * half, half),
                )
                for h in range(2)
            ]
            self.heads = Heads(layer)

        def cat_rows(self, zh, zl, h):
            return cat_all.at[self.layer, pl.ds(zh * 16 + zl * 8 + me["x"] * 4 + 2 * h, 2)]

        def down_rows(self, zh, start, count):
            size = down.shape[1]
            return dp_all.at[
                self.layer, pl.ds(PAIR + (me[D2] * 2 + zh) * size + start, count)
            ]

        def start_trades(self):
            self.keep[0].start()
            for copy in self.trades:
                copy.start()

        def traded(self):
            self.keep[0].wait()
            for copy in self.trades:
                copy.wait()

        def cat_done(self):
            for piece in self.cat:
                piece.done()

        def rows_done(self):
            self.keep[1].wait()
            for piece in self.down:
                piece.done()
            self.heads.done()

    def turn(value, sign):
        return (
            value * tables[0]
            + pltpu.roll(value, PAIR - ROT // 2, 1) * (tables[1] * sign)
            + pltpu.roll(value, ROT // 2, 1) * (tables[2] * sign)
        )

    def by_head(value):
        zero = jnp.zeros_like(value)
        return jnp.concatenate(
            [jnp.where(first_head, value, zero), jnp.where(first_head, zero, value)], axis=0
        )

    def of_heads(value):
        return jnp.where(first_head, value[:pack], value[pack:])

    def forward(layer, j):
        hidden = hid[layer, j].reshape(2 * rows, width)
        for cut in (slice(0, QKV), slice(QKV, wide)):
            columns = cat_all[layer, :, :, cut].reshape(width, -1)
            scratch[0, :, cut] = dot(hidden, columns, ((1,), (0,)))
        bias = rank_bias[layer : layer + 1, :]

        def each(p, carry):
            at = pl.ds(pl.multiple_of(p * pack, pack), pack)
            turned = scratch[0, at, :QKV] + bias[:, :QKV]
            queries = turn(turned[:, :PAIR], 1.0).astype(BF16)
            keys = turn(turned[:, PAIR : 2 * PAIR], 1.0).astype(BF16)
            values = turned[:, 2 * PAIR :].astype(BF16)
            qkv_kept[layer, j, at, :PAIR] = queries
            qkv_kept[layer, j, at, PAIR : 2 * PAIR] = keys
            qkv_kept[layer, j, at, 2 * PAIR :] = values
            hide = mask_all[j, p // micros, p % micros][:, :pack].astype(F32)
            scores = dot(by_head(queries), keys, ((1,), (1,))) * scale
            scores = scores + jnp.concatenate([hide, hide], axis=0)
            shifted = jnp.exp(scores - jnp.max(scores, axis=-1, keepdims=True))
            soft = shifted / jnp.sum(shifted, axis=-1, keepdims=True)
            soft = soft.astype(BF16)
            probs[layer, j, p] = soft
            ca[layer, j, at, :PAIR] = of_heads(dot(soft, values, ((1,), (0,)))).astype(BF16)
            for start in range(QKV, wide, 2 * PAIR):
                cut = slice(start, start + 2 * PAIR)
                raised = scratch[0, at, cut] + bias[:, cut]
                cdf = 0.5 * (1.0 + lax.erf(raised * 0.7071067811865476))
                density = jnp.exp(-0.5 * raised * raised) * 0.3989422804014327
                to = start - QKV
                ca[layer, j, at, PAIR + to : PAIR + to + 2 * PAIR] = (raised * cdf).astype(BF16)
                slope[layer, j, at, to : to + 2 * PAIR] = (cdf + raised * density).astype(BF16)
            return carry

        lax.fori_loop(0, 2 * micros, each, 0, unroll=4)

    def backward(layer, j):
        rounded = rnd[j].reshape(2 * rows, width)
        for cut in (slice(0, PAIR), slice(PAIR, PAIR + lift)):
            scratch[0, :, cut] = dot(rounded, dp_all[layer, cut], ((1,), (1,)))

        def each(p, carry):
            at = pl.ds(pl.multiple_of(p * pack, pack), pack)
            for start in range(0, lift, 2 * PAIR):
                cut = slice(start, start + 2 * PAIR)
                grown = scratch[0, at, PAIR + start : 3 * PAIR + start]
                grown = (grown * slope[layer, j, at, cut].astype(F32)).astype(BF16)
                mdud[j, at, QKV + start : QKV + start + 2 * PAIR] = grown
                sums[:, QKV + start : QKV + start + 2 * PAIR] += jnp.sum(
                    grown.astype(F32).reshape(pack // 8, 8, 2 * PAIR), axis=0
                )
            context = by_head(scratch[0, at, :PAIR].astype(BF16))
            queries = by_head(qkv_kept[layer, j, at, :PAIR])
            keys = qkv_kept[layer, j, at, PAIR : 2 * PAIR]
            values = qkv_kept[layer, j, at, 2 * PAIR :]
            kept = probs[layer, j, p]
            soft = kept.astype(F32)
            prob_delta = dot(context, values, ((1,), (1,)))
            row_delta = jnp.sum(soft * prob_delta, axis=-1, keepdims=True)
            score_delta = (soft * (prob_delta - row_delta)).astype(BF16)
            value_delta = dot(kept, context, ((0,), (0,)))
            query_delta = of_heads(dot(score_delta, keys, ((1,), (0,)))) * scale
            key_delta = dot(score_delta, queries, ((0,), (0,))) * scale
            three = (turn(query_delta, -1.0), turn(key_delta, -1.0), value_delta)
            for i, delta in enumerate(three):
                delta = delta.astype(BF16)
                cut = slice(i * PAIR, (i + 1) * PAIR)
                mdud[j, at, cut] = delta
                sums[:, cut] += jnp.sum(delta.astype(F32).reshape(pack // 8, 8, PAIR), axis=0)
            return carry

        lax.fori_loop(0, 2 * micros, each, 0, unroll=4)

    halves = (slice(0, width // 2), slice(width // 2, width))

    def out_term(layer):
        def put(j, target):
            for cut in halves:
                target[:, cut] = dot(ca[layer, j], dp_all[layer, :, cut], ((1,), (0,)))

        return put

    def hidden_term(layer):
        def put(j, target):
            for half, cut in enumerate(halves):
                columns = cat_all[layer, pl.ds(16 * half, 16)].reshape(width // 2, wide)
                target[:, cut] = dot(mdud[j], columns, ((1,), (1,)))

        return put

    class Grads:
        def __init__(self, layer):
            self.layer = layer
            self.down_one = links.copy(down_s1, down_r1.at[layer], (D2,))
            self.down_two = links.copy(down_s2, down_r2.at[layer], (D1,))
            self.proj_one = links.copy(proj_s1, proj_r1.at[layer], (D2,))
            self.proj_two = links.copy(proj_s2, proj_r2.at[layer], (D1,))
            self.proj_three = links.copy(proj_s3, proj_r3.at[layer], ("c",))
            self.cat_one = [
                [links.copy(cat_s1.at[i, zl], cat_r1.at[layer, i, zl], (D2,)) for zl in range(2)]
                for i in range(2)
            ]
            self.cat_two = [
                links.copy(cat_s2.at[zl], cat_r2.at[layer, zl], (D1,)) for zl in range(2)
            ]
            self.trades = []
            for axes in NEAR:
                there = flipped(me, axes)
                part = cat_a.at[there["zl"], there["y"] * 2 + there["c"]]
                self.trades.append(links.copy(part, parts.at[layer, rank], axes))
            self.keep = pltpu.make_async_copy(
                cat_a.at[me["zl"], me["y"] * 2 + me["c"]], parts.at[layer, rank], own_sem.at[layer, 3]
            )

        def rows_terms(self, start, stop):
            layer = self.layer
            size = (stop - start) * 2 * rows
            kept = ca[layer, start:stop].reshape(size, PAIR + lift)
            for cut in halves:
                rounded = rnd[start:stop, :, :, cut].reshape(size, width // 2)
                for part in (pl.ds(PAIR, lift), pl.ds(0, PAIR)):
                    side = kept[:, PAIR:] if part.start else kept[:, :PAIR]
                    value = dot(side, rounded, ((0,), (0,)))
                    if start:
                        value = value + dp_grad[part, cut]
                    dp_grad[part, cut] = value

        def rows_one(self):
            half = lift // 2
            down_s1[...] = dp_grad[pl.ds(PAIR + (1 - me[D2]) * half, half)].astype(BF16)
            self.down_one.start()

            @pl.when(others)
            def _():
                proj_s1[...] = dp_grad[pl.ds(0, PAIR)].astype(BF16)
                self.proj_one.start()

        def rows_two(self):
            layer = self.layer
            half, quarter = lift // 2, lift // 4
            base = PAIR + me[D2] * half
            self.down_one.wait()
            at = (1 - me[D1]) * quarter
            down_s2[...] = (
                dp_grad[pl.ds(base + at, quarter)]
                + down_r1[layer, pl.ds(at, quarter)].astype(F32)
            ).astype(BF16)
            self.down_two.start()

            @pl.when(others)
            def _():
                self.proj_one.wait_send()

            @pl.when(mine)
            def _():
                self.proj_one.wait_recv()
                at = (1 - me[D1]) * HEAD_DIM
                proj_s2[...] = (
                    dp_grad[pl.ds(at, HEAD_DIM)]
                    + proj_r1[layer, pl.ds(at, HEAD_DIM)].astype(F32)
                ).astype(BF16)
                self.proj_two.start()

        def rows_three(self):
            layer = self.layer
            half, quarter = lift // 2, lift // 4
            base = PAIR + me[D2] * half
            self.down_two.wait()
            at = me[D1] * quarter
            down_out[layer] = (
                dp_grad[pl.ds(base + at, quarter)]
                + down_r1[layer, pl.ds(at, quarter)].astype(F32)
                + down_r2[layer].astype(F32)
            )
            count = proj.shape[1]

            @pl.when(mine)
            def _():
                self.proj_two.wait()
                at = me[D1] * HEAD_DIM

                def half_of(which):
                    return (
                        dp_grad[pl.ds(at + which * count, count)]
                        + proj_r1[layer, pl.ds(at + which * count, count)].astype(F32)
                        + proj_r2[layer, pl.ds(which * count, count)].astype(F32)
                    )

                proj_out[layer] = half_of(me["c"])
                proj_s3[...] = half_of(1 - me["c"]).astype(BF16)
                self.proj_three.start()
                self.proj_three.wait_send()

            @pl.when(others)
            def _():
                self.proj_three.wait_recv()
                proj_out[layer] = proj_r3[layer].astype(F32)

        def cat_terms(self, i):
            layer = self.layer
            zh = me["zh"] if i else 1 - me["zh"]
            deltas = mdud[...].reshape(8 * rows, wide)
            for zl in range(2):
                start = pl.multiple_of((zh * 2 + zl) * (width // 4), width // 4)
                kept = hid[layer, :, :, :, pl.ds(start, width // 4)].reshape(8 * rows, width // 4)
                scratch[0, : width // 4, :wide] = dot(kept, deltas, ((0,), (0,)))
                size = width // 8
                cat_s1[i, zl] = scratch[0, pl.ds((1 - me["x"]) * size, size), :wide].astype(BF16)
                self.cat_one[i][zl].start()
                cat_own[i, zl] = scratch[0, pl.ds(me["x"] * size, size), :wide]

        def cat_step_two(self, zl):
            layer = self.layer
            self.cat_one[0][zl].wait()
            cat_s2[zl] = (cat_own[0, zl] + cat_r1[layer, 0, zl].astype(F32)).astype(BF16)
            self.cat_two[zl].start()

        def cat_step_three(self, zl):
            layer = self.layer
            self.cat_one[1][zl].wait()
            self.cat_two[zl].wait()
            total = (
                cat_own[1, zl]
                + cat_r1[layer, 1, zl].astype(F32)
                + cat_r2[layer, zl].astype(F32)
            )
            cat_a[zl] = total.astype(BF16).reshape(cat_a.shape[1:])

        def cat_trade(self):
            for copy in self.trades:
                copy.start()
            self.keep.start()

        def cat_done(self):
            for copy in self.trades:
                copy.wait()
            self.keep.wait()

    def put_sums(layer, index, value):
        grad_sum[layer, 0, pl.ds(index, 1), : value.shape[1]] = value

    def own_rows(layer, total, stream_at, up_at, put):
        gain = bias_row(layer, 0)
        gain_sum = jnp.zeros((1, width), F32)
        shift_sum = jnp.zeros((1, width), F32)
        for m in range(2 * micros):
            at = pl.ds(m * (rows // (2 * micros)), rows // (2 * micros))
            delta = total(at)
            normed, inverse = normalise(stream_at(at))
            gain_sum = gain_sum + jnp.sum(delta * normed, axis=0, keepdims=True)
            shift_sum = shift_sum + jnp.sum(delta, axis=0, keepdims=True)
            scaled = delta * gain
            put(
                at,
                up_at(at) + inverse * (scaled - mean_of(scaled) - normed * mean_of(scaled * normed)),
            )
        put_sums(layer, RANKS + 0, gain_sum)
        put_sums(layer, RANKS + 1, shift_sum)

    def bias_sums(layer):
        put_sums(layer, rank, jnp.sum(sums[...], axis=0, keepdims=True))
        rounded = jnp.zeros((8, width), F32)
        for m in range(2 * micros):
            size = rows // (2 * micros)
            part = rnd[0, 0, pl.ds(m * size, size)].astype(F32)
            rounded = rounded + jnp.sum(part.reshape(size // 8, 8, width), axis=0)
        put_sums(layer, RANKS + 2, jnp.sum(rounded, axis=0, keepdims=True))

    def give_back(turn_index):
        for axes in (("c",), (T1,), (T2,)):
            pl.semaphore_signal(
                free_sem.at[turn_index], inc=1, device_id=links.peer(axes), device_id_type=MESH
            )

    def await_places(turn_index):
        pl.semaphore_wait(free_sem.at[turn_index], 3)

    taken = [Weights(layer) for layer in range(layers)]
    grads = [Grads(layer) for layer in range(layers)]
    row_gathers = [Rows(links, hid.at[1]), Rows(links, mask_all), Rows(links, rnd)]
    hidden_two, rounded_one = Rows(links, hid.at[1]), Rows(links, rnd)
    sets = (core_in, chip_in, core_out, chip_out)
    out_one, delta_two, delta_one = Sums(links, *sets), Sums(links, *sets), Sums(links, *sets)
    spare = hid.at[1]
    out_two = Sums(links, core_in, spare.at[0:3, 0], core_out, spare.at[0:3, 1], True)
    small_copies = []
    for i, axis in enumerate(SMALL_AXES):
        tiles = small_all.at[pl.ds(own_tile // 2**i * 2**i, 2**i)]
        small_copies.append(links.copy(tiles, tiles, (axis,)))
    grad_copies = [
        [
            links.copy(grad_sum.at[layer, i], grad_in.at[layer, i], (axis,))
            for i, axis in enumerate(GRAD_AXES)
        ]
        for layer in range(layers)
    ]

    def grad_step(layer, i):
        grad_copies[layer][i].wait()
        grad_sum[layer, i + 1] = grad_sum[layer, i] + grad_in[layer, i]
        if i + 1 < len(SMALL_AXES):
            grad_copies[layer][i + 1].start()
        else:
            own_small(layer)

    chain = [taken[0].down[0]] + taken[0].cat + [taken[0].down[1], taken[0].heads]
    chain = chain + taken[1].cat + taken[1].down + [taken[1].heads]

    def pump(k):
        chain[k].step()
        for piece in chain[max(ahead(k - 1), 2) : ahead(k)]:
            piece.start()
        chain[k].start_far()

    def ahead(k):
        return min(k + 3 if k < 5 else k + 5, len(chain))

    def small_step(i):
        small_copies[i].wait()
        if i + 1 < len(SMALL_AXES):
            small_copies[i + 1].start()
        else:
            expand_small()

    fetched = fetch_columns()
    for copy in fetched:
        copy.start()
    for one in taken:
        one.keep[1].start()
    small_all[own_tile] = small[...]
    links.meet()
    small_copies[0].start()
    chain[0].start()
    for copy in fetched[:pieces]:
        copy.wait()
    columns_by_rank(0)
    taken[0].start_trades()
    for piece in taken[0].down:
        piece.start_near()
    hid[1, 0, 0] = inputs[...]
    for m in range(micros):
        build_mask(m)
    taken[0].heads.prepare()
    taken[1].heads.prepare()
    for layer in range(layers):
        grad_sum[layer, 0] = jnp.zeros_like(grad_sum[layer, 0])
    small_step(0)
    taken[0].traded()
    chain[1].start()
    row_gathers[1].start()
    row_gathers[0].start()
    for piece in taken[0].cat:
        piece.start_near()
    small_step(1)
    pump(0)
    small_step(2)
    row_gathers[1].forward()
    for copy in fetched[pieces:]:
        copy.wait()
    columns_by_rank(1)
    small_step(3)
    pump(1)
    small_step(4)
    row_gathers[0].forward()
    taken[1].start_trades()

    gain, shift = bias_row(0, 0), bias_row(0, 1)

    def first_norm(j, carry):
        row_gathers[0].arrive(j)
        row_gathers[1].arrive(j)

        def each(p, carry):
            size = rows // 4
            at = pl.ds(pl.multiple_of((p % 4) * size, size), size)
            normed, _ = normalise(hid[1, j, p // 4, at].astype(F32))
            hid[0, j, p // 4, at] = (normed * gain + shift).astype(BF16)
            return carry

        lax.fori_loop(0, 8, each, 0)
        for k in range(3):

            @pl.when(j == k)
            def _():
                pump(2 + k)

        return carry

    lax.fori_loop(0, 4, first_norm, 0)
    row_gathers[0].finish()
    row_gathers[1].finish()
    row_gathers[2].start()
    taken[1].traded()
    pump(5)
    for piece in taken[1].cat + taken[1].down:
        piece.start_near()
    taken[0].cat_done()

    def first(i, j):
        forward(0, j)

        @pl.when(i == 0)
        def _():
            pump(6)
            taken[0].rows_done()
            row_gathers[2].forward()

        for k in range(1, 4):

            @pl.when(i == k)
            def _():
                pump(6 + k)

    out_one.run(first, out_term(0), scratch, own, far_first)()
    pump(10)

    def rest_of_rounded(j, carry):
        row_gathers[2].arrive(j)
        return carry

    lax.fori_loop(0, 4, rest_of_rounded, 0)
    row_gathers[2].finish()
    total = out_one.total(own)
    out_bias = bias_row(0, 2)
    gain, shift = bias_row(1, 0), bias_row(1, 1)
    for m in range(4):
        at = pl.ds(m * (rows // 4), rows // 4)
        stream = inputs[at].astype(F32) + total(at) + out_bias
        stream_two[at] = stream
        normed, _ = normalise(stream)
        hid[1, 0, 0, at] = (normed * gain + shift).astype(BF16)
    hidden_two.start()
    pump(11)
    taken[1].cat_done()

    def second(j, carry):
        hidden_two.arrive(j)
        forward(1, j)

        @pl.when(j == 0)
        def _():
            hidden_two.forward()
            pump(12)
            pump(13)

        return carry

    lax.fori_loop(0, 4, second, 0)
    hidden_two.finish()
    taken[1].rows_done()

    sums[...] = jnp.zeros_like(sums)

    delta_two.run(lambda i, j: backward(1, j), hidden_term(1), scratch, own, far_first)()
    grads[1].cat_terms(0)
    grads[1].cat_terms(1)
    grads[1].rows_terms(0, 4)
    bias_sums(1)
    give_back(2)
    grads[1].rows_one()
    total = delta_two.total(own)
    await_places(2)

    def put_one(at, value):
        up_one[at] = value
        rnd[0, 0, at] = value.astype(BF16)

    own_rows(1, total, lambda at: stream_two[at], lambda at: rnd[0, 0, at].astype(F32), put_one)
    rounded_one.start()
    grad_copies[1][0].start()
    sums[...] = jnp.zeros_like(sums)
    out_two.run(lambda i, j: None, out_term(1), scratch, own, far_first, True)()
    for m in range(4):
        at = pl.ds(m * (rows // 4), rows // 4)
        stream_two[at] = stream_two[at] + own[at] + bias_row(1, 2)
    give_back(0)
    rounded_one.forward()
    out_two.release()
    for j in range(4):
        out_two.core(j).wait_send()
    await_places(0)

    def third(i, j):
        for k in range(4):

            @pl.when(i == k)
            def _():
                grad_step(1, k)

        @pl.when(i == 1)
        def _():
            for zl in range(2):
                grads[1].cat_step_two(zl)

        @pl.when(i == 2)
        def _():
            rounded_one.arrive(1)

        @pl.when(i < 3)
        def _():
            rounded_one.arrive(j)

        @pl.when(i == 2)
        def _():
            rounded_one.finish()

        @pl.when(i == 3)
        def _():
            grads[1].rows_two()

        backward(0, j)

    last = delta_one.run(third, hidden_term(0), scratch, own, near_first)
    for zl in range(2):
        grads[1].cat_step_three(zl)
    grads[0].cat_terms(0)
    grads[1].cat_trade()
    grads[0].cat_terms(1)
    grads[1].rows_three()
    grads[0].rows_terms(0, 4)
    grads[0].rows_one()
    out_two.relay()
    bias_sums(0)
    grad_step(1, 4)
    last()
    for zl in range(2):
        grads[0].cat_step_two(zl)
    grads[1].cat_done()
    returned = return_columns(1) + return_columns(0)
    columns_by_name(1)
    for copy in returned[:pieces]:
        copy.start()
    total = delta_one.total(own)

    def put_last(at, value):
        input_grad[at] = value

    own_rows(0, total, lambda at: inputs[at].astype(F32), lambda at: up_one[at], put_last)
    grad_copies[0][0].start()
    for i in range(len(GRAD_AXES)):
        grad_step(0, i)
    total = out_two.total(stream_two, True)
    for m in range(4):
        at = pl.ds(m * (rows // 4), rows // 4)
        outputs[at] = total(at).astype(BF16)
    for zl in range(2):
        grads[0].cat_step_three(zl)
    grads[0].cat_trade()
    grads[0].rows_two()
    grads[0].cat_done()
    columns_by_name(0)
    for copy in returned[pieces:]:
        copy.start()
    grads[0].rows_three()
    for copy in returned:
        copy.wait()


def run_layers(qkv, up, down, proj, inputs, cotangent, marks, small, tables):
    layers, count = qkv.shape[:2]
    rows, width = inputs.shape
    micros, lanes = marks.shape
    pack = rows // micros
    lift = up.shape[2] // RANKS
    wide = QKV + lift
    vmem = pl.BlockSpec(memory_space=pltpu.VMEM)
    anywhere = pl.BlockSpec(memory_space=pltpu.HBM)
    shape = jax.ShapeDtypeStruct
    stages = len(SMALL_AXES)
    copies = 256
    cat_size = width // 8
    buffers = [
        ((layers, RANKS, count, wide), BF16),
        ((layers, 32, count, wide), BF16),
        ((layers, PAIR + lift, width), BF16),
        ((layers, 4, 2, rows, width), BF16),
        ((4, 2, rows, width), BF16),
        ((4, 2, micros, pack, lanes), BF16),
        ((layers, 4, 2 * rows, QKV), BF16),
        ((layers, 4, 2 * micros, 2 * pack, pack), BF16),
        ((layers, 4, 2 * rows, PAIR + lift), BF16),
        ((layers, 4, 2 * rows, lift), BF16),
        ((4, 2 * rows, wide), BF16),
        ((2, 2 * rows, width), F32),
        ((4, rows, width), BF16),
        ((3, rows, width), BF16),
        ((4, rows, width), BF16),
        ((3, rows, width), BF16),
        ((rows, width), F32),
        ((rows, width), F32),
        ((rows, width), F32),
        ((32,) + small.shape, F32),
        ((3, 8, width), F32),
        ((8, wide), F32),
        ((8, wide), F32),
        ((layers, stages + 1, 2 * RANKS, width), F32),
        ((layers, stages, 2 * RANKS, width), F32),
        ((2, 2, cat_size, wide), F32),
        ((2, 2, cat_size, wide), BF16),
        ((layers, 2, 2, cat_size, wide), BF16),
        ((2, cat_size, wide), BF16),
        ((layers, 2, cat_size, wide), BF16),
        ((2, 4, count, wide), BF16),
        ((PAIR + lift, width), F32),
        ((lift // 2, width), BF16),
        ((layers, lift // 2, width), BF16),
        ((lift // 4, width), BF16),
        ((layers, lift // 4, width), BF16),
        ((PAIR, width), BF16),
        ((layers, PAIR, width), BF16),
        ((HEAD_DIM, width), BF16),
        ((layers, HEAD_DIM, width), BF16),
        ((HEAD_DIM // 2, width), BF16),
        ((layers, HEAD_DIM // 2, width), BF16),
    ]
    return pl.pallas_call(
        layers_kernel,
        out_shape=(
            shape((rows, width), BF16),
            shape((rows, width), F32),
            shape((layers, width // 32), F32),
            shape((layers, width // 32), F32),
            shape(qkv.shape, F32),
            shape((layers, 2 * width // 32), F32),
            shape(proj.shape, F32),
            shape((layers, width // 32), F32),
            shape(up.shape, F32),
            shape((layers, up.shape[2] // 32), F32),
            shape(down.shape, F32),
        ),
        in_specs=[anywhere] * 4 + [vmem] * 5,
        out_specs=(vmem,) * 4 + (anywhere,) + (vmem,) * 3 + (anywhere,) + (vmem,) * 2,
        scratch_shapes=[pltpu.VMEM(dims, kind) for dims, kind in buffers]
        + [
            pltpu.SemaphoreType.DMA((copies,)),
            pltpu.SemaphoreType.DMA((copies,)),
            pltpu.SemaphoreType.DMA((layers, 4)),
            pltpu.SemaphoreType.REGULAR((3,)),
            pltpu.SemaphoreType.DMA((layers * 7,)),
        ],
        compiler_params=pltpu.CompilerParams(
            collective_id=0, has_side_effects=True, vmem_limit_bytes=63 << 20
        ),
    )(qkv, up, down, proj, inputs, cotangent, marks, small, tables)


def refold(block, extra):
    if extra == 1:
        return block
    whole = lax.all_gather(block, AXES, axis=1, tiled=True)
    rows = whole.shape[1] // 32
    return lax.dynamic_slice_in_dim(whole, lax.axis_index(AXES[1:]) * rows, rows, 1)


def unfold(block, extra):
    if extra == 1:
        return block
    rows = block.shape[1]
    whole = jnp.zeros((block.shape[0], 32 * rows) + block.shape[2:], F32)
    whole = lax.dynamic_update_slice_in_dim(whole, block, lax.axis_index(AXES[1:]) * rows, 1)
    return lax.psum_scatter(whole, AXES, scatter_dimension=1, tiled=True)


def rope_tables(pack):
    half = ROT // 2
    angle = np.arange(pack, dtype=np.float32)[:, None] * (
        np.float32(10000.0) ** (-np.arange(0, ROT, 2, dtype=np.float32) / np.float32(ROT))
    )
    angle = angle.astype(np.float32)
    tables = np.zeros((3, pack, 2, HEAD_DIM), np.float32)
    tables[0] = 1.0
    tables[0, :, :, :half] = tables[0, :, :, half:ROT] = np.cos(angle)[:, None]
    tables[1, :, :, :half] = -np.sin(angle)[:, None]
    tables[2, :, :, half:ROT] = np.sin(angle)[:, None]
    return tables.reshape(3, pack, PAIR)


def shards(
    inputs,
    cotangent,
    segments,
    pack_length,
    norm_gain,
    norm_shift,
    qkv_weight,
    qv_bias,
    proj_weight,
    proj_bias,
    up_weight,
    up_bias,
    down_weight,
    down_bias,
):
    micros, pack, width = inputs.shape
    layers = qkv_weight.shape[0]
    extra = lax.axis_size("e")
    marks = jnp.concatenate([segments, pack_length], axis=1).astype(F32)
    marks = jnp.pad(marks, ((0, 0), (0, -(pack + 1) % 128)))

    def wide(value):
        return jnp.pad(value.astype(F32), ((0, 0), (0, PAIR - value.shape[1])))

    biases = refold(proj_bias, extra).astype(F32) + refold(down_bias, extra).astype(F32)
    three = [refold(norm_gain, extra).astype(F32), refold(norm_shift, extra).astype(F32), biases]
    small = [
        wide(jnp.concatenate(three, axis=1)),
        wide(refold(qv_bias, extra).reshape(1, -1)),
        wide(refold(up_bias, extra)),
    ]
    small = jnp.concatenate(small)
    small = jnp.pad(small, ((0, -small.shape[0] % 8), (0, 0)))
    given = run_layers(
        refold(qkv_weight, extra),
        refold(up_weight, extra),
        refold(down_weight, extra),
        refold(proj_weight, extra),
        inputs.reshape(micros * pack, width),
        cotangent.reshape(micros * pack, width),
        marks,
        small,
        jnp.asarray(rope_tables(pack)),
    )
    out, input_grad = given[:2]
    gain, shift, qkv, qvb, proj, bias, up, upb, down = [unfold(g, extra) for g in given[2:]]
    return (
        out.reshape(micros, pack, width),
        input_grad.reshape(micros, pack, width),
        gain,
        shift,
        qkv,
        qvb,
        proj,
        bias,
        up,
        upb,
        down,
        bias,
    )


def solution(mesh):
    devices = mesh.devices.size
    fine = Mesh(mesh.devices.reshape(devices // 32, 2, 2, 2, 2, 2), AXES)
    cube, flat = P(None, AXES, None), P(None, AXES)
    placed = (cube, cube, flat, flat, flat, flat, cube, flat, cube, flat, cube, flat, cube, flat)
    given = (cube, cube, flat, flat, cube, flat, cube, flat, cube, flat, cube, flat)
    return jax.shard_map(shards, mesh=fine, in_specs=placed, out_specs=given, check_vma=False)
```

```python
import math

import jax
import jax.numpy as jnp
import numpy as np
from jax import lax
from jax.experimental import pallas as pl
from jax.experimental.pallas import tpu as pltpu
from jax.sharding import Mesh
from jax.sharding import PartitionSpec as P

HEAD_DIM = 64
ROT = 16
EPS = 1e-05
MASKED = -1e30

AXES = ("e", "zh", "zl", "x", "y", "c")
T1, T2, D1, D2 = "y", "zl", "zh", "x"
TP = (T1, T2, "c")
RANKS = 8
NEAR = (("c",), (T1,), (T2,), (T1, "c"), (T2, "c"), (T1, T2), (T1, T2, "c"))
FAR = ((D1,), (D2,))
SMALL_AXES = ("zh", "x", "zl", "y", "c")
GRAD_AXES = ("c", T1, T2, D1, D2)

F32, BF16 = jnp.float32, jnp.bfloat16
MESH = pl.DeviceIdType.MESH

PAIR = 2 * HEAD_DIM
QKV = 3 * PAIR


def dot(a, b, contract):
    return lax.dot_general(a, b, (contract, ((), ())), preferred_element_type=F32)


class Links:
    def __init__(self, send_sem, recv_sem):
        self.place = {axis: lax.axis_index(axis) for axis in AXES}
        self.send_sem, self.recv_sem, self.used = send_sem, recv_sem, 0

    def reserve(self, count):
        self.used += count
        return self.used - count

    def peer(self, axes):
        return {axis: 1 - self.place[axis] for axis in axes}

    def meet(self):
        barrier = pltpu.get_barrier_semaphore()
        for axes in NEAR + FAR:
            pl.semaphore_signal(barrier, inc=1, device_id=self.peer(axes), device_id_type=MESH)
        pl.semaphore_wait(barrier, len(NEAR) + len(FAR))

    def copy(self, source, target, device, slot=None):
        if slot is None:
            slot = self.reserve(1)
        if not isinstance(device, dict):
            device = self.peer(device)
        return pltpu.make_async_remote_copy(
            src_ref=source,
            dst_ref=target,
            send_sem=self.send_sem.at[slot],
            recv_sem=self.recv_sem.at[slot],
            device_id=device,
            device_id_type=MESH,
        )


def rank_of(place):
    return place[T1] * 4 + place[T2] * 2 + place["c"]


def block_of(place):
    index = place["zh"]
    for axis in AXES[2:]:
        index = index * 2 + place[axis]
    return index


def flipped(place, axes):
    return {a: (1 - i if a in axes else i) for a, i in place.items()}


class Rows:
    def __init__(self, links, buffer):
        self.links, self.buffer, self.base = links, buffer, links.reserve(9)
        self.near = [
            None,
            links.copy(buffer.at[0, 0], buffer.at[1, 0], (T2,), self.base + 5),
            links.copy(buffer.at[0, 0], buffer.at[2, 0], (T1,), self.base + 6),
        ]
        self.far = [
            links.copy(buffer.at[1, 0], buffer.at[3, 0], (T1,), self.base + 7),
        ]

    def core(self, j):
        return self.links.copy(
            self.buffer.at[j, 0], self.buffer.at[j, 1], ("c",), self.base + j
        )

    def start(self):
        self.core(0).start()
        self.near[1].start()
        self.near[2].start()

    def forward(self):
        self.near[1].wait_recv()
        self.far[0].start()
        self.core(1).start()
        self.near[2].wait_recv()
        self.core(2).start()

    def arrive(self, j):
        @pl.when(j == 3)
        def _():
            self.far[0].wait_recv()
            self.core(3).start()

        self.core(j).wait_recv()

    def finish(self):
        for j in range(4):
            self.core(j).wait_send()
        for copy in self.near[1:] + self.far:
            copy.wait_send()


def far_first(i):
    return 3 - i


def near_first(i):
    return i + 1 - 3 * (i // 3) - (3 - i) // 3


class Sums:
    def __init__(self, links, core_in, chip_in, core_out, chip_out, turned=False):
        self.links, self.base = links, links.reserve(8)
        self.relayed, self.far_axis = (2, T2) if turned else (1, T1)
        self.core_in, self.chip_in, self.core_out, self.chip_out = core_in, chip_in, core_out, chip_out

    def core(self, j):
        return self.links.copy(
            self.core_out.at[j], self.core_in.at[j], ("c",), self.base + j
        )

    def chip(self, j):
        return self.links.copy(
            self.chip_out.at[j - 1],
            self.chip_in.at[j - 1],
            ((T2,), (T1,), (self.far_axis,))[j - 1],
            self.base + 4 + j,
        )

    def run(self, before, term, scratch, own, order, hold=False):
        rows = own.shape[0]

        def pass_on(j):
            self.core(j).wait_recv()
            for m in range(2):
                at = pl.ds(m * (rows // 2), rows // 2)
                total = scratch[1, at] + self.core_in[j, at].astype(F32)
                for k in (1, 2, 3):

                    @pl.when(j == k)
                    def _():
                        value = total
                        if k == self.relayed and not hold:
                            if m == 0:
                                self.chip(3).wait_recv()
                            value = value + self.chip_in[2, at].astype(F32)
                        self.chip_out[k - 1, at] = value.astype(BF16)
                        if m == 1 and not hold:
                            self.chip(k).start()

                @pl.when(j == 0)
                def _():
                    own[at] = total

        def step(i, carry):
            j = order(i)
            before(i, j)

            @pl.when(i > 0)
            def _():
                pass_on(order(i - 1))

            term(j, scratch.at[1])
            self.core_out[j] = scratch[1, rows:].astype(BF16)
            self.core(j).start()
            return carry

        lax.fori_loop(0, 4, step, 0)
        return lambda: pass_on(order(3))

    def release(self):
        self.chip(3).start()
        self.chip(3 - self.relayed).start()

    def relay(self):
        self.chip(3).wait_recv()
        rows, place = self.chip_out.shape[1], self.relayed - 1
        for m in range(4):
            at = pl.ds(m * (rows // 4), rows // 4)
            value = self.chip_out[place, at].astype(F32) + self.chip_in[2, at].astype(F32)
            self.chip_out[place, at] = value.astype(BF16)
        self.chip(self.relayed).start()

    def total(self, own, held=False):
        for j in (1, 2):
            self.chip(j).wait_recv()
        if not held:
            for j in range(4):
                self.core(j).wait_send()
        for j in (1, 2, 3):
            self.chip(j).wait_send()

        def at(rows):
            value = own[rows]
            for j in (1, 2):
                value = value + self.chip_in[j - 1, rows].astype(F32)
            return value

        return at


def mean_of(value):
    return jnp.sum(value, axis=-1, keepdims=True) * (1.0 / value.shape[-1])


def normalise(stream):
    centred = stream - mean_of(stream)
    inverse = lax.rsqrt(mean_of(centred * centred) + EPS)
    return centred * inverse, inverse


def layers_kernel(
    qkv,
    up,
    down,
    proj,
    inputs,
    cotangent,
    marks,
    small,
    tables,
    outputs,
    input_grad,
    gain_out,
    shift_out,
    qkv_out,
    qvb_out,
    proj_out,
    bias_out,
    up_out,
    upb_out,
    down_out,
    parts,
    cat_all,
    dp_all,
    hid,
    rnd,
    mask_all,
    qkv_kept,
    probs,
    ca,
    slope,
    mdud,
    scratch,
    core_in,
    chip_in,
    core_out,
    chip_out,
    own,
    stream_two,
    up_one,
    small_all,
    named,
    rank_bias,
    sums,
    grad_sum,
    grad_in,
    cat_own,
    cat_s1,
    cat_r1,
    cat_s2,
    cat_r2,
    cat_a,
    dp_grad,
    down_s1,
    down_r1,
    down_s2,
    down_r2,
    proj_s1,
    proj_r1,
    proj_s2,
    proj_r2,
    proj_s3,
    proj_r3,
    send_sem,
    recv_sem,
    own_sem,
    free_sem,
    fetch_sem,
):
    links = Links(send_sem, recv_sem)
    me = links.place
    rank, block, slot = rank_of(me), block_of(me), me[D2] * 2 + me[D1]
    mine = me["c"] == me[D2]
    others = jnp.logical_not(mine)
    layers, wide = parts.shape[0], parts.shape[3]
    micros, lanes = marks.shape
    rows, width = inputs.shape
    pack = rows // micros
    count = qkv.shape[1]
    lift = wide - QKV
    scale = 1.0 / math.sqrt(HEAD_DIM)
    lane = lax.broadcasted_iota(jnp.int32, (pack, PAIR), 1)
    first_head = lane < HEAD_DIM

    def bias_row(layer, kind):
        return named[kind, layer : layer + 1, :]

    pieces = 3 + up.shape[2] // width
    raw = [core_out.at[i // 6, pl.ds(i % 6 * count, count)] for i in range(layers * pieces)]
    final = [scratch.at[i // 8, pl.ds(i % 8 * count, count)] for i in range(layers * pieces)]

    def fetch_columns():
        copies = []
        for i in range(layers * pieces):
            layer, k = i // pieces, i % pieces
            source = qkv.at[layer, :, pl.ds(k * width, width)] if k < 3 else up.at[
                layer, :, pl.ds((k - 3) * width, width)
            ]
            copies.append(pltpu.make_async_copy(source, raw[i], fetch_sem.at[i]))
        return copies

    def return_columns(layer):
        copies = []
        for k in range(pieces):
            i = layer * pieces + k
            target = qkv_out.at[layer, :, pl.ds(k * width, width)] if k < 3 else up_out.at[
                layer, :, pl.ds((k - 3) * width, width)
            ]
            copies.append(pltpu.make_async_copy(final[i], target, fetch_sem.at[i]))
        return copies

    lane_row = lax.broadcasted_iota(jnp.int32, (count, PAIR), 1) < HEAD_DIM

    def shared(one, other):
        one, other = one.astype(F32), other.astype(F32)
        return (
            jnp.where(lane_row, one, pltpu.roll(other, HEAD_DIM, 1)),
            jnp.where(lane_row, pltpu.roll(one, HEAD_DIM, 1), other),
        )

    def columns_by_rank(layer):
        base = layer * pieces
        for p in range(3):
            for zl in range(2):
                for x in range(2):
                    tiles = [
                        raw[base + p][:, (zh * 4 + zl * 2 + x) * PAIR : (zh * 4 + zl * 2 + x + 1) * PAIR]
                        for zh in range(2)
                    ]
                    for y, tile in enumerate(shared(*tiles)):
                        parts[layer, y * 4 + zl * 2 + x, :, p * PAIR : (p + 1) * PAIR] = tile.astype(BF16)
        size = up.shape[2] // 32
        for b in range(32):
            zh, zl, x, y, c = b // 16, b // 8 % 2, b // 4 % 2, b // 2 % 2, b % 2
            k, at = b * size // width, b * size % width
            to = QKV + (x * 2 + zh) * size
            parts[layer, y * 4 + zl * 2 + c, :, to : to + size] = raw[base + 3 + k][:, at : at + size]

    def columns_by_name(layer):
        base = layer * pieces
        for p in range(3):
            for zl in range(2):
                for x in range(2):
                    tiles = [
                        parts[layer, y * 4 + zl * 2 + x, :, p * PAIR : (p + 1) * PAIR] for y in range(2)
                    ]
                    for zh, tile in enumerate(shared(*tiles)):
                        at = (zh * 4 + zl * 2 + x) * PAIR
                        final[base + p][:, at : at + PAIR] = tile
        size = up.shape[2] // 32
        for b in range(32):
            zh, zl, x, y, c = b // 16, b // 8 % 2, b // 4 % 2, b // 2 % 2, b % 2
            k, at = b * size // width, b * size % width
            to = QKV + (x * 2 + zh) * size
            tile = parts[layer, y * 4 + zl * 2 + c, :, to : to + size]
            final[base + 3 + k][:, at : at + size] = tile.astype(F32)

    head_rank = me["c"] * 4 + me["x"] * 2 + me["y"]
    head_cut = pl.ds(pl.multiple_of(me["zh"] * 2 * PAIR, PAIR), PAIR)
    up_size = up.shape[2] // 32
    up_cut = pl.ds(pl.multiple_of(QKV + slot * up_size, PAIR), up_size)

    rank_row = lax.broadcasted_iota(jnp.int32, (RANKS, PAIR), 0)
    own_tile = me["c"] * 16 + me["y"] * 8 + me["zl"] * 4 + me["x"] * 2 + me["zh"]

    def expand_small():
        share = width // 32
        lanes_of = lax.broadcasted_iota(jnp.int32, (8, PAIR), 1) // share
        for group in range(8):
            zh, zl, x = group // 4, group // 2 % 2, group % 2
            tiles = [small_all[c * 16 + y * 8 + zl * 4 + x * 2 + zh] for y in range(2) for c in range(2)]
            for kind in range(3):
                value = jnp.zeros((8, PAIR), F32)
                for r, tile in enumerate(tiles):
                    moved = (r - kind) % 4 * share
                    tile = pltpu.roll(tile, moved, 1) if moved else tile
                    value = jnp.where(lanes_of == r, tile, value)
                named[kind, :, group * PAIR : (group + 1) * PAIR] = value
        rank_bias[...] = jnp.zeros_like(rank_bias)
        here = lax.broadcasted_iota(jnp.int32, (8, PAIR), 1) < HEAD_DIM
        for layer in range(layers):
            at = slice(layer, layer + 1)
            for part in range(2):
                heads = []
                for zh in range(2):
                    tile = small_all[
                        me["y"] * 16 + me["c"] * 8 + zh * 4 + me["zl"] * 2 + part, layers : layers + 1, :
                    ]
                    tile = jnp.broadcast_to(tile, (8, PAIR))
                    heads.append(tile if zh == layer else pltpu.roll(tile, HEAD_DIM, 1))
                cut = slice(2 * part * PAIR, (2 * part + 1) * PAIR)
                rank_bias[at, cut] = jnp.where(here, heads[0], heads[1])[:1]
            for x in range(2):
                for zh in range(2):
                    tile = me["c"] * 16 + me["y"] * 8 + me["zl"] * 4 + x * 2 + zh
                    to = QKV + (x * 2 + zh) * up_size
                    line = layers + 1 + layer
                    rank_bias[at, to : to + up_size] = small_all[tile, line : line + 1, :]

    def own_small(layer):
        share = width // 32
        total = grad_sum.at[layer, len(SMALL_AXES)]
        moved = pltpu.roll(total[RANKS:], (32 - block) % 32 * share, 1)
        at = slice(layer, layer + 1)
        gain_out[at] = moved[0:1, :share]
        shift_out[at] = moved[1:2, :share]
        bias_out[at] = moved[2:3, :share]
        pair = pltpu.roll(total[:RANKS, head_cut], me["zl"] * HEAD_DIM, 1)
        pair = jnp.where(rank_row == head_rank, pair, 0.0)
        qvb_out[at] = jnp.sum(pair, axis=0, keepdims=True)[:, :HEAD_DIM]
        more = jnp.where(rank_row == rank, total[:RANKS, up_cut], 0.0)
        upb_out[at] = jnp.sum(more, axis=0, keepdims=True)

    def build_mask(m):
        row = lax.broadcasted_iota(jnp.int32, (lanes, lanes), 0)
        column = lax.broadcasted_iota(jnp.int32, (lanes, lanes), 1)
        across = jnp.broadcast_to(marks[pl.ds(m, 1), :], (lanes, lanes))
        length = marks[pl.ds(m, 1), pack : pack + 1]
        live = column.astype(F32) < length
        allowed = (across.T == across) & (column <= row) & (live | (column == row))
        hidden = jnp.where(allowed, 0.0, MASKED).astype(BF16)
        mask_all[0, 0, m] = hidden[:pack]
        live = lax.broadcasted_iota(jnp.int32, (pack, 1), 0).astype(F32) < length
        at = pl.ds(m * pack, pack)
        rnd[0, 0, at] = jnp.where(live, cotangent[at].astype(F32), 0.0).astype(BF16)

    class Piece:
        def __init__(self, own, at):
            here, there = at(me["zh"]), at(1 - me["zh"])
            self.one = links.copy(here if own is None else own, here, (D1,))
            self.near = links.copy(here if own is None else own, here, (D2,))
            self.far = links.copy(there, there, (D2,))

        def start(self):
            self.one.start()

        def start_near(self):
            self.near.start()

        def step(self):
            self.one.wait()

        def start_far(self):
            self.far.start()

        def done(self):
            self.near.wait()
            self.far.wait()

    class Heads:
        def __init__(self, layer):
            self.layer = layer
            count = proj.shape[1]
            half = dp_all.at[layer, pl.ds(me["zh"] * HEAD_DIM + me["c"] * count, count)]
            self.to_core = links.copy(proj.at[layer], half, ("c",))
            self.stays = pltpu.make_async_copy(proj.at[layer], half, own_sem.at[layer, 2])
            head = dp_all.at[layer, pl.ds(me["zh"] * HEAD_DIM, HEAD_DIM)]
            self.one = links.copy(head, head, (D1,))
            heads = dp_all.at[layer, pl.ds(0, PAIR)]
            self.two = links.copy(heads, heads, (D2,))

        def prepare(self):
            @pl.when(mine)
            def _():
                self.stays.start()
                self.stays.wait()

            @pl.when(others)
            def _():
                self.to_core.start()
                self.to_core.wait_send()

        def start(self):
            @pl.when(mine)
            def _():
                self.to_core.wait_recv()
                self.one.start()

        def step(self):
            @pl.when(mine)
            def _():
                self.one.wait()

        def start_far(self):
            @pl.when(mine)
            def _():
                self.two.start()

        def done(self):
            @pl.when(mine)
            def _():
                self.two.wait_send()

            @pl.when(others)
            def _():
                self.two.wait_recv()

    class Weights:
        def __init__(self, layer):
            self.layer = layer
            size = down.shape[1]
            self.keep = [
                pltpu.make_async_copy(
                    parts.at[layer, rank], cat_all.at[layer, block], own_sem.at[layer, 0]
                ),
                pltpu.make_async_copy(
                    down.at[layer], self.down_rows(me["zh"], 0, size), own_sem.at[layer, 1]
                ),
            ]
            self.trades = [
                links.copy(
                    parts.at[layer, rank_of(flipped(me, axes))], cat_all.at[layer, block], axes
                )
                for axes in NEAR
            ]
            self.cat = [
                Piece(None, lambda zh, zl=zl, h=h: self.cat_rows(zh, zl, h))
                for zl in range(2)
                for h in range(2)
            ]
            half = size // 2
            self.down = [
                Piece(
                    down.at[layer, pl.ds(h * half, half)],
                    lambda zh, h=h: self.down_rows(zh, h * half, half),
                )
                for h in range(2)
            ]
            self.heads = Heads(layer)

        def cat_rows(self, zh, zl, h):
            return cat_all.at[self.layer, pl.ds(zh * 16 + zl * 8 + me["x"] * 4 + 2 * h, 2)]

        def down_rows(self, zh, start, count):
            size = down.shape[1]
            return dp_all.at[
                self.layer, pl.ds(PAIR + (me[D2] * 2 + zh) * size + start, count)
            ]

        def start_trades(self):
            self.keep[0].start()
            for copy in self.trades:
                copy.start()

        def traded(self):
            self.keep[0].wait()
            for copy in self.trades:
                copy.wait()

        def cat_done(self):
            for piece in self.cat:
                piece.done()

        def rows_done(self):
            self.keep[1].wait()
            for piece in self.down:
                piece.done()
            self.heads.done()

    def turn(value, sign):
        return (
            value * tables[0]
            + pltpu.roll(value, PAIR - ROT // 2, 1) * (tables[1] * sign)
            + pltpu.roll(value, ROT // 2, 1) * (tables[2] * sign)
        )

    def by_head(value):
        zero = jnp.zeros_like(value)
        return jnp.concatenate(
            [jnp.where(first_head, value, zero), jnp.where(first_head, zero, value)], axis=0
        )

    def of_heads(value):
        return jnp.where(first_head, value[:pack], value[pack:])

    def forward(layer, j):
        hidden = hid[layer, j].reshape(2 * rows, width)
        for cut in (slice(0, QKV), slice(QKV, wide)):
            columns = cat_all[layer, :, :, cut].reshape(width, -1)
            scratch[0, :, cut] = dot(hidden, columns, ((1,), (0,)))
        bias = rank_bias[layer : layer + 1, :]

        def each(p, carry):
            at = pl.ds(pl.multiple_of(p * pack, pack), pack)
            turned = scratch[0, at, :QKV] + bias[:, :QKV]
            queries = turn(turned[:, :PAIR], 1.0).astype(BF16)
            keys = turn(turned[:, PAIR : 2 * PAIR], 1.0).astype(BF16)
            values = turned[:, 2 * PAIR :].astype(BF16)
            qkv_kept[layer, j, at, :PAIR] = queries
            qkv_kept[layer, j, at, PAIR : 2 * PAIR] = keys
            qkv_kept[layer, j, at, 2 * PAIR :] = values
            hide = mask_all[j, p // micros, p % micros][:, :pack].astype(F32)
            scores = dot(by_head(queries), keys, ((1,), (1,))) * scale
            scores = scores + jnp.concatenate([hide, hide], axis=0)
            shifted = jnp.exp(scores - jnp.max(scores, axis=-1, keepdims=True))
            soft = shifted / jnp.sum(shifted, axis=-1, keepdims=True)
            soft = soft.astype(BF16)
            probs[layer, j, p] = soft
            ca[layer, j, at, :PAIR] = of_heads(dot(soft, values, ((1,), (0,)))).astype(BF16)
            for start in range(QKV, wide, 2 * PAIR):
                cut = slice(start, start + 2 * PAIR)
                raised = scratch[0, at, cut] + bias[:, cut]
                cdf = 0.5 * (1.0 + lax.erf(raised * 0.7071067811865476))
                density = jnp.exp(-0.5 * raised * raised) * 0.3989422804014327
                to = start - QKV
                ca[layer, j, at, PAIR + to : PAIR + to + 2 * PAIR] = (raised * cdf).astype(BF16)
                slope[layer, j, at, to : to + 2 * PAIR] = (cdf + raised * density).astype(BF16)
            return carry

        lax.fori_loop(0, 2 * micros, each, 0, unroll=4)

    def backward(layer, j):
        rounded = rnd[j].reshape(2 * rows, width)
        for cut in (slice(0, PAIR), slice(PAIR, PAIR + lift)):
            scratch[0, :, cut] = dot(rounded, dp_all[layer, cut], ((1,), (1,)))

        def each(p, carry):
            at = pl.ds(pl.multiple_of(p * pack, pack), pack)
            for start in range(0, lift, 2 * PAIR):
                cut = slice(start, start + 2 * PAIR)
                grown = scratch[0, at, PAIR + start : 3 * PAIR + start]
                grown = (grown * slope[layer, j, at, cut].astype(F32)).astype(BF16)
                mdud[j, at, QKV + start : QKV + start + 2 * PAIR] = grown
                sums[:, QKV + start : QKV + start + 2 * PAIR] += jnp.sum(
                    grown.astype(F32).reshape(pack // 8, 8, 2 * PAIR), axis=0
                )
            context = by_head(scratch[0, at, :PAIR].astype(BF16))
            queries = by_head(qkv_kept[layer, j, at, :PAIR])
            keys = qkv_kept[layer, j, at, PAIR : 2 * PAIR]
            values = qkv_kept[layer, j, at, 2 * PAIR :]
            kept = probs[layer, j, p]
            soft = kept.astype(F32)
            prob_delta = dot(context, values, ((1,), (1,)))
            row_delta = jnp.sum(soft * prob_delta, axis=-1, keepdims=True)
            score_delta = (soft * (prob_delta - row_delta)).astype(BF16)
            value_delta = dot(kept, context, ((0,), (0,)))
            query_delta = of_heads(dot(score_delta, keys, ((1,), (0,)))) * scale
            key_delta = dot(score_delta, queries, ((0,), (0,))) * scale
            three = (turn(query_delta, -1.0), turn(key_delta, -1.0), value_delta)
            for i, delta in enumerate(three):
                delta = delta.astype(BF16)
                cut = slice(i * PAIR, (i + 1) * PAIR)
                mdud[j, at, cut] = delta
                sums[:, cut] += jnp.sum(delta.astype(F32).reshape(pack // 8, 8, PAIR), axis=0)
            return carry

        lax.fori_loop(0, 2 * micros, each, 0, unroll=4)

    halves = (slice(0, width // 2), slice(width // 2, width))

    def out_term(layer):
        def put(j, target):
            for cut in halves:
                target[:, cut] = dot(ca[layer, j], dp_all[layer, :, cut], ((1,), (0,)))

        return put

    def hidden_term(layer):
        def put(j, target):
            for half, cut in enumerate(halves):
                columns = cat_all[layer, pl.ds(16 * half, 16)].reshape(width // 2, wide)
                target[:, cut] = dot(mdud[j], columns, ((1,), (1,)))

        return put

    class Grads:
        def __init__(self, layer):
            self.layer = layer
            self.down_one = links.copy(down_s1, down_r1.at[layer], (D2,))
            self.down_two = links.copy(down_s2, down_r2.at[layer], (D1,))
            self.proj_one = links.copy(proj_s1, proj_r1.at[layer], (D2,))
            self.proj_two = links.copy(proj_s2, proj_r2.at[layer], (D1,))
            self.proj_three = links.copy(proj_s3, proj_r3.at[layer], ("c",))
            self.cat_one = [
                [links.copy(cat_s1.at[i, zl], cat_r1.at[layer, i, zl], (D2,)) for zl in range(2)]
                for i in range(2)
            ]
            self.cat_two = [
                links.copy(cat_s2.at[zl], cat_r2.at[layer, zl], (D1,)) for zl in range(2)
            ]
            self.trades = []
            for axes in NEAR:
                there = flipped(me, axes)
                part = cat_a.at[there["zl"], there["y"] * 2 + there["c"]]
                self.trades.append(links.copy(part, parts.at[layer, rank], axes))
            self.keep = pltpu.make_async_copy(
                cat_a.at[me["zl"], me["y"] * 2 + me["c"]], parts.at[layer, rank], own_sem.at[layer, 3]
            )

        def rows_terms(self, start, stop):
            layer = self.layer
            size = (stop - start) * 2 * rows
            kept = ca[layer, start:stop].reshape(size, PAIR + lift)
            for cut in halves:
                rounded = rnd[start:stop, :, :, cut].reshape(size, width // 2)
                for part in (pl.ds(PAIR, lift), pl.ds(0, PAIR)):
                    side = kept[:, PAIR:] if part.start else kept[:, :PAIR]
                    value = dot(side, rounded, ((0,), (0,)))
                    if start:
                        value = value + dp_grad[part, cut]
                    dp_grad[part, cut] = value

        def rows_one(self):
            half = lift // 2
            down_s1[...] = dp_grad[pl.ds(PAIR + (1 - me[D2]) * half, half)].astype(BF16)
            self.down_one.start()

            @pl.when(others)
            def _():
                proj_s1[...] = dp_grad[pl.ds(0, PAIR)].astype(BF16)
                self.proj_one.start()

        def rows_two(self):
            layer = self.layer
            half, quarter = lift // 2, lift // 4
            base = PAIR + me[D2] * half
            self.down_one.wait()
            at = (1 - me[D1]) * quarter
            down_s2[...] = (
                dp_grad[pl.ds(base + at, quarter)]
                + down_r1[layer, pl.ds(at, quarter)].astype(F32)
            ).astype(BF16)
            self.down_two.start()

            @pl.when(others)
            def _():
                self.proj_one.wait_send()

            @pl.when(mine)
            def _():
                self.proj_one.wait_recv()
                at = (1 - me[D1]) * HEAD_DIM
                proj_s2[...] = (
                    dp_grad[pl.ds(at, HEAD_DIM)]
                    + proj_r1[layer, pl.ds(at, HEAD_DIM)].astype(F32)
                ).astype(BF16)
                self.proj_two.start()

        def rows_three(self):
            layer = self.layer
            half, quarter = lift // 2, lift // 4
            base = PAIR + me[D2] * half
            self.down_two.wait()
            at = me[D1] * quarter
            down_out[layer] = (
                dp_grad[pl.ds(base + at, quarter)]
                + down_r1[layer, pl.ds(at, quarter)].astype(F32)
                + down_r2[layer].astype(F32)
            )
            count = proj.shape[1]

            @pl.when(mine)
            def _():
                self.proj_two.wait()
                at = me[D1] * HEAD_DIM

                def half_of(which):
                    return (
                        dp_grad[pl.ds(at + which * count, count)]
                        + proj_r1[layer, pl.ds(at + which * count, count)].astype(F32)
                        + proj_r2[layer, pl.ds(which * count, count)].astype(F32)
                    )

                proj_out[layer] = half_of(me["c"])
                proj_s3[...] = half_of(1 - me["c"]).astype(BF16)
                self.proj_three.start()
                self.proj_three.wait_send()

            @pl.when(others)
            def _():
                self.proj_three.wait_recv()
                proj_out[layer] = proj_r3[layer].astype(F32)

        def cat_terms(self, i):
            layer = self.layer
            zh = me["zh"] if i else 1 - me["zh"]
            deltas = mdud[...].reshape(8 * rows, wide)
            for zl in range(2):
                start = pl.multiple_of((zh * 2 + zl) * (width // 4), width // 4)
                kept = hid[layer, :, :, :, pl.ds(start, width // 4)].reshape(8 * rows, width // 4)
                scratch[0, : width // 4, :wide] = dot(kept, deltas, ((0,), (0,)))
                size = width // 8
                cat_s1[i, zl] = scratch[0, pl.ds((1 - me["x"]) * size, size), :wide].astype(BF16)
                self.cat_one[i][zl].start()
                cat_own[i, zl] = scratch[0, pl.ds(me["x"] * size, size), :wide]

        def cat_step_two(self, zl):
            layer = self.layer
            self.cat_one[0][zl].wait()
            cat_s2[zl] = (cat_own[0, zl] + cat_r1[layer, 0, zl].astype(F32)).astype(BF16)
            self.cat_two[zl].start()

        def cat_step_three(self, zl):
            layer = self.layer
            self.cat_one[1][zl].wait()
            self.cat_two[zl].wait()
            total = (
                cat_own[1, zl]
                + cat_r1[layer, 1, zl].astype(F32)
                + cat_r2[layer, zl].astype(F32)
            )
            cat_a[zl] = total.astype(BF16).reshape(cat_a.shape[1:])

        def cat_trade(self):
            for copy in self.trades:
                copy.start()
            self.keep.start()

        def cat_done(self):
            for copy in self.trades:
                copy.wait()
            self.keep.wait()

    def put_sums(layer, index, value):
        grad_sum[layer, 0, pl.ds(index, 1), : value.shape[1]] = value

    def own_rows(layer, total, stream_at, up_at, put):
        gain = bias_row(layer, 0)
        gain_sum = jnp.zeros((1, width), F32)
        shift_sum = jnp.zeros((1, width), F32)
        for m in range(2 * micros):
            at = pl.ds(m * (rows // (2 * micros)), rows // (2 * micros))
            delta = total(at)
            normed, inverse = normalise(stream_at(at))
            gain_sum = gain_sum + jnp.sum(delta * normed, axis=0, keepdims=True)
            shift_sum = shift_sum + jnp.sum(delta, axis=0, keepdims=True)
            scaled = delta * gain
            put(
                at,
                up_at(at) + inverse * (scaled - mean_of(scaled) - normed * mean_of(scaled * normed)),
            )
        put_sums(layer, RANKS + 0, gain_sum)
        put_sums(layer, RANKS + 1, shift_sum)

    def bias_sums(layer):
        put_sums(layer, rank, jnp.sum(sums[...], axis=0, keepdims=True))
        rounded = jnp.zeros((8, width), F32)
        for m in range(2 * micros):
            size = rows // (2 * micros)
            part = rnd[0, 0, pl.ds(m * size, size)].astype(F32)
            rounded = rounded + jnp.sum(part.reshape(size // 8, 8, width), axis=0)
        put_sums(layer, RANKS + 2, jnp.sum(rounded, axis=0, keepdims=True))

    def give_back(turn_index):
        for axes in (("c",), (T1,), (T2,)):
            pl.semaphore_signal(
                free_sem.at[turn_index], inc=1, device_id=links.peer(axes), device_id_type=MESH
            )

    def await_places(turn_index):
        pl.semaphore_wait(free_sem.at[turn_index], 3)

    taken = [Weights(layer) for layer in range(layers)]
    grads = [Grads(layer) for layer in range(layers)]
    row_gathers = [Rows(links, hid.at[1]), Rows(links, mask_all), Rows(links, rnd)]
    hidden_two, rounded_one = Rows(links, hid.at[1]), Rows(links, rnd)
    sets = (core_in, chip_in, core_out, chip_out)
    out_one, delta_two, delta_one = Sums(links, *sets), Sums(links, *sets), Sums(links, *sets)
    spare = hid.at[1]
    out_two = Sums(links, core_in, spare.at[0:3, 0], core_out, spare.at[0:3, 1], True)
    small_copies = []
    for i, axis in enumerate(SMALL_AXES):
        tiles = small_all.at[pl.ds(own_tile // 2**i * 2**i, 2**i)]
        small_copies.append(links.copy(tiles, tiles, (axis,)))
    grad_copies = [
        [
            links.copy(grad_sum.at[layer, i], grad_in.at[layer, i], (axis,))
            for i, axis in enumerate(GRAD_AXES)
        ]
        for layer in range(layers)
    ]

    def grad_step(layer, i):
        grad_copies[layer][i].wait()
        grad_sum[layer, i + 1] = grad_sum[layer, i] + grad_in[layer, i]
        if i + 1 < len(SMALL_AXES):
            grad_copies[layer][i + 1].start()
        else:
            own_small(layer)

    chain = [taken[0].down[0]] + taken[0].cat + [taken[0].down[1], taken[0].heads]
    chain = chain + taken[1].cat + taken[1].down + [taken[1].heads]

    def pump(k):
        chain[k].step()
        for piece in chain[max(ahead(k - 1), 2) : ahead(k)]:
            piece.start()
        chain[k].start_far()

    def ahead(k):
        return min(k + 3 if k < 5 else k + 5, len(chain))

    def small_step(i):
        small_copies[i].wait()
        if i + 1 < len(SMALL_AXES):
            small_copies[i + 1].start()
        else:
            expand_small()

    fetched = fetch_columns()
    for copy in fetched:
        copy.start()
    for one in taken:
        one.keep[1].start()
    small_all[own_tile] = small[...]
    links.meet()
    small_copies[0].start()
    chain[0].start()
    for copy in fetched[:pieces]:
        copy.wait()
    columns_by_rank(0)
    taken[0].start_trades()
    for piece in taken[0].down:
        piece.start_near()
    hid[1, 0, 0] = inputs[...]
    for m in range(micros):
        build_mask(m)
    taken[0].heads.prepare()
    taken[1].heads.prepare()
    for layer in range(layers):
        grad_sum[layer, 0] = jnp.zeros_like(grad_sum[layer, 0])
    small_step(0)
    taken[0].traded()
    chain[1].start()
    row_gathers[1].start()
    row_gathers[0].start()
    for piece in taken[0].cat:
        piece.start_near()
    small_step(1)
    pump(0)
    small_step(2)
    row_gathers[1].forward()
    for copy in fetched[pieces:]:
        copy.wait()
    columns_by_rank(1)
    small_step(3)
    pump(1)
    small_step(4)
    row_gathers[0].forward()
    taken[1].start_trades()

    gain, shift = bias_row(0, 0), bias_row(0, 1)

    def first_norm(j, carry):
        row_gathers[0].arrive(j)
        row_gathers[1].arrive(j)

        def each(p, carry):
            size = rows // 4
            at = pl.ds(pl.multiple_of((p % 4) * size, size), size)
            normed, _ = normalise(hid[1, j, p // 4, at].astype(F32))
            hid[0, j, p // 4, at] = (normed * gain + shift).astype(BF16)
            return carry

        lax.fori_loop(0, 8, each, 0)
        for k in range(3):

            @pl.when(j == k)
            def _():
                pump(2 + k)

        return carry

    lax.fori_loop(0, 4, first_norm, 0)
    row_gathers[0].finish()
    row_gathers[1].finish()
    row_gathers[2].start()
    taken[1].traded()
    pump(5)
    taken[0].cat_done()

    def first(i, j):
        forward(0, j)

        @pl.when(i == 0)
        def _():
            pump(6)
            taken[0].rows_done()
            for piece in taken[1].cat + taken[1].down:
                piece.start_near()
            row_gathers[2].forward()

        for k in range(1, 4):

            @pl.when(i == k)
            def _():
                pump(6 + k)

    out_one.run(first, out_term(0), scratch, own, far_first)()
    pump(10)

    def rest_of_rounded(j, carry):
        row_gathers[2].arrive(j)
        return carry

    lax.fori_loop(0, 4, rest_of_rounded, 0)
    row_gathers[2].finish()
    total = out_one.total(own)
    out_bias = bias_row(0, 2)
    gain, shift = bias_row(1, 0), bias_row(1, 1)
    for m in range(4):
        at = pl.ds(m * (rows // 4), rows // 4)
        stream = inputs[at].astype(F32) + total(at) + out_bias
        stream_two[at] = stream
        normed, _ = normalise(stream)
        hid[1, 0, 0, at] = (normed * gain + shift).astype(BF16)
    hidden_two.start()
    pump(11)
    taken[1].cat_done()

    def second(j, carry):
        hidden_two.arrive(j)
        forward(1, j)

        @pl.when(j == 0)
        def _():
            hidden_two.forward()
            pump(12)
            pump(13)

        return carry

    lax.fori_loop(0, 4, second, 0)
    hidden_two.finish()
    taken[1].rows_done()

    sums[...] = jnp.zeros_like(sums)

    delta_two.run(lambda i, j: backward(1, j), hidden_term(1), scratch, own, far_first)()
    grads[1].cat_terms(0)
    grads[1].cat_terms(1)
    grads[1].rows_terms(0, 4)
    bias_sums(1)
    give_back(2)
    grads[1].rows_one()
    total = delta_two.total(own)
    await_places(2)

    def put_one(at, value):
        up_one[at] = value
        rnd[0, 0, at] = value.astype(BF16)

    own_rows(1, total, lambda at: stream_two[at], lambda at: rnd[0, 0, at].astype(F32), put_one)
    rounded_one.start()
    grad_copies[1][0].start()
    sums[...] = jnp.zeros_like(sums)
    out_two.run(lambda i, j: None, out_term(1), scratch, own, far_first, True)()
    for m in range(4):
        at = pl.ds(m * (rows // 4), rows // 4)
        stream_two[at] = stream_two[at] + own[at] + bias_row(1, 2)
    give_back(0)
    rounded_one.forward()
    out_two.release()
    for j in range(4):
        out_two.core(j).wait_send()
    await_places(0)

    def third(i, j):
        for k in range(4):

            @pl.when(i == k)
            def _():
                grad_step(1, k)

        @pl.when(i == 1)
        def _():
            for zl in range(2):
                grads[1].cat_step_two(zl)

        @pl.when(i == 2)
        def _():
            rounded_one.arrive(1)

        @pl.when(i < 3)
        def _():
            rounded_one.arrive(j)

        @pl.when(i == 2)
        def _():
            rounded_one.finish()

        @pl.when(i == 3)
        def _():
            grads[1].rows_two()

        backward(0, j)

    last = delta_one.run(third, hidden_term(0), scratch, own, near_first)
    for zl in range(2):
        grads[1].cat_step_three(zl)
    grads[0].cat_terms(0)
    grads[1].cat_trade()
    grads[0].cat_terms(1)
    grads[1].rows_three()
    grads[0].rows_terms(0, 4)
    grads[0].rows_one()
    out_two.relay()
    bias_sums(0)
    grad_step(1, 4)
    last()
    for zl in range(2):
        grads[0].cat_step_two(zl)
    grads[1].cat_done()
    returned = return_columns(1) + return_columns(0)
    columns_by_name(1)
    for copy in returned[:pieces]:
        copy.start()
    total = delta_one.total(own)

    def put_last(at, value):
        input_grad[at] = value

    own_rows(0, total, lambda at: inputs[at].astype(F32), lambda at: up_one[at], put_last)
    grad_copies[0][0].start()
    for i in range(len(GRAD_AXES)):
        grad_step(0, i)
    total = out_two.total(stream_two, True)
    for m in range(4):
        at = pl.ds(m * (rows // 4), rows // 4)
        outputs[at] = total(at).astype(BF16)
    for zl in range(2):
        grads[0].cat_step_three(zl)
    grads[0].cat_trade()
    grads[0].rows_two()
    grads[0].cat_done()
    columns_by_name(0)
    for copy in returned[pieces:]:
        copy.start()
    grads[0].rows_three()
    for copy in returned:
        copy.wait()


def run_layers(qkv, up, down, proj, inputs, cotangent, marks, small, tables):
    layers, count = qkv.shape[:2]
    rows, width = inputs.shape
    micros, lanes = marks.shape
    pack = rows // micros
    lift = up.shape[2] // RANKS
    wide = QKV + lift
    vmem = pl.BlockSpec(memory_space=pltpu.VMEM)
    anywhere = pl.BlockSpec(memory_space=pltpu.HBM)
    shape = jax.ShapeDtypeStruct
    stages = len(SMALL_AXES)
    copies = 256
    cat_size = width // 8
    buffers = [
        ((layers, RANKS, count, wide), BF16),
        ((layers, 32, count, wide), BF16),
        ((layers, PAIR + lift, width), BF16),
        ((layers, 4, 2, rows, width), BF16),
        ((4, 2, rows, width), BF16),
        ((4, 2, micros, pack, lanes), BF16),
        ((layers, 4, 2 * rows, QKV), BF16),
        ((layers, 4, 2 * micros, 2 * pack, pack), BF16),
        ((layers, 4, 2 * rows, PAIR + lift), BF16),
        ((layers, 4, 2 * rows, lift), BF16),
        ((4, 2 * rows, wide), BF16),
        ((2, 2 * rows, width), F32),
        ((4, rows, width), BF16),
        ((3, rows, width), BF16),
        ((4, rows, width), BF16),
        ((3, rows, width), BF16),
        ((rows, width), F32),
        ((rows, width), F32),
        ((rows, width), F32),
        ((32,) + small.shape, F32),
        ((3, 8, width), F32),
        ((8, wide), F32),
        ((8, wide), F32),
        ((layers, stages + 1, 2 * RANKS, width), F32),
        ((layers, stages, 2 * RANKS, width), F32),
        ((2, 2, cat_size, wide), F32),
        ((2, 2, cat_size, wide), BF16),
        ((layers, 2, 2, cat_size, wide), BF16),
        ((2, cat_size, wide), BF16),
        ((layers, 2, cat_size, wide), BF16),
        ((2, 4, count, wide), BF16),
        ((PAIR + lift, width), F32),
        ((lift // 2, width), BF16),
        ((layers, lift // 2, width), BF16),
        ((lift // 4, width), BF16),
        ((layers, lift // 4, width), BF16),
        ((PAIR, width), BF16),
        ((layers, PAIR, width), BF16),
        ((HEAD_DIM, width), BF16),
        ((layers, HEAD_DIM, width), BF16),
        ((HEAD_DIM // 2, width), BF16),
        ((layers, HEAD_DIM // 2, width), BF16),
    ]
    return pl.pallas_call(
        layers_kernel,
        out_shape=(
            shape((rows, width), BF16),
            shape((rows, width), F32),
            shape((layers, width // 32), F32),
            shape((layers, width // 32), F32),
            shape(qkv.shape, F32),
            shape((layers, 2 * width // 32), F32),
            shape(proj.shape, F32),
            shape((layers, width // 32), F32),
            shape(up.shape, F32),
            shape((layers, up.shape[2] // 32), F32),
            shape(down.shape, F32),
        ),
        in_specs=[anywhere] * 4 + [vmem] * 5,
        out_specs=(vmem,) * 4 + (anywhere,) + (vmem,) * 3 + (anywhere,) + (vmem,) * 2,
        scratch_shapes=[pltpu.VMEM(dims, kind) for dims, kind in buffers]
        + [
            pltpu.SemaphoreType.DMA((copies,)),
            pltpu.SemaphoreType.DMA((copies,)),
            pltpu.SemaphoreType.DMA((layers, 4)),
            pltpu.SemaphoreType.REGULAR((3,)),
            pltpu.SemaphoreType.DMA((layers * 7,)),
        ],
        compiler_params=pltpu.CompilerParams(
            collective_id=0, has_side_effects=True, vmem_limit_bytes=63 << 20
        ),
    )(qkv, up, down, proj, inputs, cotangent, marks, small, tables)


def refold(block, extra):
    if extra == 1:
        return block
    whole = lax.all_gather(block, AXES, axis=1, tiled=True)
    rows = whole.shape[1] // 32
    return lax.dynamic_slice_in_dim(whole, lax.axis_index(AXES[1:]) * rows, rows, 1)


def unfold(block, extra):
    if extra == 1:
        return block
    rows = block.shape[1]
    whole = jnp.zeros((block.shape[0], 32 * rows) + block.shape[2:], F32)
    whole = lax.dynamic_update_slice_in_dim(whole, block, lax.axis_index(AXES[1:]) * rows, 1)
    return lax.psum_scatter(whole, AXES, scatter_dimension=1, tiled=True)


def rope_tables(pack):
    half = ROT // 2
    angle = np.arange(pack, dtype=np.float32)[:, None] * (
        np.float32(10000.0) ** (-np.arange(0, ROT, 2, dtype=np.float32) / np.float32(ROT))
    )
    angle = angle.astype(np.float32)
    tables = np.zeros((3, pack, 2, HEAD_DIM), np.float32)
    tables[0] = 1.0
    tables[0, :, :, :half] = tables[0, :, :, half:ROT] = np.cos(angle)[:, None]
    tables[1, :, :, :half] = -np.sin(angle)[:, None]
    tables[2, :, :, half:ROT] = np.sin(angle)[:, None]
    return tables.reshape(3, pack, PAIR)


def shards(
    inputs,
    cotangent,
    segments,
    pack_length,
    norm_gain,
    norm_shift,
    qkv_weight,
    qv_bias,
    proj_weight,
    proj_bias,
    up_weight,
    up_bias,
    down_weight,
    down_bias,
):
    micros, pack, width = inputs.shape
    layers = qkv_weight.shape[0]
    extra = lax.axis_size("e")
    marks = jnp.concatenate([segments, pack_length], axis=1).astype(F32)
    marks = jnp.pad(marks, ((0, 0), (0, -(pack + 1) % 128)))

    def wide(value):
        return jnp.pad(value.astype(F32), ((0, 0), (0, PAIR - value.shape[1])))

    biases = refold(proj_bias, extra).astype(F32) + refold(down_bias, extra).astype(F32)
    three = [refold(norm_gain, extra).astype(F32), refold(norm_shift, extra).astype(F32), biases]
    small = [
        wide(jnp.concatenate(three, axis=1)),
        wide(refold(qv_bias, extra).reshape(1, -1)),
        wide(refold(up_bias, extra)),
    ]
    small = jnp.concatenate(small)
    small = jnp.pad(small, ((0, -small.shape[0] % 8), (0, 0)))
    given = run_layers(
        refold(qkv_weight, extra),
        refold(up_weight, extra),
        refold(down_weight, extra),
        refold(proj_weight, extra),
        inputs.reshape(micros * pack, width),
        cotangent.reshape(micros * pack, width),
        marks,
        small,
        jnp.asarray(rope_tables(pack)),
    )
    out, input_grad = given[:2]
    gain, shift, qkv, qvb, proj, bias, up, upb, down = [unfold(g, extra) for g in given[2:]]
    return (
        out.reshape(micros, pack, width),
        input_grad.reshape(micros, pack, width),
        gain,
        shift,
        qkv,
        qvb,
        proj,
        bias,
        up,
        upb,
        down,
        bias,
    )


def solution(mesh):
    devices = mesh.devices.size
    fine = Mesh(mesh.devices.reshape(devices // 32, 2, 2, 2, 2, 2), AXES)
    cube, flat = P(None, AXES, None), P(None, AXES)
    placed = (cube, cube, flat, flat, flat, flat, cube, flat, cube, flat, cube, flat, cube, flat)
    given = (cube, cube, flat, flat, cube, flat, cube, flat, cube, flat, cube, flat)
    return jax.shard_map(shards, mesh=fine, in_specs=placed, out_specs=given, check_vma=False)
```
